32 devices in a mesh: grp: 2 (over y), ep: 16 (over z, x, core).
Axes of the slice: x: 2, y: 2, z: 4, core: 2. Of those that a mesh axis runs over, the one named last changes fastest.
Arguments:
- latent_in: bfloat16 [4096, 1024], P(('grp', 'ep')), parts along dimension 0, may hold values from -6 to 6
- routes: int32 [4096, 8], P(('grp', 'ep')), parts along dimension 0, may hold values from 0 to 15, all different within a row; in each aligned block of 128 rows (0 to 127, 128 to 255, ...) at most 96 rows name the same one
- combine_weights: float32 [4096, 8], P(('grp', 'ep')), parts along dimension 0, may hold values from 0.1 to 1
- cotangent: bfloat16 [4096, 1024], P(('grp', 'ep')), parts along dimension 0, may hold values from -6 to 6
- w_gate: bfloat16 [16, 1024, 512], P('ep'), may hold values from -0.1875 to 0.1875
- w_up: bfloat16 [16, 1024, 512], P('ep'), may hold values from -0.1875 to 0.1875
- w_down: bfloat16 [16, 512, 1024], P('ep'), may hold values from -0.25 to 0.25
Outputs:
- combined: bfloat16 [4096, 1024], P(('grp', 'ep')), parts along dimension 0
- grad_latent: bfloat16 [4096, 1024], P(('grp', 'ep')), parts along dimension 0
- grad_combine: float32 [4096, 8], P(('grp', 'ep')), parts along dimension 0
- grad_w_gate: bfloat16 [32, 1024, 512], P(('grp', 'ep')), parts along dimension 0
- grad_w_up: bfloat16 [32, 1024, 512], P(('grp', 'ep')), parts along dimension 0
- grad_w_down: bfloat16 [32, 512, 1024], P(('grp', 'ep')), parts along dimension 0
The draws below stay inside these ranges and needn't reach their ends.
There are 2 independent parts, one for each index of `grp`. The reference program is written for one: setup_inputs(seed, part) draws one part's arguments, and reference() takes and returns one part's arrays. A program takes and returns all parts, laid end to end along the dimension named above; an argument that names none is the same for every part. Nothing has to cross between parts.
Inputs may be any that keep to these rules, and one draw needn't show every extreme that they name: `routes`: each row names 8 different experts. Within the 128 rows of one device no expert is named more than 96 times, a bound that some block reaches.
All inputs are finite; a program needn't handle non-finite values.
Results may differ from the reference program's by a relative error of at most 0.0065.
Values may be sent and summed in bfloat16 or wider, within the bound.
No kernel may reach another device: no remote copies, remote signals or barrier semaphores. Data moves between devices by JAX's collectives and lax.ppermute only.
A program may use at most 128 MiB of HBM per device.

```python
import math
import jax
import jax.numpy as jnp
import numpy as np
from jax import lax

L = 1024
F = 512
TOP = 8
TOK_DEV = 128
EXPERTS = 16
TOKENS = 2048
CAP = 96
N_EP = 16


def level_of(stream_key, shape, shards, low, top_value):
    level, own = 1.0, jax.random.fold_in(stream_key, 6)
    for dim, parts in shards:
        heights = jnp.exp(jax.random.uniform(jax.random.fold_in(own, dim), (parts,), jnp.float32, low / len(shards), top_value / len(shards)))
        level = level * jnp.repeat(heights, shape[dim] // parts).reshape([-1 if axis == dim else 1 for axis in range(len(shape))])
    return level


def assign_block(stream_key, own, number, rows, number_of, top, bound, skew):
    ranking = jax.random.permutation(stream_key, number_of)
    crowded, usual = shares(number_of, rows * top, bound, skew, True), shares(number_of, rows * top, bound, skew, False)
    places = jnp.arange(number_of)

    def named(lengths, rotation):
        used = int((lengths > 0).sum())
        fixed = max(1, used // 4)
        moved = fixed + (places - fixed + rotation * (used - fixed)) % max(1, number_of - fixed)
        return jnp.zeros((number_of,), jnp.int32).at[ranking[jnp.where(places < fixed, places, moved)]].set(jnp.asarray(lengths, jnp.int32))

    lengths = jnp.where(number % 4 == 0, named(crowded, number // 4), named(usual, number - number // 4 - 1))
    mixed = jax.random.permutation(jax.random.fold_in(own, 3), number_of)
    source_of, taker = mixed[0:number_of // 2 * 2:2], mixed[1:number_of // 2 * 2:2]
    margin = jnp.minimum(lengths[source_of] - 1, bound - lengths[taker]) // 2
    margin = jnp.where((source_of == ranking[0]) | (taker == ranking[0]) | (lengths[taker] == 0), 0, jnp.maximum(margin, 0))
    moved = jax.random.randint(jax.random.fold_in(own, 4), (number_of // 2,), 0, 1 << 20) % (margin + 1)
    lengths = lengths.at[source_of].add(-moved).at[taker].add(moved)
    items = jnp.searchsorted(jnp.cumsum(lengths), jnp.arange(rows * top), side="right").astype(jnp.int32)
    listing = items.reshape(top, rows).T
    listing = listing[jax.random.permutation(jax.random.fold_in(own, 1), rows)]
    rotation = jax.random.randint(jax.random.fold_in(own, 2), (rows, 1), 0, top)
    return jnp.take_along_axis(listing, (jnp.arange(top)[None, :] + rotation) % top, axis=1)


def shares(amount, total, reach, skew, full):
    weights = [(1 << 20) // math.isqrt(standing ** skew) + 1 for standing in range(1, amount + 1)]
    largest = reach if full else min(reach, max(-(-total // amount), total * weights[0] // sum(weights)))
    least = 1 if total - largest >= amount - 1 else 0
    given, rest = [largest] + [least] * (amount - 1), total - largest - least * (amount - 1)
    while rest > 0:
        movable = [i for i in range(1, amount) if given[i] < largest] or [i for i in range(1, amount) if given[i] < reach]
        whole, remaining = sum([weights[i] for i in movable]), rest
        for i in movable:
            extra = min(reach - given[i], max(1, remaining * weights[i] // whole), rest)
            given[i] = given[i] + extra
            rest = rest - extra
    return np.array(given)


def centred(own_key, extent, deviation, reach, cuts=(), kind=jnp.bfloat16):
    values = jax.random.normal(own_key, extent, jnp.float32) * deviation
    if len(cuts) > 0:
        values = level_of(own_key, extent, cuts, -0.22, 0.18) * values
    return jnp.clip(values, min=-reach, max=reach).astype(kind)


def setup_inputs(seed: int = 0, part: int = 0) -> dict:
    streams_of = jax.random.split(jax.random.key(seed), 8)
    part_splits = jax.random.split(jax.random.fold_in(streams_of[7], part), 8)
    latent_in = centred(part_splits[0], (TOKENS, L), 1.0, 6.0, ((0, 16),))
    routes_keys = jax.random.split(jax.random.fold_in(part_splits[1], 1), TOKENS // TOK_DEV)
    routes_turns = jax.random.permutation(jax.random.fold_in(part_splits[1], 3), TOKENS // TOK_DEV)
    routes = jax.vmap(lambda own, number: assign_block(jax.random.fold_in(part_splits[1], 2), own, number, TOK_DEV, EXPERTS, TOP, CAP, 1))(routes_keys, routes_turns).reshape((TOKENS, TOP))
    combine_weights = jnp.clip(jnp.exp(math.log(1.0) - 2.3025851 * jax.random.uniform(part_splits[2], (TOKENS, TOP), jnp.float32) ** level_of(part_splits[2], (TOKENS, TOP), ((0, 16),), -0.2, 0.2)), 0.1, 1.0)
    cotangent = centred(part_splits[3], (TOKENS, L), 1.0, 6.0, ((0, 16),))
    w_gate = centred(streams_of[4], (EXPERTS, L, F), L ** -0.5, 0.1875, ((0, 16),))
    w_up = centred(streams_of[5], (EXPERTS, L, F), L ** -0.5, 0.1875, ((0, 16),))
    w_down = centred(streams_of[6], (EXPERTS, F, L), F ** -0.5, 0.25, ((0, 16),))
    return {"latent_in": latent_in, "routes": routes, "combine_weights": combine_weights, "cotangent": cotangent, "w_gate": w_gate, "w_up": w_up, "w_down": w_down}


def assign_slots(route_rows):
    flat_ids = route_rows.reshape(-1).astype(jnp.int32)
    onehot = (flat_ids[:, None] == jnp.arange(EXPERTS, dtype=jnp.int32)[None, :]).astype(jnp.int32)
    ranks = jnp.cumsum(onehot, axis=0) - 1
    return flat_ids, jnp.sum(onehot * ranks, axis=1).astype(jnp.int32)


def one_expert(operands):
    rows, grad_out, gate_w, up_w, down_w = operands
    gate_pre = jnp.dot(rows, gate_w, preferred_element_type=jnp.float32)
    up_pre = jnp.dot(rows, up_w, preferred_element_type=jnp.float32)
    sigma = jax.nn.sigmoid(gate_pre)
    silu_val = gate_pre * sigma
    hidden = (silu_val * up_pre).astype(jnp.bfloat16)
    expert_out = jnp.dot(hidden, down_w, preferred_element_type=jnp.float32).astype(jnp.bfloat16)
    grad_down = jnp.dot(hidden.T, grad_out, preferred_element_type=jnp.float32).astype(jnp.bfloat16)
    grad_hidden = jnp.dot(grad_out, down_w.T, preferred_element_type=jnp.float32)
    grad_gate = (grad_hidden * up_pre * sigma * (1.0 + gate_pre * (1.0 - sigma))).astype(jnp.bfloat16)
    grad_up = (grad_hidden * silu_val).astype(jnp.bfloat16)
    grad_gw = jnp.dot(rows.T, grad_gate, preferred_element_type=jnp.float32).astype(jnp.bfloat16)
    grad_uw = jnp.dot(rows.T, grad_up, preferred_element_type=jnp.float32).astype(jnp.bfloat16)
    grad_rows = (jnp.dot(grad_gate, gate_w.T, preferred_element_type=jnp.float32)
                 + jnp.dot(grad_up, up_w.T, preferred_element_type=jnp.float32)).astype(jnp.bfloat16)
    return expert_out, grad_rows, grad_gw, grad_uw, grad_down


def reference(latent_in, routes, combine_weights, cotangent, w_gate, w_up, w_down):
    expert_ids, slot_ids = jax.vmap(assign_slots)(routes.reshape(N_EP, TOK_DEV, TOP))
    source = jnp.arange(N_EP, dtype=jnp.int32)[:, None]
    position = ((expert_ids * N_EP + source) * CAP + slot_ids).reshape(-1).astype(jnp.int32)
    total_rows = EXPERTS * N_EP * CAP
    repeated = jnp.repeat(latent_in, TOP, axis=0)
    weighted = (combine_weights[:, :, None] * cotangent.astype(jnp.float32)[:, None, :]).astype(jnp.bfloat16)
    expert_rows = jnp.zeros((total_rows, L), jnp.bfloat16).at[position].set(repeated)
    cotangent_rows = jnp.zeros((total_rows, L), jnp.bfloat16).at[position].set(weighted.reshape(-1, L))
    outs = lax.map(one_expert, (expert_rows.reshape(EXPERTS, N_EP * CAP, L),
                                cotangent_rows.reshape(EXPERTS, N_EP * CAP, L), w_gate, w_up, w_down))
    expert_out, grad_rows, grad_w_gate, grad_w_up, grad_w_down = outs
    out_rows = expert_out.reshape(-1, L)[position].reshape(TOKENS, TOP, L).astype(jnp.float32)
    back_rows = grad_rows.reshape(-1, L)[position].reshape(TOKENS, TOP, L).astype(jnp.float32)
    combined = jnp.sum(combine_weights[:, :, None] * out_rows, axis=1).astype(jnp.bfloat16)
    grad_combine = jnp.sum(cotangent.astype(jnp.float32)[:, None, :] * out_rows, axis=2)
    grad_latent = jnp.sum(back_rows, axis=1).astype(jnp.bfloat16)
    return combined, grad_latent, grad_combine, grad_w_gate, grad_w_up, grad_w_down
```

```python
import jax
import jax.numpy as jnp
from jax import lax
from jax.sharding import PartitionSpec as P


def assign_slots(route_rows, expert_count):
    flat_ids = route_rows.reshape(-1)
    onehot = (flat_ids[:, None] == jnp.arange(expert_count, dtype=jnp.int32)[None, :]).astype(
        jnp.int32
    )
    ranks = jnp.cumsum(onehot, axis=0) - 1
    return (flat_ids, jnp.sum(onehot * ranks, axis=1))


def expert_forward(rows, gate_w, up_w, down_w):
    gate_pre = jnp.einsum("erl,elf->erf", rows, gate_w, preferred_element_type=jnp.float32)
    up_pre = jnp.einsum("erl,elf->erf", rows, up_w, preferred_element_type=jnp.float32)
    sigma = jax.nn.sigmoid(gate_pre)
    silu_val = gate_pre * sigma
    hidden = (silu_val * up_pre).astype(jnp.bfloat16)
    expert_out = jnp.einsum(
        "erf,efl->erl", hidden, down_w, preferred_element_type=jnp.float32
    ).astype(jnp.bfloat16)
    return (expert_out, (gate_pre, up_pre, sigma, silu_val, hidden))


def expert_backward(rows, grad_out, saved, gate_w, up_w, down_w):
    gate_pre, up_pre, sigma, silu_val, hidden = saved
    grad_down = jnp.einsum(
        "erf,erl->efl", hidden, grad_out, preferred_element_type=jnp.float32
    ).astype(jnp.bfloat16)
    grad_hidden = jnp.einsum("erl,efl->erf", grad_out, down_w, preferred_element_type=jnp.float32)
    grad_gate = (grad_hidden * up_pre * sigma * (1.0 + gate_pre * (1.0 - sigma))).astype(
        jnp.bfloat16
    )
    grad_up = (grad_hidden * silu_val).astype(jnp.bfloat16)
    grad_gw = jnp.einsum(
        "erl,erf->elf", rows, grad_gate, preferred_element_type=jnp.float32
    ).astype(jnp.bfloat16)
    grad_uw = jnp.einsum("erl,erf->elf", rows, grad_up, preferred_element_type=jnp.float32).astype(
        jnp.bfloat16
    )
    grad_rows = (
        jnp.einsum("erf,elf->erl", grad_gate, gate_w, preferred_element_type=jnp.float32)
        + jnp.einsum("erf,elf->erl", grad_up, up_w, preferred_element_type=jnp.float32)
    ).astype(jnp.bfloat16)
    return (grad_rows, grad_gw, grad_uw, grad_down)


def exchanged(latent_in, routes, combine_weights, cotangent, w_gate, w_up, w_down):
    devices_ep = lax.axis_size("ep")
    local_experts = w_gate.shape[0]
    expert_count = local_experts * devices_ep
    tok_count = latent_in.shape[0]
    top_count = routes.shape[1]
    width = latent_in.shape[1]
    capacity = tok_count * top_count * 3 // (2 * expert_count)
    expert_ids, slot_ids = assign_slots(routes, expert_count)
    position = expert_ids * capacity + slot_ids
    repeated = jnp.repeat(latent_in, top_count, axis=0)
    weighted = (combine_weights[:, :, None] * cotangent.astype(jnp.float32)[:, None, :]).astype(
        jnp.bfloat16
    )
    send_rows = jnp.zeros((expert_count * capacity, width), jnp.bfloat16).at[position].set(repeated)
    send_rows = send_rows.reshape(expert_count, capacity, width)
    send_cot = (
        jnp.zeros((expert_count * capacity, width), jnp.bfloat16)
        .at[position]
        .set(weighted.reshape(-1, width))
    )
    send_cot = send_cot.reshape(expert_count, capacity, width)

    def to_local(received):
        shaped = received.reshape(devices_ep, local_experts, capacity, width)
        return shaped.transpose(1, 0, 2, 3).reshape(local_experts, devices_ep * capacity, width)

    def to_home(local_rows):
        shaped = local_rows.reshape(local_experts, devices_ep, capacity, width)
        return shaped.transpose(1, 0, 2, 3).reshape(expert_count, capacity, width)

    got_rows = lax.all_to_all(send_rows, "ep", split_axis=0, concat_axis=0, tiled=True)
    rows_local = to_local(got_rows)
    expert_out, saved = expert_forward(rows_local, w_gate, w_up, w_down)
    back_out = lax.all_to_all(to_home(expert_out), "ep", split_axis=0, concat_axis=0, tiled=True)
    got_cot = lax.all_to_all(send_cot, "ep", split_axis=0, concat_axis=0, tiled=True)
    grad_rows, grad_gw, grad_uw, grad_down = expert_backward(
        rows_local, to_local(got_cot), saved, w_gate, w_up, w_down
    )
    back_grad = lax.all_to_all(to_home(grad_rows), "ep", split_axis=0, concat_axis=0, tiled=True)
    out_rows = (
        back_out.reshape(-1, width)[position]
        .reshape(tok_count, top_count, width)
        .astype(jnp.float32)
    )
    grad_back = (
        back_grad.reshape(-1, width)[position]
        .reshape(tok_count, top_count, width)
        .astype(jnp.float32)
    )
    combined = jnp.sum(combine_weights[:, :, None] * out_rows, axis=1).astype(jnp.bfloat16)
    grad_combine = jnp.sum(cotangent.astype(jnp.float32)[:, None, :] * out_rows, axis=2)
    grad_latent = jnp.sum(grad_back, axis=1).astype(jnp.bfloat16)
    return (combined, grad_latent, grad_combine, grad_gw, grad_uw, grad_down)


def dot(a, b, dims):
    return lax.dot_general(a, b, (dims, ((), ())), preferred_element_type=jnp.float32)


def gathered(latent_in, routes, combine_weights, cotangent, w_gate, w_up, w_down):
    devices_ep = lax.axis_size("ep")
    tok_count = latent_in.shape[0]
    bf16, f32 = jnp.bfloat16, jnp.float32
    chosen = routes[:, :, None] == jnp.arange(devices_ep, dtype=jnp.int32)[None, None, :]
    share = jnp.sum(jnp.where(chosen, combine_weights[:, :, None], 0.0), axis=1)
    share = lax.all_to_all(
        share.T.reshape(devices_ep, 1, tok_count), "ep", split_axis=0, concat_axis=0, tiled=True
    )
    share = share.reshape(devices_ep * tok_count, 1)
    rows = lax.all_gather(latent_in, "ep", axis=0, tiled=True)
    cot = lax.all_gather(cotangent, "ep", axis=0, tiled=True)
    gate_w, up_w, down_w = w_gate[0], w_up[0], w_down[0]

    gate_pre = dot(rows, gate_w, ((1,), (0,)))
    up_pre = dot(rows, up_w, ((1,), (0,)))
    sigma = jax.nn.sigmoid(gate_pre)
    silu_val = gate_pre * sigma
    hidden = (silu_val * up_pre).astype(bf16)
    out = dot(hidden, down_w, ((1,), (0,)))
    back_out = lax.psum_scatter(
        (share * out).astype(bf16), "ep", scatter_dimension=0, tiled=True
    )
    cot32 = cot.astype(f32)
    inner = jnp.sum(cot32 * out, axis=1)
    inner = lax.all_to_all(
        inner.reshape(devices_ep, tok_count), "ep", split_axis=0, concat_axis=0, tiled=True
    )
    weighted = (share * cot32).astype(bf16)
    grad_hidden = dot(weighted, down_w, ((1,), (1,)))
    grad_gate = (grad_hidden * up_pre * sigma * (1.0 + gate_pre * (1.0 - sigma))).astype(bf16)
    grad_up = (grad_hidden * silu_val).astype(bf16)
    grad_rows = dot(grad_gate, gate_w, ((1,), (1,))) + dot(grad_up, up_w, ((1,), (1,)))
    back_grad = lax.psum_scatter(
        grad_rows.astype(bf16), "ep", scatter_dimension=0, tiled=True
    )
    grad_down = dot(hidden, weighted, ((0,), (0,))).astype(bf16)
    grad_gw = dot(rows, grad_gate, ((0,), (0,))).astype(bf16)
    grad_uw = dot(rows, grad_up, ((0,), (0,))).astype(bf16)
    grad_combine = jnp.sum(jnp.where(chosen, inner.T[:, None, :], 0.0), axis=2)
    return (back_out, back_grad, grad_combine, grad_gw[None], grad_uw[None], grad_down[None])


def local(latent_in, routes, combine_weights, cotangent, w_gate, w_up, w_down):
    every = latent_in.shape[0] * lax.axis_size("ep")
    slots = latent_in.shape[0] * routes.shape[1] * 3 // 2
    plan = gathered if w_gate.shape[0] == 1 and every <= 2 * slots else exchanged
    return plan(latent_in, routes, combine_weights, cotangent, w_gate, w_up, w_down)


def solution(mesh):
    return jax.shard_map(
        local,
        mesh=mesh,
        in_specs=(
            P(("grp", "ep"), None),
            P(("grp", "ep"), None),
            P(("grp", "ep"), None),
            P(("grp", "ep"), None),
            P("ep", None, None),
            P("ep", None, None),
            P("ep", None, None),
        ),
        out_specs=(
            P(("grp", "ep"), None),
            P(("grp", "ep"), None),
            P(("grp", "ep"), None),
            P(("grp", "ep"), None, None),
            P(("grp", "ep"), None, None),
            P(("grp", "ep"), None, None),
        ),
        check_vma=False,
    )
```

```python
import jax
import jax.numpy as jnp
from jax import lax
from jax.sharding import PartitionSpec as P


def assign_slots(route_rows, expert_count):
    flat_ids = route_rows.reshape(-1)
    onehot = (flat_ids[:, None] == jnp.arange(expert_count, dtype=jnp.int32)[None, :]).astype(
        jnp.int32
    )
    ranks = jnp.cumsum(onehot, axis=0) - 1
    return (flat_ids, jnp.sum(onehot * ranks, axis=1))


def expert_forward(rows, gate_w, up_w, down_w):
    gate_pre = jnp.einsum("erl,elf->erf", rows, gate_w, preferred_element_type=jnp.float32)
    up_pre = jnp.einsum("erl,elf->erf", rows, up_w, preferred_element_type=jnp.float32)
    sigma = jax.nn.sigmoid(gate_pre)
    silu_val = gate_pre * sigma
    hidden = (silu_val * up_pre).astype(jnp.bfloat16)
    expert_out = jnp.einsum(
        "erf,efl->erl", hidden, down_w, preferred_element_type=jnp.float32
    ).astype(jnp.bfloat16)
    return (expert_out, (gate_pre, up_pre, sigma, silu_val, hidden))


def expert_backward(rows, grad_out, saved, gate_w, up_w, down_w):
    gate_pre, up_pre, sigma, silu_val, hidden = saved
    grad_down = jnp.einsum(
        "erf,erl->efl", hidden, grad_out, preferred_element_type=jnp.float32
    ).astype(jnp.bfloat16)
    grad_hidden = jnp.einsum("erl,efl->erf", grad_out, down_w, preferred_element_type=jnp.float32)
    grad_gate = (grad_hidden * up_pre * sigma * (1.0 + gate_pre * (1.0 - sigma))).astype(
        jnp.bfloat16
    )
    grad_up = (grad_hidden * silu_val).astype(jnp.bfloat16)
    grad_gw = jnp.einsum(
        "erl,erf->elf", rows, grad_gate, preferred_element_type=jnp.float32
    ).astype(jnp.bfloat16)
    grad_uw = jnp.einsum("erl,erf->elf", rows, grad_up, preferred_element_type=jnp.float32).astype(
        jnp.bfloat16
    )
    grad_rows = (
        jnp.einsum("erf,elf->erl", grad_gate, gate_w, preferred_element_type=jnp.float32)
        + jnp.einsum("erf,elf->erl", grad_up, up_w, preferred_element_type=jnp.float32)
    ).astype(jnp.bfloat16)
    return (grad_rows, grad_gw, grad_uw, grad_down)


def exchanged(latent_in, routes, combine_weights, cotangent, w_gate, w_up, w_down):
    devices_ep = lax.axis_size("ep")
    local_experts = w_gate.shape[0]
    expert_count = local_experts * devices_ep
    tok_count = latent_in.shape[0]
    top_count = routes.shape[1]
    width = latent_in.shape[1]
    capacity = tok_count * top_count * 3 // (2 * expert_count)
    expert_ids, slot_ids = assign_slots(routes, expert_count)
    position = expert_ids * capacity + slot_ids
    repeated = jnp.repeat(latent_in, top_count, axis=0)
    weighted = (combine_weights[:, :, None] * cotangent.astype(jnp.float32)[:, None, :]).astype(
        jnp.bfloat16
    )
    send_rows = jnp.zeros((expert_count * capacity, width), jnp.bfloat16).at[position].set(repeated)
    send_rows = send_rows.reshape(expert_count, capacity, width)
    send_cot = (
        jnp.zeros((expert_count * capacity, width), jnp.bfloat16)
        .at[position]
        .set(weighted.reshape(-1, width))
    )
    send_cot = send_cot.reshape(expert_count, capacity, width)

    def to_local(received):
        shaped = received.reshape(devices_ep, local_experts, capacity, width)
        return shaped.transpose(1, 0, 2, 3).reshape(local_experts, devices_ep * capacity, width)

    def to_home(local_rows):
        shaped = local_rows.reshape(local_experts, devices_ep, capacity, width)
        return shaped.transpose(1, 0, 2, 3).reshape(expert_count, capacity, width)

    got_rows = lax.all_to_all(send_rows, "ep", split_axis=0, concat_axis=0, tiled=True)
    rows_local = to_local(got_rows)
    expert_out, saved = expert_forward(rows_local, w_gate, w_up, w_down)
    back_out = lax.all_to_all(to_home(expert_out), "ep", split_axis=0, concat_axis=0, tiled=True)
    got_cot = lax.all_to_all(send_cot, "ep", split_axis=0, concat_axis=0, tiled=True)
    grad_rows, grad_gw, grad_uw, grad_down = expert_backward(
        rows_local, to_local(got_cot), saved, w_gate, w_up, w_down
    )
    back_grad = lax.all_to_all(to_home(grad_rows), "ep", split_axis=0, concat_axis=0, tiled=True)
    out_rows = (
        back_out.reshape(-1, width)[position]
        .reshape(tok_count, top_count, width)
        .astype(jnp.float32)
    )
    grad_back = (
        back_grad.reshape(-1, width)[position]
        .reshape(tok_count, top_count, width)
        .astype(jnp.float32)
    )
    combined = jnp.sum(combine_weights[:, :, None] * out_rows, axis=1).astype(jnp.bfloat16)
    grad_combine = jnp.sum(cotangent.astype(jnp.float32)[:, None, :] * out_rows, axis=2)
    grad_latent = jnp.sum(grad_back, axis=1).astype(jnp.bfloat16)
    return (combined, grad_latent, grad_combine, grad_gw, grad_uw, grad_down)


def dot(a, b, dims):
    return lax.dot_general(a, b, (dims, ((), ())), preferred_element_type=jnp.float32)


def swap(value, bit):
    pairs = [(i, i ^ bit) for i in range(lax.axis_size("ep"))]
    return lax.ppermute(value, "ep", pairs)


CORE, SIDE, NEAR, FAR = 1, 2, 4, 8
REACH = (0, NEAR, FAR, NEAR | FAR, SIDE, SIDE | NEAR, SIDE | FAR, SIDE | NEAR | FAR)


def collect(block):
    near = swap(block, NEAR)
    far = swap(block, FAR)
    both = swap(far, NEAR)
    line = [block, near, far, both]
    return line + [swap(item, SIDE) for item in line]


def give_back(parts):
    bf16, f32 = jnp.bfloat16, jnp.float32
    other = [swap(item, SIDE) for item in parts[4:]]
    line = [a.astype(f32) + b.astype(f32) for a, b in zip(parts[:4], other)]
    both = swap(line[3].astype(bf16), NEAR)
    near = swap(line[1].astype(bf16), NEAR)
    far = swap((line[2] + both.astype(f32)).astype(bf16), FAR)
    return (line[0] + near.astype(f32) + far.astype(f32)).astype(bf16)


def paired(latent_in, routes, combine_weights, cotangent, w_gate, w_up, w_down):
    devices_ep = lax.axis_size("ep")
    me = lax.axis_index("ep")
    tok_count = latent_in.shape[0]
    bf16, f32 = jnp.bfloat16, jnp.float32
    experts = jnp.arange(devices_ep, dtype=jnp.int32)
    sources = jnp.stack([me ^ bits for bits in REACH])
    mine = jnp.stack([me, me ^ CORE])

    chosen = routes[None, :, :] == experts[:, None, None]
    share = jnp.sum(jnp.where(chosen, combine_weights[None, :, :], 0.0), axis=2)
    share = lax.all_gather(share, "ep", axis=0, tiled=False)
    rows = jnp.concatenate(collect(latent_in), axis=0)
    weights = [w_gate[0], w_up[0], w_down[0]]
    both_w = [weights, [swap(w, CORE) for w in weights]]
    cot = jnp.concatenate(collect(cotangent), axis=0)
    share = share[sources][:, mine, :]

    partial_out, saved = 0.0, []
    for i, (gate_w, up_w, down_w) in enumerate(both_w):
        part = share[:, i, :].reshape(-1, 1)
        gate_pre = dot(rows, gate_w, ((1,), (0,)))
        up_pre = dot(rows, up_w, ((1,), (0,)))
        sigma = jax.nn.sigmoid(gate_pre)
        silu_val = gate_pre * sigma
        hidden = silu_val * up_pre
        weighted = (part * hidden).astype(bf16)
        partial_out = partial_out + dot(weighted, down_w, ((1,), (0,)))
        saved.append((part, gate_pre, up_pre, sigma, silu_val, hidden, weighted))
    back = partial_out.astype(bf16).reshape(len(REACH), tok_count, -1)
    combined = give_back([back[i] for i in range(len(REACH))])

    inner, grad_rows, grads = [], 0.0, []
    for (gate_w, up_w, down_w), kept in zip(both_w, saved):
        part, gate_pre, up_pre, sigma, silu_val, hidden, weighted = kept
        plain = dot(cot, down_w, ((1,), (1,)))
        inner.append(jnp.sum(hidden * plain, axis=1).reshape(len(REACH), tok_count))
        grad_hidden = part * plain
        grad_gate = (grad_hidden * up_pre * sigma * (1.0 + gate_pre * (1.0 - sigma))).astype(bf16)
        grad_up = (grad_hidden * silu_val).astype(bf16)
        grad_rows = grad_rows + dot(grad_gate, gate_w, ((1,), (1,)))
        grad_rows = grad_rows + dot(grad_up, up_w, ((1,), (1,)))
        grads.append((weighted, grad_gate, grad_up))
    inner = jnp.stack(inner, axis=1)
    at_source = (sources[None, :] == experts[:, None]).astype(f32)
    at_expert = (mine[None, :] == experts[:, None]).astype(f32)
    inner = jnp.einsum("ds,ei,sit->det", at_source, at_expert, inner, precision="highest")
    inner = lax.psum_scatter(inner, "ep", scatter_dimension=0, tiled=False)
    grad_combine = jnp.sum(jnp.where(chosen, inner[:, :, None], 0.0), axis=0)

    back = grad_rows.astype(bf16).reshape(len(REACH), tok_count, -1)
    grad_latent = give_back([back[i] for i in range(len(REACH))])

    def weight_grads(weighted, grad_gate, grad_up):
        return (
            dot(rows, grad_gate, ((0,), (0,))),
            dot(rows, grad_up, ((0,), (0,))),
            dot(weighted, cot, ((0,), (0,))),
        )

    away = [swap(g.astype(bf16), CORE) for g in weight_grads(*grads[1])]
    grad_w = [(g + a.astype(f32)).astype(bf16)[None] for g, a in zip(weight_grads(*grads[0]), away)]
    return (combined, grad_latent, grad_combine, *grad_w)


def local(latent_in, routes, combine_weights, cotangent, w_gate, w_up, w_down):
    plan = paired if w_gate.shape[0] == 1 and lax.axis_size("ep") == 2 * len(REACH) else exchanged
    return plan(latent_in, routes, combine_weights, cotangent, w_gate, w_up, w_down)


def solution(mesh):
    return jax.shard_map(
        local,
        mesh=mesh,
        in_specs=(
            P(("grp", "ep"), None),
            P(("grp", "ep"), None),
            P(("grp", "ep"), None),
            P(("grp", "ep"), None),
            P("ep", None, None),
            P("ep", None, None),
            P("ep", None, None),
        ),
        out_specs=(
            P(("grp", "ep"), None),
            P(("grp", "ep"), None),
            P(("grp", "ep"), None),
            P(("grp", "ep"), None, None),
            P(("grp", "ep"), None, None),
            P(("grp", "ep"), None, None),
        ),
        check_vma=False,
    )
```

```python
import jax
import jax.numpy as jnp
from jax import lax
from jax.sharding import PartitionSpec as P


def assign_slots(route_rows, expert_count):
    flat_ids = route_rows.reshape(-1)
    onehot = (flat_ids[:, None] == jnp.arange(expert_count, dtype=jnp.int32)[None, :]).astype(
        jnp.int32
    )
    ranks = jnp.cumsum(onehot, axis=0) - 1
    return (flat_ids, jnp.sum(onehot * ranks, axis=1))


def expert_forward(rows, gate_w, up_w, down_w):
    gate_pre = jnp.einsum("erl,elf->erf", rows, gate_w, preferred_element_type=jnp.float32)
    up_pre = jnp.einsum("erl,elf->erf", rows, up_w, preferred_element_type=jnp.float32)
    sigma = jax.nn.sigmoid(gate_pre)
    silu_val = gate_pre * sigma
    hidden = (silu_val * up_pre).astype(jnp.bfloat16)
    expert_out = jnp.einsum(
        "erf,efl->erl", hidden, down_w, preferred_element_type=jnp.float32
    ).astype(jnp.bfloat16)
    return (expert_out, (gate_pre, up_pre, sigma, silu_val, hidden))


def expert_backward(rows, grad_out, saved, gate_w, up_w, down_w):
    gate_pre, up_pre, sigma, silu_val, hidden = saved
    grad_down = jnp.einsum(
        "erf,erl->efl", hidden, grad_out, preferred_element_type=jnp.float32
    ).astype(jnp.bfloat16)
    grad_hidden = jnp.einsum("erl,efl->erf", grad_out, down_w, preferred_element_type=jnp.float32)
    grad_gate = (grad_hidden * up_pre * sigma * (1.0 + gate_pre * (1.0 - sigma))).astype(
        jnp.bfloat16
    )
    grad_up = (grad_hidden * silu_val).astype(jnp.bfloat16)
    grad_gw = jnp.einsum(
        "erl,erf->elf", rows, grad_gate, preferred_element_type=jnp.float32
    ).astype(jnp.bfloat16)
    grad_uw = jnp.einsum("erl,erf->elf", rows, grad_up, preferred_element_type=jnp.float32).astype(
        jnp.bfloat16
    )
    grad_rows = (
        jnp.einsum("erf,elf->erl", grad_gate, gate_w, preferred_element_type=jnp.float32)
        + jnp.einsum("erf,elf->erl", grad_up, up_w, preferred_element_type=jnp.float32)
    ).astype(jnp.bfloat16)
    return (grad_rows, grad_gw, grad_uw, grad_down)


def exchanged(latent_in, routes, combine_weights, cotangent, w_gate, w_up, w_down):
    devices_ep = lax.axis_size("ep")
    local_experts = w_gate.shape[0]
    expert_count = local_experts * devices_ep
    tok_count = latent_in.shape[0]
    top_count = routes.shape[1]
    width = latent_in.shape[1]
    capacity = tok_count * top_count * 3 // (2 * expert_count)
    expert_ids, slot_ids = assign_slots(routes, expert_count)
    position = expert_ids * capacity + slot_ids
    repeated = jnp.repeat(latent_in, top_count, axis=0)
    weighted = (combine_weights[:, :, None] * cotangent.astype(jnp.float32)[:, None, :]).astype(
        jnp.bfloat16
    )
    send_rows = jnp.zeros((expert_count * capacity, width), jnp.bfloat16).at[position].set(repeated)
    send_rows = send_rows.reshape(expert_count, capacity, width)
    send_cot = (
        jnp.zeros((expert_count * capacity, width), jnp.bfloat16)
        .at[position]
        .set(weighted.reshape(-1, width))
    )
    send_cot = send_cot.reshape(expert_count, capacity, width)

    def to_local(received):
        shaped = received.reshape(devices_ep, local_experts, capacity, width)
        return shaped.transpose(1, 0, 2, 3).reshape(local_experts, devices_ep * capacity, width)

    def to_home(local_rows):
        shaped = local_rows.reshape(local_experts, devices_ep, capacity, width)
        return shaped.transpose(1, 0, 2, 3).reshape(expert_count, capacity, width)

    got_rows = lax.all_to_all(send_rows, "ep", split_axis=0, concat_axis=0, tiled=True)
    rows_local = to_local(got_rows)
    expert_out, saved = expert_forward(rows_local, w_gate, w_up, w_down)
    back_out = lax.all_to_all(to_home(expert_out), "ep", split_axis=0, concat_axis=0, tiled=True)
    got_cot = lax.all_to_all(send_cot, "ep", split_axis=0, concat_axis=0, tiled=True)
    grad_rows, grad_gw, grad_uw, grad_down = expert_backward(
        rows_local, to_local(got_cot), saved, w_gate, w_up, w_down
    )
    back_grad = lax.all_to_all(to_home(grad_rows), "ep", split_axis=0, concat_axis=0, tiled=True)
    out_rows = (
        back_out.reshape(-1, width)[position]
        .reshape(tok_count, top_count, width)
        .astype(jnp.float32)
    )
    grad_back = (
        back_grad.reshape(-1, width)[position]
        .reshape(tok_count, top_count, width)
        .astype(jnp.float32)
    )
    combined = jnp.sum(combine_weights[:, :, None] * out_rows, axis=1).astype(jnp.bfloat16)
    grad_combine = jnp.sum(cotangent.astype(jnp.float32)[:, None, :] * out_rows, axis=2)
    grad_latent = jnp.sum(grad_back, axis=1).astype(jnp.bfloat16)
    return (combined, grad_latent, grad_combine, grad_gw, grad_uw, grad_down)


def dot(a, b, dims):
    return lax.dot_general(a, b, (dims, ((), ())), preferred_element_type=jnp.float32)


def swap(value, bit):
    pairs = [(i, i ^ bit) for i in range(lax.axis_size("ep"))]
    return lax.ppermute(value, "ep", pairs)


CORE, SIDE, NEAR, FAR = 1, 2, 4, 8
REACH = (0, NEAR, FAR, NEAR | FAR, SIDE, SIDE | NEAR, SIDE | FAR, SIDE | NEAR | FAR)
HALVED = (0, SIDE, FAR, FAR | SIDE, NEAR, NEAR | SIDE, NEAR | FAR, NEAR | FAR | SIDE)


def collect(block):
    near = swap(block, NEAR)
    far = swap(block, FAR)
    both = swap(far, NEAR)
    line = [block, near, far, both]
    return line + [swap(item, SIDE) for item in line]


def give_back(parts):
    bf16, f32 = jnp.bfloat16, jnp.float32
    other = [swap(item, SIDE) for item in parts[4:]]
    line = [a.astype(f32) + b.astype(f32) for a, b in zip(parts[:4], other)]
    both = swap(line[3].astype(bf16), NEAR)
    near = swap(line[1].astype(bf16), NEAR)
    far = swap((line[2] + both.astype(f32)).astype(bf16), FAR)
    return (line[0] + near.astype(f32) + far.astype(f32)).astype(bf16)


def collect_small(value):
    value = value[None]
    for bit in (NEAR, FAR, SIDE):
        value = jnp.concatenate([value, swap(value, bit)], axis=0)
    return value


def give_back_small(parts):
    count = len(REACH)
    parts = parts[:, None]
    for bit in (SIDE, FAR, NEAR):
        count = count // 2
        parts = jnp.concatenate([parts[:count], swap(parts[count:], bit)], axis=1)
    return parts[0]


def paired(latent_in, routes, combine_weights, cotangent, w_gate, w_up, w_down):
    devices_ep = lax.axis_size("ep")
    me = lax.axis_index("ep")
    tok_count = latent_in.shape[0]
    bf16, f32 = jnp.bfloat16, jnp.float32
    experts = jnp.arange(devices_ep, dtype=jnp.int32)
    mine = jnp.stack([me, me ^ CORE])

    chosen = routes[None, :, :] == experts[:, None, None]
    share = jnp.sum(jnp.where(chosen, combine_weights[None, :, :], 0.0), axis=2)
    share = collect_small(share)
    rows = jnp.concatenate(collect(latent_in), axis=0)
    weights = [w_gate[0], w_up[0], w_down[0]]
    both_w = [weights, [swap(w, CORE) for w in weights]]
    cot = jnp.concatenate(collect(cotangent), axis=0)
    share = share[:, mine, :]

    partial_out, saved = 0.0, []
    for i, (gate_w, up_w, down_w) in enumerate(both_w):
        part = share[:, i, :].reshape(-1, 1)
        gate_pre = dot(rows, gate_w, ((1,), (0,)))
        up_pre = dot(rows, up_w, ((1,), (0,)))
        sigma = jax.nn.sigmoid(gate_pre)
        silu_val = gate_pre * sigma
        hidden = silu_val * up_pre
        weighted = (part * hidden).astype(bf16)
        partial_out = partial_out + dot(weighted, down_w, ((1,), (0,)))
        saved.append((part, gate_pre, up_pre, sigma, silu_val, hidden, weighted))
    back = partial_out.astype(bf16).reshape(len(REACH), tok_count, -1)
    combined = give_back([back[i] for i in range(len(REACH))])

    inner, grad_rows, grads = [], 0.0, []
    for (gate_w, up_w, down_w), kept in zip(both_w, saved):
        part, gate_pre, up_pre, sigma, silu_val, hidden, weighted = kept
        plain = dot(cot, down_w, ((1,), (1,)))
        inner.append(jnp.sum(hidden * plain, axis=1).reshape(len(REACH), tok_count))
        grad_hidden = part * plain
        grad_gate = (grad_hidden * up_pre * sigma * (1.0 + gate_pre * (1.0 - sigma))).astype(bf16)
        grad_up = (grad_hidden * silu_val).astype(bf16)
        grad_rows = grad_rows + dot(grad_gate, gate_w, ((1,), (1,)))
        grad_rows = grad_rows + dot(grad_up, up_w, ((1,), (1,)))
        grads.append((weighted, grad_gate, grad_up))
    inner = jnp.stack(inner, axis=1)
    inner = give_back_small(inner)
    owner = jnp.stack([me ^ bits for bits in HALVED])
    owner = jnp.stack([owner, owner ^ CORE], axis=1)
    owns = routes[None, None, :, :] == owner[:, :, None, None]
    grad_combine = jnp.sum(jnp.where(owns, inner[:, :, :, None], 0.0), axis=(0, 1))

    back = grad_rows.astype(bf16).reshape(len(REACH), tok_count, -1)
    grad_latent = give_back([back[i] for i in range(len(REACH))])

    def weight_grads(weighted, grad_gate, grad_up):
        return (
            dot(rows, grad_gate, ((0,), (0,))),
            dot(rows, grad_up, ((0,), (0,))),
            dot(weighted, cot, ((0,), (0,))),
        )

    away = [swap(g.astype(bf16), CORE) for g in weight_grads(*grads[1])]
    grad_w = [(g + a.astype(f32)).astype(bf16)[None] for g, a in zip(weight_grads(*grads[0]), away)]
    return (combined, grad_latent, grad_combine, *grad_w)


def local(latent_in, routes, combine_weights, cotangent, w_gate, w_up, w_down):
    plan = paired if w_gate.shape[0] == 1 and lax.axis_size("ep") == 2 * len(REACH) else exchanged
    return plan(latent_in, routes, combine_weights, cotangent, w_gate, w_up, w_down)


def solution(mesh):
    return jax.shard_map(
        local,
        mesh=mesh,
        in_specs=(
            P(("grp", "ep"), None),
            P(("grp", "ep"), None),
            P(("grp", "ep"), None),
            P(("grp", "ep"), None),
            P("ep", None, None),
            P("ep", None, None),
            P("ep", None, None),
        ),
        out_specs=(
            P(("grp", "ep"), None),
            P(("grp", "ep"), None),
            P(("grp", "ep"), None),
            P(("grp", "ep"), None, None),
            P(("grp", "ep"), None, None),
            P(("grp", "ep"), None, None),
        ),
        check_vma=False,
    )
```

```python
import jax
import jax.numpy as jnp
from jax import lax
from jax.experimental import pallas as pl
from jax.experimental.pallas import tpu as pltpu
from jax.sharding import PartitionSpec as P


def assign_slots(route_rows, expert_count):
    flat_ids = route_rows.reshape(-1)
    onehot = (flat_ids[:, None] == jnp.arange(expert_count, dtype=jnp.int32)[None, :]).astype(
        jnp.int32
    )
    ranks = jnp.cumsum(onehot, axis=0) - 1
    return (flat_ids, jnp.sum(onehot * ranks, axis=1))


def expert_forward(rows, gate_w, up_w, down_w):
    gate_pre = jnp.einsum("erl,elf->erf", rows, gate_w, preferred_element_type=jnp.float32)
    up_pre = jnp.einsum("erl,elf->erf", rows, up_w, preferred_element_type=jnp.float32)
    sigma = jax.nn.sigmoid(gate_pre)
    silu_val = gate_pre * sigma
    hidden = (silu_val * up_pre).astype(jnp.bfloat16)
    expert_out = jnp.einsum(
        "erf,efl->erl", hidden, down_w, preferred_element_type=jnp.float32
    ).astype(jnp.bfloat16)
    return (expert_out, (gate_pre, up_pre, sigma, silu_val, hidden))


def expert_backward(rows, grad_out, saved, gate_w, up_w, down_w):
    gate_pre, up_pre, sigma, silu_val, hidden = saved
    grad_down = jnp.einsum(
        "erf,erl->efl", hidden, grad_out, preferred_element_type=jnp.float32
    ).astype(jnp.bfloat16)
    grad_hidden = jnp.einsum("erl,efl->erf", grad_out, down_w, preferred_element_type=jnp.float32)
    grad_gate = (grad_hidden * up_pre * sigma * (1.0 + gate_pre * (1.0 - sigma))).astype(
        jnp.bfloat16
    )
    grad_up = (grad_hidden * silu_val).astype(jnp.bfloat16)
    grad_gw = jnp.einsum(
        "erl,erf->elf", rows, grad_gate, preferred_element_type=jnp.float32
    ).astype(jnp.bfloat16)
    grad_uw = jnp.einsum("erl,erf->elf", rows, grad_up, preferred_element_type=jnp.float32).astype(
        jnp.bfloat16
    )
    grad_rows = (
        jnp.einsum("erf,elf->erl", grad_gate, gate_w, preferred_element_type=jnp.float32)
        + jnp.einsum("erf,elf->erl", grad_up, up_w, preferred_element_type=jnp.float32)
    ).astype(jnp.bfloat16)
    return (grad_rows, grad_gw, grad_uw, grad_down)


def exchanged(latent_in, routes, combine_weights, cotangent, w_gate, w_up, w_down):
    devices_ep = lax.axis_size("ep")
    local_experts = w_gate.shape[0]
    expert_count = local_experts * devices_ep
    tok_count = latent_in.shape[0]
    top_count = routes.shape[1]
    width = latent_in.shape[1]
    capacity = tok_count * top_count * 3 // (2 * expert_count)
    expert_ids, slot_ids = assign_slots(routes, expert_count)
    position = expert_ids * capacity + slot_ids
    repeated = jnp.repeat(latent_in, top_count, axis=0)
    weighted = (combine_weights[:, :, None] * cotangent.astype(jnp.float32)[:, None, :]).astype(
        jnp.bfloat16
    )
    send_rows = jnp.zeros((expert_count * capacity, width), jnp.bfloat16).at[position].set(repeated)
    send_rows = send_rows.reshape(expert_count, capacity, width)
    send_cot = (
        jnp.zeros((expert_count * capacity, width), jnp.bfloat16)
        .at[position]
        .set(weighted.reshape(-1, width))
    )
    send_cot = send_cot.reshape(expert_count, capacity, width)

    def to_local(received):
        shaped = received.reshape(devices_ep, local_experts, capacity, width)
        return shaped.transpose(1, 0, 2, 3).reshape(local_experts, devices_ep * capacity, width)

    def to_home(local_rows):
        shaped = local_rows.reshape(local_experts, devices_ep, capacity, width)
        return shaped.transpose(1, 0, 2, 3).reshape(expert_count, capacity, width)

    got_rows = lax.all_to_all(send_rows, "ep", split_axis=0, concat_axis=0, tiled=True)
    rows_local = to_local(got_rows)
    expert_out, saved = expert_forward(rows_local, w_gate, w_up, w_down)
    back_out = lax.all_to_all(to_home(expert_out), "ep", split_axis=0, concat_axis=0, tiled=True)
    got_cot = lax.all_to_all(send_cot, "ep", split_axis=0, concat_axis=0, tiled=True)
    grad_rows, grad_gw, grad_uw, grad_down = expert_backward(
        rows_local, to_local(got_cot), saved, w_gate, w_up, w_down
    )
    back_grad = lax.all_to_all(to_home(grad_rows), "ep", split_axis=0, concat_axis=0, tiled=True)
    out_rows = (
        back_out.reshape(-1, width)[position]
        .reshape(tok_count, top_count, width)
        .astype(jnp.float32)
    )
    grad_back = (
        back_grad.reshape(-1, width)[position]
        .reshape(tok_count, top_count, width)
        .astype(jnp.float32)
    )
    combined = jnp.sum(combine_weights[:, :, None] * out_rows, axis=1).astype(jnp.bfloat16)
    grad_combine = jnp.sum(cotangent.astype(jnp.float32)[:, None, :] * out_rows, axis=2)
    grad_latent = jnp.sum(grad_back, axis=1).astype(jnp.bfloat16)
    return (combined, grad_latent, grad_combine, grad_gw, grad_uw, grad_down)


def dot(a, b, dims):
    return lax.dot_general(a, b, (dims, ((), ())), preferred_element_type=jnp.float32)


def swap(value, bit):
    pairs = [(i, i ^ bit) for i in range(lax.axis_size("ep"))]
    return lax.ppermute(value, "ep", pairs)


CORE, SIDE, NEAR, FAR = 1, 2, 4, 8
REACH = (0, NEAR, FAR, NEAR | FAR, SIDE, SIDE | NEAR, SIDE | FAR, SIDE | NEAR | FAR)
HALVED = (0, SIDE, FAR, FAR | SIDE, NEAR, NEAR | SIDE, NEAR | FAR, NEAR | FAR | SIDE)


def fence(*values):
    return lax.optimization_barrier(values)


def added(a, b):
    return a.astype(jnp.float32) + b.astype(jnp.float32)


def narrow(value):
    return value.astype(jnp.bfloat16)


MIB = 1 << 20


def kernel(body, outs, flops, *operands):
    whole = pl.BlockSpec(memory_space=pltpu.VMEM)
    moved = sum(v.size * v.dtype.itemsize for v in (*operands, *outs))
    return pl.pallas_call(
        body,
        out_shape=outs,
        in_specs=[whole] * len(operands),
        out_specs=[whole] * len(outs),
        compiler_params=pltpu.CompilerParams(vmem_limit_bytes=24 * MIB),
        cost_estimate=pl.CostEstimate(flops=flops, bytes_accessed=moved, transcendentals=0),
    )(*operands)


def shape(rows, columns, dtype):
    return jax.ShapeDtypeStruct((rows, columns), dtype)


def forward(blocks, weights, share):
    bf16, f32 = jnp.bfloat16, jnp.float32
    count, (tok_count, width) = len(blocks), blocks[0].shape
    units, half = weights[0][0].shape[1], len(blocks) // 2
    every = count * tok_count

    def body(*refs):
        x_refs, refs = refs[:count], refs[count:]
        w_refs, share_ref, refs = (refs[0:3], refs[3:6]), refs[6], refs[7:]
        y_refs, (rows_ref, gate_ref, up_ref, weighted_ref) = refs[:count], refs[count:]
        for i, x_ref in enumerate(x_refs):
            rows_ref[i * tok_count : (i + 1) * tok_count, :] = x_ref[...]
        for start in (half, 0):
            at = slice(start * tok_count, (start + half) * tok_count)
            x, total = rows_ref[at, :], 0.0
            for e, (gate_w, up_w, down_w) in enumerate(w_refs):
                lanes = slice(e * units, (e + 1) * units)
                gate_pre = dot(x, gate_w[...], ((1,), (0,)))
                up_pre = dot(x, up_w[...], ((1,), (0,)))
                gate_ref[at, lanes] = gate_pre
                up_ref[at, lanes] = up_pre
                hidden = gate_pre * jax.nn.sigmoid(gate_pre) * up_pre
                part = []
                for j in range(half):
                    column = e * count + start + j
                    part.append(share_ref[:, column : column + 1])
                weighted = (jnp.concatenate(part, axis=0) * hidden).astype(bf16)
                weighted_ref[at, lanes] = weighted
                total = total + dot(weighted, down_w[...], ((1,), (0,)))
            for j in range(half):
                y_refs[start + j][...] = total[j * tok_count : (j + 1) * tok_count].astype(bf16)

    outs = [shape(tok_count, width, bf16)] * count + [
        shape(every, width, bf16),
        shape(every, 2 * units, f32),
        shape(every, 2 * units, f32),
        shape(every, 2 * units, bf16),
    ]
    flops = 12 * every * width * units
    outs = kernel(body, outs, flops, *blocks, *weights[0], *weights[1], share)
    return outs[:count], *outs[count:]


def backward(blocks, weights, share, gate_pre, up_pre):
    bf16, f32 = jnp.bfloat16, jnp.float32
    count, (tok_count, width) = len(blocks), blocks[0].shape
    units, half = weights[0][0].shape[1], len(blocks) // 2
    every = count * tok_count

    def body(*refs):
        c_refs, refs = refs[:count], refs[count:]
        w_refs, (share_ref, gate_ref, up_ref), refs = (refs[0:3], refs[3:6]), refs[6:9], refs[9:]
        g_refs, (cot_ref, inner_ref, factor_ref) = refs[:count], refs[count:]
        for i, c_ref in enumerate(c_refs):
            cot_ref[i * tok_count : (i + 1) * tok_count, :] = c_ref[...]
        for start in (half, 0):
            at = slice(start * tok_count, (start + half) * tok_count)
            cot, total = cot_ref[at, :], 0.0
            for e, (gate_w, up_w, down_w) in enumerate(w_refs):
                lanes = slice(e * units, (e + 1) * units)
                plain = dot(cot, down_w[...], ((1,), (1,)))
                gate, up = gate_ref[at, lanes], up_ref[at, lanes]
                sigma = jax.nn.sigmoid(gate)
                silu_val = gate * sigma
                inner = jnp.sum(silu_val * up * plain, axis=1, keepdims=True)
                part = []
                for j in range(half):
                    column = e * count + start + j
                    part.append(share_ref[:, column : column + 1])
                    inner_ref[:, column : column + 1] = inner[j * tok_count : (j + 1) * tok_count]
                grad_hidden = jnp.concatenate(part, axis=0) * plain
                slope = sigma * (1.0 + gate * (1.0 - sigma))
                grad_gate = (grad_hidden * up * slope).astype(bf16)
                grad_up = (grad_hidden * silu_val).astype(bf16)
                factor_ref[at, 2 * e * units : (2 * e + 1) * units] = grad_gate
                factor_ref[at, (2 * e + 1) * units : (2 * e + 2) * units] = grad_up
                total = total + dot(grad_gate, gate_w[...], ((1,), (1,)))
                total = total + dot(grad_up, up_w[...], ((1,), (1,)))
            for j in range(half):
                g_refs[start + j][...] = total[j * tok_count : (j + 1) * tok_count].astype(bf16)

    outs = [shape(tok_count, width, bf16)] * count + [
        shape(every, width, bf16),
        shape(tok_count, 2 * count, f32),
        shape(every, 4 * units, bf16),
    ]
    flops = 12 * every * width * units
    outs = kernel(body, outs, flops, *blocks, *weights[0], *weights[1], share, gate_pre, up_pre)
    return outs[:count], *outs[count:]


def weight_grads(expert, rows, cot, weighted, factors, away=None):
    bf16 = jnp.bfloat16
    (every, width), units = rows.shape, weighted.shape[1] // 2

    def body(rows_ref, cot_ref, weighted_ref, factor_ref, *refs):
        for number in range(3):
            if number < 2:
                left, right, lead = rows_ref, factor_ref, 0
                lanes = slice((2 * expert + number) * units, (2 * expert + number + 1) * units)
                columns, into = slice(number * units, (number + 1) * units), slice(0, width)
            else:
                left, right, lead = weighted_ref, cot_ref, expert * units
                lanes, columns, into = slice(0, width), slice(0, width), slice(width, width + units)
            for start in range(0, into.stop - into.start, units):
                part = left[:, lead + start : lead + start + units]
                value = dot(part, right[:, lanes], ((0,), (0,)))
                at = slice(into.start + start, into.start + start + units)
                if away is None:
                    refs[0][at, columns] = value.astype(bf16)
                else:
                    value = value + refs[0][at, columns].astype(jnp.float32)
                    refs[1 + number][start : start + units, :] = value.astype(bf16)

    flops = 6 * every * width * units
    operands = (rows, cot, weighted, factors)
    if away is None:
        return kernel(body, [shape(width + units, width, bf16)], flops, *operands)[0]
    outs = [shape(width, units, bf16)] * 2 + [shape(units, width, bf16)]
    return kernel(body, outs, flops, *operands, away)


def doubled(value, arrived):
    return jnp.concatenate([value, arrived], axis=0)


def paired(latent_in, routes, combine_weights, cotangent, w_gate, w_up, w_down):
    devices_ep = lax.axis_size("ep")
    me = lax.axis_index("ep")
    experts = jnp.arange(devices_ep, dtype=jnp.int32)
    mine = jnp.stack([me, me ^ CORE])
    own = (w_gate[0], w_up[0], w_down[0])

    chosen = routes[None, :, :] == experts[:, None, None]
    share = jnp.sum(jnp.where(chosen, combine_weights[None, :, :], 0.0), axis=2)[None]
    x0, c0 = latent_in, cotangent

    x2, x1, x4, c4 = swap(x0, FAR), swap(x0, NEAR), swap(x0, SIDE), swap(c0, SIDE)
    arrived, gate_w = swap(share, NEAR), swap(own[0], CORE)
    x1, x2, x4, c0, c4, arrived, gate_w, own = fence(x1, x2, x4, c0, c4, arrived, gate_w, own)
    share = doubled(share, arrived)
    x3, x5, x6, c2 = swap(x2, NEAR), swap(x1, SIDE), swap(x2, SIDE), swap(c0, FAR)
    arrived, up_w = swap(share, FAR), swap(own[1], CORE)
    x3, x5, x6, c0, c2, arrived, up_w, own = fence(x3, x5, x6, c0, c2, arrived, up_w, own)
    share = doubled(share, arrived)
    x7, c1, c3, c6 = swap(x3, SIDE), swap(c0, NEAR), swap(c2, NEAR), swap(c2, SIDE)
    arrived, down_w = swap(share, SIDE), swap(own[2], CORE)
    x7, c1, c3, c6, arrived, down_w, own = fence(x7, c1, c3, c6, arrived, down_w, own)
    weights = (own, (gate_w, up_w, down_w))
    share = doubled(share, arrived)[:, mine, :]
    share = share.transpose(2, 1, 0).reshape(share.shape[2], -1)
    share, c1, c3 = fence(share, c1, c3)
    c5, c7 = swap(c1, SIDE), swap(c3, SIDE)
    y, rows, gate_pre, up_pre, weighted = forward(
        [x0, x1, x2, x3, x4, x5, x6, x7], weights, share
    )
    y, rows, c5, c7 = fence(y, rows, c5, c7)
    y7, y6 = swap(y[7], SIDE), swap(y[6], SIDE)
    g, cot, inner, factors = backward(
        [c0, c1, c2, c3, c4, c5, c6, c7], weights, share, gate_pre, up_pre
    )
    y, g, cot, factors, inner, y7, y6 = fence(y, g, cot, factors, inner, y7, y6)
    y3, y2 = narrow(added(y[3], y7)), added(y[2], y6)
    inner = inner.T.reshape(2, len(REACH), 1, -1).transpose(1, 2, 0, 3)
    y3, y2, inner, g = fence(y3, y2, inner, g)
    y3, g7, g6, arrived = swap(y3, NEAR), swap(g[7], SIDE), swap(g[6], SIDE), swap(inner[4:], SIDE)
    away = weight_grads(1, rows, cot, weighted, factors)
    y, g, arrived, away, y3, y2, g7, g6 = fence(y, g, arrived, away, y3, y2, g7, g6)
    g3, g2 = narrow(added(g[3], g7)), added(g[2], g6)
    y2 = narrow(added(y2, y3))
    inner = jnp.concatenate([inner[:4], arrived], axis=1)
    y2, g3, g2, inner, g, y, away = fence(y2, g3, g2, inner, g, y, away)
    y2, g3, g5, y5 = swap(y2, FAR), swap(g3, NEAR), swap(g[5], SIDE), swap(y[5], SIDE)
    arrived, away = swap(inner[2:], FAR), swap(away, CORE)
    y, g, arrived, away, y2, g3, g2, g5, y5 = fence(y, g, arrived, away, y2, g3, g2, g5, y5)
    y1, g1 = narrow(added(y[1], y5)), narrow(added(g[1], g5))
    g2 = narrow(added(g2, g3))
    inner = jnp.concatenate([inner[:2], arrived], axis=1)
    y1, g1, g2, inner, g, y, away = fence(y1, g1, g2, inner, g, y, away)
    g2, y1, g1, y4, g4 = (
        swap(g2, FAR), swap(y1, NEAR), swap(g1, NEAR), swap(y[4], SIDE), swap(g[4], SIDE),
    )
    arrived = swap(inner[1:], NEAR)
    grad_w = weight_grads(0, rows, cot, weighted, factors, away)
    y, g, arrived, grad_w, y1, g1, g2, y4, g4 = fence(y, g, arrived, grad_w, y1, g1, g2, y4, g4)

    inner = jnp.concatenate([inner[:1], arrived], axis=1)[0]
    combined = narrow(added(added(y[0], y4), added(y1, y2)))
    grad_latent = narrow(added(added(g[0], g4), added(g1, g2)))
    owner = jnp.stack([me ^ bits for bits in HALVED])
    owner = jnp.stack([owner, owner ^ CORE], axis=1)
    owns = routes[None, None, :, :] == owner[:, :, None, None]
    grad_combine = jnp.sum(jnp.where(owns, inner[:, :, :, None], 0.0), axis=(0, 1))
    return (combined, grad_latent, grad_combine, *[v[None] for v in grad_w])


def local(latent_in, routes, combine_weights, cotangent, w_gate, w_up, w_down):
    plan = paired if w_gate.shape[0] == 1 and lax.axis_size("ep") == 2 * len(REACH) else exchanged
    return plan(latent_in, routes, combine_weights, cotangent, w_gate, w_up, w_down)


def solution(mesh):
    return jax.shard_map(
        local,
        mesh=mesh,
        in_specs=(
            P(("grp", "ep"), None),
            P(("grp", "ep"), None),
            P(("grp", "ep"), None),
            P(("grp", "ep"), None),
            P("ep", None, None),
            P("ep", None, None),
            P("ep", None, None),
        ),
        out_specs=(
            P(("grp", "ep"), None),
            P(("grp", "ep"), None),
            P(("grp", "ep"), None),
            P(("grp", "ep"), None, None),
            P(("grp", "ep"), None, None),
            P(("grp", "ep"), None, None),
        ),
        check_vma=False,
    )
```

```python
import jax
import jax.numpy as jnp
from jax import lax
from jax.experimental import pallas as pl
from jax.experimental.pallas import tpu as pltpu
from jax.sharding import PartitionSpec as P


def assign_slots(route_rows, expert_count):
    flat_ids = route_rows.reshape(-1)
    onehot = (flat_ids[:, None] == jnp.arange(expert_count, dtype=jnp.int32)[None, :]).astype(
        jnp.int32
    )
    ranks = jnp.cumsum(onehot, axis=0) - 1
    return (flat_ids, jnp.sum(onehot * ranks, axis=1))


def expert_forward(rows, gate_w, up_w, down_w):
    gate_pre = jnp.einsum("erl,elf->erf", rows, gate_w, preferred_element_type=jnp.float32)
    up_pre = jnp.einsum("erl,elf->erf", rows, up_w, preferred_element_type=jnp.float32)
    sigma = jax.nn.sigmoid(gate_pre)
    silu_val = gate_pre * sigma
    hidden = (silu_val * up_pre).astype(jnp.bfloat16)
    expert_out = jnp.einsum(
        "erf,efl->erl", hidden, down_w, preferred_element_type=jnp.float32
    ).astype(jnp.bfloat16)
    return (expert_out, (gate_pre, up_pre, sigma, silu_val, hidden))


def expert_backward(rows, grad_out, saved, gate_w, up_w, down_w):
    gate_pre, up_pre, sigma, silu_val, hidden = saved
    grad_down = jnp.einsum(
        "erf,erl->efl", hidden, grad_out, preferred_element_type=jnp.float32
    ).astype(jnp.bfloat16)
    grad_hidden = jnp.einsum("erl,efl->erf", grad_out, down_w, preferred_element_type=jnp.float32)
    grad_gate = (grad_hidden * up_pre * sigma * (1.0 + gate_pre * (1.0 - sigma))).astype(
        jnp.bfloat16
    )
    grad_up = (grad_hidden * silu_val).astype(jnp.bfloat16)
    grad_gw = jnp.einsum(
        "erl,erf->elf", rows, grad_gate, preferred_element_type=jnp.float32
    ).astype(jnp.bfloat16)
    grad_uw = jnp.einsum("erl,erf->elf", rows, grad_up, preferred_element_type=jnp.float32).astype(
        jnp.bfloat16
    )
    grad_rows = (
        jnp.einsum("erf,elf->erl", grad_gate, gate_w, preferred_element_type=jnp.float32)
        + jnp.einsum("erf,elf->erl", grad_up, up_w, preferred_element_type=jnp.float32)
    ).astype(jnp.bfloat16)
    return (grad_rows, grad_gw, grad_uw, grad_down)


def exchanged(latent_in, routes, combine_weights, cotangent, w_gate, w_up, w_down):
    devices_ep = lax.axis_size("ep")
    local_experts = w_gate.shape[0]
    expert_count = local_experts * devices_ep
    tok_count = latent_in.shape[0]
    top_count = routes.shape[1]
    width = latent_in.shape[1]
    capacity = tok_count * top_count * 3 // (2 * expert_count)
    expert_ids, slot_ids = assign_slots(routes, expert_count)
    position = expert_ids * capacity + slot_ids
    repeated = jnp.repeat(latent_in, top_count, axis=0)
    weighted = (combine_weights[:, :, None] * cotangent.astype(jnp.float32)[:, None, :]).astype(
        jnp.bfloat16
    )
    send_rows = jnp.zeros((expert_count * capacity, width), jnp.bfloat16).at[position].set(repeated)
    send_rows = send_rows.reshape(expert_count, capacity, width)
    send_cot = (
        jnp.zeros((expert_count * capacity, width), jnp.bfloat16)
        .at[position]
        .set(weighted.reshape(-1, width))
    )
    send_cot = send_cot.reshape(expert_count, capacity, width)

    def to_local(received):
        shaped = received.reshape(devices_ep, local_experts, capacity, width)
        return shaped.transpose(1, 0, 2, 3).reshape(local_experts, devices_ep * capacity, width)

    def to_home(local_rows):
        shaped = local_rows.reshape(local_experts, devices_ep, capacity, width)
        return shaped.transpose(1, 0, 2, 3).reshape(expert_count, capacity, width)

    got_rows = lax.all_to_all(send_rows, "ep", split_axis=0, concat_axis=0, tiled=True)
    rows_local = to_local(got_rows)
    expert_out, saved = expert_forward(rows_local, w_gate, w_up, w_down)
    back_out = lax.all_to_all(to_home(expert_out), "ep", split_axis=0, concat_axis=0, tiled=True)
    got_cot = lax.all_to_all(send_cot, "ep", split_axis=0, concat_axis=0, tiled=True)
    grad_rows, grad_gw, grad_uw, grad_down = expert_backward(
        rows_local, to_local(got_cot), saved, w_gate, w_up, w_down
    )
    back_grad = lax.all_to_all(to_home(grad_rows), "ep", split_axis=0, concat_axis=0, tiled=True)
    out_rows = (
        back_out.reshape(-1, width)[position]
        .reshape(tok_count, top_count, width)
        .astype(jnp.float32)
    )
    grad_back = (
        back_grad.reshape(-1, width)[position]
        .reshape(tok_count, top_count, width)
        .astype(jnp.float32)
    )
    combined = jnp.sum(combine_weights[:, :, None] * out_rows, axis=1).astype(jnp.bfloat16)
    grad_combine = jnp.sum(cotangent.astype(jnp.float32)[:, None, :] * out_rows, axis=2)
    grad_latent = jnp.sum(grad_back, axis=1).astype(jnp.bfloat16)
    return (combined, grad_latent, grad_combine, grad_gw, grad_uw, grad_down)


def dot(a, b, dims):
    return lax.dot_general(a, b, (dims, ((), ())), preferred_element_type=jnp.float32)


def swap(value, bit):
    pairs = [(i, i ^ bit) for i in range(lax.axis_size("ep"))]
    return lax.ppermute(value, "ep", pairs)


CORE, SIDE, NEAR, FAR = 1, 2, 4, 8
REACH = (0, NEAR, FAR, NEAR | FAR, SIDE, SIDE | NEAR, SIDE | FAR, SIDE | NEAR | FAR)
HALVED = (0, SIDE, FAR, FAR | SIDE, NEAR, NEAR | SIDE, NEAR | FAR, NEAR | FAR | SIDE)


def fence(*values):
    return lax.optimization_barrier(values)


def added(a, b):
    return a.astype(jnp.float32) + b.astype(jnp.float32)


def narrow(value):
    return value.astype(jnp.bfloat16)


MIB = 1 << 20


class Fetch:
    def __init__(self, sems):
        self.sems, self.waiting = sems, {}

    def start(self, name, source, target):
        copy = pltpu.make_async_copy(source, target, self.sems.at[len(self.waiting)])
        copy.start()
        self.waiting[name] = [copy, False]

    def wait(self, *names):
        for name in names:
            if not self.waiting[name][1]:
                self.waiting[name][0].wait()
                self.waiting[name][1] = True

    def wait_all(self):
        self.wait(*self.waiting)


def kernel(body, outs, scratch, copies, flops, *operands):
    moved = sum(v.size * v.dtype.itemsize for v in (*operands, *outs))
    return pl.pallas_call(
        body,
        out_shape=outs,
        in_specs=[pl.BlockSpec(memory_space=pl.ANY)] * len(operands),
        out_specs=[pl.BlockSpec(memory_space=pl.ANY)] * len(outs),
        scratch_shapes=[*scratch, pltpu.SemaphoreType.DMA((copies,))],
        compiler_params=pltpu.CompilerParams(vmem_limit_bytes=56 * MIB),
        cost_estimate=pl.CostEstimate(flops=flops, bytes_accessed=moved, transcendentals=0),
    )(*operands)


def shape(rows, columns, dtype):
    return jax.ShapeDtypeStruct((rows, columns), dtype)


def forward(blocks, weights, share):
    bf16, f32 = jnp.bfloat16, jnp.float32
    count, (tok_count, width) = len(blocks), blocks[0].shape
    units, half = weights[0][0].shape[1], len(blocks) // 2
    every = count * tok_count

    def body(*refs):
        x_refs, w_refs, share_ref, refs = refs[:count], refs[count : count + 6], refs[count + 6], refs[count + 7 :]
        y_refs, saved_refs, refs = refs[:count], refs[count : count + 3], refs[count + 3 :]
        w_bufs, (rows, share_buf, gate_buf, up_buf, weighted_buf, y_buf, sems) = refs[:6], refs[6:]
        fetch = Fetch(sems)
        order = (*range(half, count), *range(half))
        for i in order[:half]:
            fetch.start(("x", i), x_refs[i], rows.at[i * tok_count : (i + 1) * tok_count])
        for i in range(6):
            fetch.start(("w", i), w_refs[i], w_bufs[i])
            if i == 0:
                fetch.start("share", share_ref, share_buf)
        for i in order[half:]:
            fetch.start(("x", i), x_refs[i], rows.at[i * tok_count : (i + 1) * tok_count])
        for start in (half, 0):
            at = slice(start * tok_count, (start + half) * tok_count)
            fetch.wait(*[("x", start + j) for j in range(half)])
            x, total = rows[at, :], 0.0
            for e in range(2):
                lanes = slice(e * units, (e + 1) * units)
                fetch.wait(("w", 3 * e))
                gate_pre = dot(x, w_bufs[3 * e][...], ((1,), (0,)))
                gate_buf[at, lanes] = gate_pre
                fetch.wait(("w", 3 * e + 1))
                up_pre = dot(x, w_bufs[3 * e + 1][...], ((1,), (0,)))
                up_buf[at, lanes] = up_pre
                hidden = gate_pre * jax.nn.sigmoid(gate_pre) * up_pre
                fetch.wait("share")
                part = []
                for j in range(half):
                    column = e * count + start + j
                    part.append(share_buf[:, column : column + 1])
                weighted = (jnp.concatenate(part, axis=0) * hidden).astype(bf16)
                weighted_buf[at, lanes] = weighted
                fetch.wait(("w", 3 * e + 2))
                total = total + dot(weighted, w_bufs[3 * e + 2][...], ((1,), (0,)))
            y_buf[at, :] = total.astype(bf16)
            for j in range(start, start + half):
                block = y_buf.at[j * tok_count : (j + 1) * tok_count]
                fetch.start(("y", j), block, y_refs[j])
            for name, buf, ref in zip("gus", (gate_buf, up_buf, weighted_buf), saved_refs):
                fetch.start((name, start), buf.at[at], ref.at[at])
        fetch.wait_all()

    saved = [
        shape(every, 2 * units, f32), shape(every, 2 * units, f32), shape(every, 2 * units, bf16)
    ]
    outs = [shape(tok_count, width, bf16)] * count + saved
    scratch = [pltpu.VMEM(w.shape, bf16) for w in (*weights[0], *weights[1])]
    scratch += [pltpu.VMEM((every, width), bf16), pltpu.VMEM(share.shape, f32)]
    scratch += [pltpu.VMEM(v.shape, v.dtype) for v in saved] + [pltpu.VMEM((every, width), bf16)]
    flops = 12 * every * width * units
    copies = 2 * count + 7 + 6
    outs = kernel(body, outs, scratch, copies, flops, *blocks, *weights[0], *weights[1], share)
    return outs[:count], *outs[count:]


def backward(blocks, weights, share, gate_pre, up_pre):
    bf16, f32 = jnp.bfloat16, jnp.float32
    count, (tok_count, width) = len(blocks), blocks[0].shape
    units, half = weights[0][0].shape[1], len(blocks) // 2
    every = count * tok_count

    def body(*refs):
        c_refs, w_refs, refs = refs[:count], refs[count : count + 6], refs[count + 6 :]
        (share_ref, gate_ref, up_ref), refs = refs[:3], refs[3:]
        g_refs, inner_ref, factor_ref, refs = refs[:count], refs[count], refs[count + 1], refs[count + 2 :]
        w_bufs, refs = refs[:6], refs[6:]
        rows, share_buf, gate_buf, up_buf, g_buf, inner_buf, factor_buf, sems = refs
        fetch = Fetch(sems)

        def fetch_half(start):
            at = slice(start * tok_count, (start + half) * tok_count)
            for i in range(start, start + half):
                fetch.start(("c", i), c_refs[i], rows.at[i * tok_count : (i + 1) * tok_count])
            if start:
                fetch.start(("w", 2), w_refs[2], w_bufs[2])
            fetch.start(("g", start), gate_ref.at[at], gate_buf.at[at])
            fetch.start(("u", start), up_ref.at[at], up_buf.at[at])

        fetch_half(half)
        fetch.start("share", share_ref, share_buf)
        for i in (0, 1, 5, 3, 4):
            fetch.start(("w", i), w_refs[i], w_bufs[i])
        fetch_half(0)
        for start in (half, 0):
            at = slice(start * tok_count, (start + half) * tok_count)
            fetch.wait(*[("c", start + j) for j in range(half)])
            cot, total = rows[at, :], 0.0
            for e in range(2):
                lanes = slice(e * units, (e + 1) * units)
                fetch.wait(("w", 3 * e + 2))
                plain = dot(cot, w_bufs[3 * e + 2][...], ((1,), (1,)))
                fetch.wait(("g", start), ("u", start), "share")
                gate, up = gate_buf[at, lanes], up_buf[at, lanes]
                sigma = jax.nn.sigmoid(gate)
                silu_val = gate * sigma
                inner = jnp.sum(silu_val * up * plain, axis=1, keepdims=True)
                part = []
                for j in range(half):
                    column = e * count + start + j
                    part.append(share_buf[:, column : column + 1])
                    inner_buf[:, column : column + 1] = inner[j * tok_count : (j + 1) * tok_count]
                grad_hidden = jnp.concatenate(part, axis=0) * plain
                slope = sigma * (1.0 + gate * (1.0 - sigma))
                grad_gate = (grad_hidden * up * slope).astype(bf16)
                grad_up = (grad_hidden * silu_val).astype(bf16)
                factor_buf[at, 2 * e * units : (2 * e + 1) * units] = grad_gate
                factor_buf[at, (2 * e + 1) * units : (2 * e + 2) * units] = grad_up
                fetch.wait(("w", 3 * e), ("w", 3 * e + 1))
                total = total + dot(grad_gate, w_bufs[3 * e][...], ((1,), (1,)))
                total = total + dot(grad_up, w_bufs[3 * e + 1][...], ((1,), (1,)))
            g_buf[at, :] = total.astype(bf16)
            for j in range(start, start + half):
                block = g_buf.at[j * tok_count : (j + 1) * tok_count]
                fetch.start(("grad", j), block, g_refs[j])
            fetch.start(("factor", start), factor_buf.at[at], factor_ref.at[at])
        fetch.start("inner", inner_buf, inner_ref)
        fetch.wait_all()

    small = shape(tok_count, 2 * count, f32)
    factors = shape(every, 4 * units, bf16)
    outs = [shape(tok_count, width, bf16)] * count + [small, factors]
    scratch = [pltpu.VMEM(w.shape, bf16) for w in (*weights[0], *weights[1])]
    scratch += [pltpu.VMEM((every, width), bf16), pltpu.VMEM(share.shape, f32)]
    scratch += [pltpu.VMEM(gate_pre.shape, f32)] * 2 + [pltpu.VMEM((every, width), bf16)]
    scratch += [pltpu.VMEM(small.shape, f32), pltpu.VMEM(factors.shape, bf16)]
    flops = 12 * every * width * units
    copies = 2 * count + 6 + 1 + 4 + 3
    operands = (*blocks, *weights[0], *weights[1], share, gate_pre, up_pre)
    outs = kernel(body, outs, scratch, copies, flops, *operands)
    return outs[:count], *outs[count:]


def weight_grads(expert, rows, cot, weighted, factors, away=None):
    bf16 = jnp.bfloat16
    count, (tok_count, width) = len(rows), rows[0].shape
    every, units = count * tok_count, weighted.shape[1] // 2
    extra = 0 if away is None else 1

    def body(*refs):
        x_refs, c_refs, refs = refs[:count], refs[count : 2 * count], refs[2 * count :]
        weighted_ref, factor_ref, refs = refs[0], refs[1], refs[2:]
        away_refs, out_refs, refs = refs[:extra], refs[extra : 3 * extra + 1], refs[3 * extra + 1 :]
        x_buf, c_buf, weighted_buf, factor_buf, *bufs, sems = refs
        away_bufs, out_bufs = bufs[:extra], bufs[extra:]
        fetch = Fetch(sems)
        for i in range(count):
            fetch.start(("x", i), x_refs[i], x_buf.at[i * tok_count : (i + 1) * tok_count])
        lanes = pl.ds(2 * expert * units, 2 * units)
        fetch.start("factor", factor_ref.at[:, lanes], factor_buf)
        if extra:
            fetch.start("away", away_refs[0], away_bufs[0])
        lanes = pl.ds(expert * units, units)
        fetch.start("weighted", weighted_ref.at[:, lanes], weighted_buf)
        for i in range(count):
            fetch.start(("c", i), c_refs[i], c_buf.at[i * tok_count : (i + 1) * tok_count])
        fetch.wait(*[("x", i) for i in range(count)], "factor")
        for number in range(3):
            if number < 2:
                left, right = x_buf, factor_buf[:, number * units : (number + 1) * units]
                columns, into = slice(number * units, (number + 1) * units), slice(0, width)
            else:
                fetch.wait("weighted", *[("c", i) for i in range(count)])
                left, right = weighted_buf, c_buf[...]
                columns, into = slice(0, width), slice(width, width + units)
            for start in range(0, into.stop - into.start, units):
                value = dot(left[:, start : start + units], right, ((0,), (0,)))
                at = slice(into.start + start, into.start + start + units)
                if not extra:
                    out_bufs[0][at, columns] = value.astype(bf16)
                else:
                    fetch.wait("away")
                    value = value + away_bufs[0][at, columns].astype(jnp.float32)
                    out_bufs[number][start : start + units, :] = value.astype(bf16)
                    block = out_bufs[number].at[start : start + units]
                    target = out_refs[number].at[start : start + units]
                    fetch.start(("out", number, start), block, target)
            if not extra and number:
                at = pl.ds(into.start, into.stop - into.start)
                fetch.start(("out", number), out_bufs[0].at[at], out_refs[0].at[at])
        fetch.wait_all()

    flops = 6 * every * width * units
    operands = (*rows, *cot, weighted, factors)
    scratch = [pltpu.VMEM((every, width), bf16)] * 2
    scratch += [pltpu.VMEM((every, units), bf16), pltpu.VMEM((every, 2 * units), bf16)]
    packed = shape(width + units, width, bf16)
    if away is None:
        outs = [packed]
        scratch += [pltpu.VMEM(packed.shape, bf16)]
    else:
        operands += (away,)
        outs = [shape(width, units, bf16)] * 2 + [shape(units, width, bf16)]
        scratch += [pltpu.VMEM(v.shape, bf16) for v in (packed, *outs)]
    copies = 2 * count + 3 + 2 * -(-width // units) + 1
    outs = kernel(body, outs, scratch, copies, flops, *operands)
    return outs if extra else outs[0]


def doubled(value, arrived):
    return jnp.concatenate([value, arrived], axis=0)


def paired(latent_in, routes, combine_weights, cotangent, w_gate, w_up, w_down):
    devices_ep = lax.axis_size("ep")
    me = lax.axis_index("ep")
    experts = jnp.arange(devices_ep, dtype=jnp.int32)
    mine = jnp.stack([me, me ^ CORE])
    own = (w_gate[0], w_up[0], w_down[0])

    chosen = routes[None, :, :] == experts[:, None, None]
    share = jnp.sum(jnp.where(chosen, combine_weights[None, :, :], 0.0), axis=2)[None]
    x0, c0 = latent_in, cotangent

    x2, x1, x4, c4 = swap(x0, FAR), swap(x0, NEAR), swap(x0, SIDE), swap(c0, SIDE)
    gate_w = swap(own[0], CORE)
    x1, x2, c0, share, up_w = fence(x1, x2, c0, share, own[1])

    x3, x5, x6, c2 = swap(x2, NEAR), swap(x1, SIDE), swap(x2, SIDE), swap(c0, FAR)
    arrived, up_w = swap(share, NEAR), swap(up_w, CORE)
    x3, x4, c4, c0, arrived, down_w = fence(x3, x4, c4, c0, arrived, own[2])

    share = doubled(share, arrived)
    x7, c1 = swap(x3, SIDE), swap(c0, NEAR)
    arrived, down_w = swap(share, FAR), swap(down_w, CORE)
    c2, x5, x6, arrived = fence(c2, x5, x6, arrived)

    share = doubled(share, arrived)
    c6, c3, arrived = swap(c2, SIDE), swap(c2, NEAR), swap(share, SIDE)
    x7, c1, arrived, gate_w, up_w, down_w = fence(x7, c1, arrived, gate_w, up_w, down_w)

    weights = (own, (gate_w, up_w, down_w))
    share = doubled(share, arrived)[:, mine, :]
    share = share.transpose(2, 1, 0).reshape(share.shape[2], -1)
    share, c1 = fence(share, c1)
    c5 = swap(c1, SIDE)
    rows = [x0, x1, x2, x3, x4, x5, x6, x7]
    y, gate_pre, up_pre, weighted = forward(rows, weights, share)
    y, c3 = fence(y, c3)

    c7, y7, y6 = swap(c3, SIDE), swap(y[7], SIDE), swap(y[6], SIDE)
    c5, c6, c7 = fence(c5, c6, c7)

    cot = [c0, c1, c2, c3, c4, c5, c6, c7]
    g, inner, factors = backward(cot, weights, share, gate_pre, up_pre)
    y, g, factors, inner, y7, y6 = fence(y, g, factors, inner, y7, y6)

    y3, y2 = narrow(added(y[3], y7)), added(y[2], y6)
    inner = inner.T.reshape(2, len(REACH), 1, -1).transpose(1, 2, 0, 3)
    y3, y2, inner, g, y = fence(y3, y2, inner, g, y)
    y3, g7, g6, y5 = swap(y3, NEAR), swap(g[7], SIDE), swap(g[6], SIDE), swap(y[5], SIDE)
    arrived = swap(inner[4:], SIDE)
    away = weight_grads(1, rows, cot, weighted, factors)
    y, g, arrived, away, y3, g7, g6 = fence(y, g, arrived, away, y3, g7, g6)

    g3, g2 = narrow(added(g[3], g7)), added(g[2], g6)
    y2 = narrow(added(y2, y3))
    inner = jnp.concatenate([inner[:4], arrived], axis=1)
    y2, g3, g2, inner, g, y, away = fence(y2, g3, g2, inner, g, y, away)
    g3, y2, g5, y4 = swap(g3, NEAR), swap(y2, FAR), swap(g[5], SIDE), swap(y[4], SIDE)
    arrived, away = swap(inner[2:], FAR), swap(away, CORE)
    y, g, arrived, g3, y5 = fence(y, g, arrived, g3, y5)

    y1, g2 = narrow(added(y[1], y5)), narrow(added(g2, g3))
    inner = jnp.concatenate([inner[:2], arrived], axis=1)
    y1, g2, inner, g = fence(y1, g2, inner, g)
    g2, y1, g4, arrived = swap(g2, FAR), swap(y1, NEAR), swap(g[4], SIDE), swap(inner[1:], NEAR)
    g5, away = fence(g5, away)

    g1 = swap(narrow(added(g[1], g5)), NEAR)
    grad_w = weight_grads(0, rows, cot, weighted, factors, away)
    arrived, grad_w, y1, g1, g2, y2, y4, g4 = fence(arrived, grad_w, y1, g1, g2, y2, y4, g4)

    inner = jnp.concatenate([inner[:1], arrived], axis=1)[0]
    combined = narrow(added(added(y[0], y4), added(y1, y2)))
    grad_latent = narrow(added(added(g[0], g4), added(g1, g2)))
    owner = jnp.stack([me ^ bits for bits in HALVED])
    owner = jnp.stack([owner, owner ^ CORE], axis=1)
    owns = routes[None, None, :, :] == owner[:, :, None, None]
    grad_combine = jnp.sum(jnp.where(owns, inner[:, :, :, None], 0.0), axis=(0, 1))
    return (combined, grad_latent, grad_combine, *[v[None] for v in grad_w])


def local(latent_in, routes, combine_weights, cotangent, w_gate, w_up, w_down):
    plan = paired if w_gate.shape[0] == 1 and lax.axis_size("ep") == 2 * len(REACH) else exchanged
    return plan(latent_in, routes, combine_weights, cotangent, w_gate, w_up, w_down)


def solution(mesh):
    return jax.shard_map(
        local,
        mesh=mesh,
        in_specs=(
            P(("grp", "ep"), None),
            P(("grp", "ep"), None),
            P(("grp", "ep"), None),
            P(("grp", "ep"), None),
            P("ep", None, None),
            P("ep", None, None),
            P("ep", None, None),
        ),
        out_specs=(
            P(("grp", "ep"), None),
            P(("grp", "ep"), None),
            P(("grp", "ep"), None),
            P(("grp", "ep"), None, None),
            P(("grp", "ep"), None, None),
            P(("grp", "ep"), None, None),
        ),
        check_vma=False,
    )
```

```python
import jax
import jax.numpy as jnp
from jax import lax
from jax.experimental import pallas as pl
from jax.experimental.pallas import tpu as pltpu
from jax.sharding import PartitionSpec as P


def assign_slots(route_rows, expert_count):
    flat_ids = route_rows.reshape(-1)
    onehot = (flat_ids[:, None] == jnp.arange(expert_count, dtype=jnp.int32)[None, :]).astype(
        jnp.int32
    )
    ranks = jnp.cumsum(onehot, axis=0) - 1
    return (flat_ids, jnp.sum(onehot * ranks, axis=1))


def expert_forward(rows, gate_w, up_w, down_w):
    gate_pre = jnp.einsum("erl,elf->erf", rows, gate_w, preferred_element_type=jnp.float32)
    up_pre = jnp.einsum("erl,elf->erf", rows, up_w, preferred_element_type=jnp.float32)
    sigma = jax.nn.sigmoid(gate_pre)
    silu_val = gate_pre * sigma
    hidden = (silu_val * up_pre).astype(jnp.bfloat16)
    expert_out = jnp.einsum(
        "erf,efl->erl", hidden, down_w, preferred_element_type=jnp.float32
    ).astype(jnp.bfloat16)
    return (expert_out, (gate_pre, up_pre, sigma, silu_val, hidden))


def expert_backward(rows, grad_out, saved, gate_w, up_w, down_w):
    gate_pre, up_pre, sigma, silu_val, hidden = saved
    grad_down = jnp.einsum(
        "erf,erl->efl", hidden, grad_out, preferred_element_type=jnp.float32
    ).astype(jnp.bfloat16)
    grad_hidden = jnp.einsum("erl,efl->erf", grad_out, down_w, preferred_element_type=jnp.float32)
    grad_gate = (grad_hidden * up_pre * sigma * (1.0 + gate_pre * (1.0 - sigma))).astype(
        jnp.bfloat16
    )
    grad_up = (grad_hidden * silu_val).astype(jnp.bfloat16)
    grad_gw = jnp.einsum(
        "erl,erf->elf", rows, grad_gate, preferred_element_type=jnp.float32
    ).astype(jnp.bfloat16)
    grad_uw = jnp.einsum("erl,erf->elf", rows, grad_up, preferred_element_type=jnp.float32).astype(
        jnp.bfloat16
    )
    grad_rows = (
        jnp.einsum("erf,elf->erl", grad_gate, gate_w, preferred_element_type=jnp.float32)
        + jnp.einsum("erf,elf->erl", grad_up, up_w, preferred_element_type=jnp.float32)
    ).astype(jnp.bfloat16)
    return (grad_rows, grad_gw, grad_uw, grad_down)


def exchanged(latent_in, routes, combine_weights, cotangent, w_gate, w_up, w_down):
    devices_ep = lax.axis_size("ep")
    local_experts = w_gate.shape[0]
    expert_count = local_experts * devices_ep
    tok_count = latent_in.shape[0]
    top_count = routes.shape[1]
    width = latent_in.shape[1]
    capacity = tok_count * top_count * 3 // (2 * expert_count)
    expert_ids, slot_ids = assign_slots(routes, expert_count)
    position = expert_ids * capacity + slot_ids
    repeated = jnp.repeat(latent_in, top_count, axis=0)
    weighted = (combine_weights[:, :, None] * cotangent.astype(jnp.float32)[:, None, :]).astype(
        jnp.bfloat16
    )
    send_rows = jnp.zeros((expert_count * capacity, width), jnp.bfloat16).at[position].set(repeated)
    send_rows = send_rows.reshape(expert_count, capacity, width)
    send_cot = (
        jnp.zeros((expert_count * capacity, width), jnp.bfloat16)
        .at[position]
        .set(weighted.reshape(-1, width))
    )
    send_cot = send_cot.reshape(expert_count, capacity, width)

    def to_local(received):
        shaped = received.reshape(devices_ep, local_experts, capacity, width)
        return shaped.transpose(1, 0, 2, 3).reshape(local_experts, devices_ep * capacity, width)

    def to_home(local_rows):
        shaped = local_rows.reshape(local_experts, devices_ep, capacity, width)
        return shaped.transpose(1, 0, 2, 3).reshape(expert_count, capacity, width)

    got_rows = lax.all_to_all(send_rows, "ep", split_axis=0, concat_axis=0, tiled=True)
    rows_local = to_local(got_rows)
    expert_out, saved = expert_forward(rows_local, w_gate, w_up, w_down)
    back_out = lax.all_to_all(to_home(expert_out), "ep", split_axis=0, concat_axis=0, tiled=True)
    got_cot = lax.all_to_all(send_cot, "ep", split_axis=0, concat_axis=0, tiled=True)
    grad_rows, grad_gw, grad_uw, grad_down = expert_backward(
        rows_local, to_local(got_cot), saved, w_gate, w_up, w_down
    )
    back_grad = lax.all_to_all(to_home(grad_rows), "ep", split_axis=0, concat_axis=0, tiled=True)
    out_rows = (
        back_out.reshape(-1, width)[position]
        .reshape(tok_count, top_count, width)
        .astype(jnp.float32)
    )
    grad_back = (
        back_grad.reshape(-1, width)[position]
        .reshape(tok_count, top_count, width)
        .astype(jnp.float32)
    )
    combined = jnp.sum(combine_weights[:, :, None] * out_rows, axis=1).astype(jnp.bfloat16)
    grad_combine = jnp.sum(cotangent.astype(jnp.float32)[:, None, :] * out_rows, axis=2)
    grad_latent = jnp.sum(grad_back, axis=1).astype(jnp.bfloat16)
    return (combined, grad_latent, grad_combine, grad_gw, grad_uw, grad_down)


def dot(a, b, dims):
    return lax.dot_general(a, b, (dims, ((), ())), preferred_element_type=jnp.float32)


def swap(value, bit):
    pairs = [(i, i ^ bit) for i in range(lax.axis_size("ep"))]
    return lax.ppermute(value, "ep", pairs)


CORE, SIDE, NEAR, FAR = 1, 2, 4, 8
REACH = (0, NEAR, FAR, NEAR | FAR, SIDE, SIDE | NEAR, SIDE | FAR, SIDE | NEAR | FAR)


def fence(*values):
    return lax.optimization_barrier(values)


def added(a, b):
    return a.astype(jnp.float32) + b.astype(jnp.float32)


def narrow(value):
    return value.astype(jnp.bfloat16)


MIB = 1 << 20


class Fetch:
    def __init__(self, sems):
        self.sems, self.waiting = sems, {}

    def start(self, name, source, target):
        copy = pltpu.make_async_copy(source, target, self.sems.at[len(self.waiting)])
        copy.start()
        self.waiting[name] = [copy, False]

    def wait(self, *names):
        for name in names:
            if not self.waiting[name][1]:
                self.waiting[name][0].wait()
                self.waiting[name][1] = True

    def wait_all(self):
        self.wait(*self.waiting)


def kernel(body, outs, scratch, copies, flops, *operands, scalar=None):
    moved = sum(v.size * v.dtype.itemsize for v in (*operands, *outs))
    in_specs = [pl.BlockSpec(memory_space=pl.ANY)] * len(operands)
    if scalar is not None:
        operands = (scalar, *operands)
        in_specs = [pl.BlockSpec(memory_space=pltpu.SMEM), *in_specs]
    return pl.pallas_call(
        body,
        out_shape=outs,
        in_specs=in_specs,
        out_specs=[pl.BlockSpec(memory_space=pl.ANY)] * len(outs),
        scratch_shapes=[*scratch, pltpu.SemaphoreType.DMA((copies,))],
        compiler_params=pltpu.CompilerParams(vmem_limit_bytes=56 * MIB),
        cost_estimate=pl.CostEstimate(flops=flops, bytes_accessed=moved, transcendentals=0),
    )(*operands)


def shape(rows, columns, dtype):
    return jax.ShapeDtypeStruct((rows, columns), dtype)


def pieces(value):
    first = narrow(value)
    value = value - first.astype(jnp.float32)
    second = narrow(value)
    return first, second, narrow(value - second.astype(jnp.float32))


EXTRA = 16


def both_ways(number, blocks, weights, me, before=None):
    bf16, f32 = jnp.bfloat16, jnp.float32
    count, width = len(blocks), blocks[0].shape[1]
    units, last = weights[0][0].shape[1], before is not None
    tok_count = (blocks[0].shape[0] - (0 if last else EXTRA)) // 2
    every, size = count * tok_count, 2 * tok_count
    lanes = 128
    back = size + (EXTRA if last else 0)

    def body(me_ref, *refs):
        b_refs, w_refs, refs = refs[:count], refs[count : count + 6], refs[count + 6 :]
        before_refs, refs = (refs[:2], refs[2:]) if last else ((), refs)
        q_refs, refs = refs[:count], refs[count:]
        weighted_ref, factor_ref, refs = refs[0], refs[1], refs[2:]
        after_refs, refs = ((), refs) if last else (refs[:2], refs[2:])
        w_bufs, refs = refs[:6], refs[6:]
        x_buf, c_buf, y_buf, g_buf, weighted_buf, factor_buf, refs = *refs[:6], refs[6:]
        share_buf, inner_buf, wide_buf, extra_buf, sems = refs
        fetch = Fetch(sems)
        me = me_ref[0]
        low = lax.rem(me, 8)
        for b in range(count):
            at = pl.ds(b * tok_count, tok_count)
            fetch.start(("x", b), b_refs[b].at[pl.ds(0, tok_count)], x_buf.at[at])
            if b == 0:
                fetch.start(("w", 0), w_refs[0], w_bufs[0])
        if last:
            fetch.start("share", before_refs[0], share_buf)
            fetch.start("inner", before_refs[1], inner_buf)
        else:
            for b in range(count):
                fetch.start(("s", b), b_refs[b].at[pl.ds(size, EXTRA)], extra_buf.at[b])
        for i in (1, 2):
            fetch.start(("w", i), w_refs[i], w_bufs[i])
        for b in range(count):
            at = pl.ds(b * tok_count, tok_count)
            fetch.start(("c", b), b_refs[b].at[pl.ds(tok_count, tok_count)], c_buf.at[at])
        for i in (3, 4, 5):
            fetch.start(("w", i), w_refs[i], w_bufs[i])

        def place(e):
            number = lax.rem(low + e, 2) + low - lax.rem(low, 2)
            return pl.ds(pl.multiple_of(number * lanes, lanes), lanes)

        upper = me >= 8
        if last:
            fetch.wait("share", "inner")
        else:
            inner_buf[...] = jnp.zeros((lanes, lanes), f32)
            share_buf[...] = jnp.zeros((lanes, lanes), f32)
            for b in range(count):
                fetch.wait(("s", b))
                wide_buf[b] = extra_buf[b].astype(f32)
            for e in range(2):
                for b in range(count):
                    tile = wide_buf[b, :, place(e)]
                    sums = [tile[r : r + 1] + tile[r + 2 : r + 3] + tile[r + 4 : r + 5] for r in (0, 1)]
                    row = e * count + b
                    share_buf[row : row + 1, :] = jnp.where(upper, sums[1], sums[0])
            share_buf[...] = share_buf[...].T

        half = slice(number * tok_count, (number + 1) * tok_count)
        fetch.wait(*[("x", b) for b in range(count)])
        x, y, g = x_buf[...], 0.0, 0.0
        for e in range(2):
            gate_w, up_w, down_w = w_bufs[3 * e : 3 * e + 3]
            columns = slice(e * units, (e + 1) * units)
            fetch.wait(("w", 3 * e))
            gate = dot(x, gate_w[...], ((1,), (0,)))
            fetch.wait(("w", 3 * e + 1))
            up = dot(x, up_w[...], ((1,), (0,)))
            sigma = jax.nn.sigmoid(gate)
            silu_val = gate * sigma
            hidden = silu_val * up
            part = [share_buf[half, e * count + b : e * count + b + 1] for b in range(count)]
            part = jnp.concatenate(part, axis=0)
            weighted = (part * hidden).astype(bf16)
            weighted_buf[:, columns] = weighted
            fetch.wait(("w", 3 * e + 2))
            if e == 0:
                fetch.wait(*[("c", b) for b in range(count)])
            plain = dot(c_buf[...], down_w[...], ((1,), (1,)))
            y = y + dot(weighted, down_w[...], ((1,), (0,)))
            inner = jnp.sum(hidden * plain, axis=1, keepdims=True)
            for b in range(count):
                value = inner[b * tok_count : (b + 1) * tok_count]
                inner_buf[half, e * count + b : e * count + b + 1] = value
            grad_hidden = part * plain
            grad_gate = (grad_hidden * up * (sigma * (1.0 + gate * (1.0 - sigma)))).astype(bf16)
            grad_up = (grad_hidden * silu_val).astype(bf16)
            factor_buf[:, 2 * e * units : (2 * e + 1) * units] = grad_gate
            factor_buf[:, (2 * e + 1) * units : (2 * e + 2) * units] = grad_up
            g = g + dot(grad_gate, gate_w[...], ((1,), (1,)))
            g = g + dot(grad_up, up_w[...], ((1,), (1,)))
        y_buf[...] = y.astype(bf16)
        g_buf[...] = g.astype(bf16)
        for b in range(count):
            at = pl.ds(b * tok_count, tok_count)
            fetch.start(("y", b), y_buf.at[at], q_refs[b].at[pl.ds(0, tok_count)])
            fetch.start(("g", b), g_buf.at[at], q_refs[b].at[pl.ds(tok_count, tok_count)])
        fetch.start("weighted", weighted_buf, weighted_ref)
        fetch.start("factor", factor_buf, factor_ref)
        if last:
            wide_buf[...] = jnp.zeros((count, EXTRA, width), f32)
            inner_buf[...] = inner_buf[...].T
            for e in range(2):
                for b in range(count):
                    row = e * count + b
                    value, lines = inner_buf[row : row + 1, :], []
                    for _ in range(3):
                        piece = value.astype(bf16).astype(f32)
                        lines += [jnp.where(upper, 0.0, piece), jnp.where(upper, piece, 0.0)]
                        value = value - piece
                    lines += [jnp.zeros((2, lanes), f32)]
                    wide_buf[b, 0:8, place(e)] = jnp.concatenate(lines, axis=0)
            for b in range(count):
                extra_buf[b] = wide_buf[b].astype(bf16)
                fetch.start(("i", b), extra_buf.at[b], q_refs[b].at[pl.ds(size, EXTRA)])
        else:
            fetch.start("share", share_buf, after_refs[0])
            fetch.start("inner", inner_buf, after_refs[1])
        fetch.wait_all()

    outs = [shape(back, width, bf16)] * count
    outs += [shape(every, 2 * units, bf16), shape(every, 4 * units, bf16)]
    small = shape(lanes, lanes, f32)
    operands = (*blocks, *weights[0], *weights[1])
    if last:
        operands += before
    else:
        outs += [small, small]
    scratch = [pltpu.VMEM(w.shape, bf16) for w in (*weights[0], *weights[1])]
    scratch += [pltpu.VMEM((every, width), bf16)] * 4
    scratch += [pltpu.VMEM((every, 2 * units), bf16), pltpu.VMEM((every, 4 * units), bf16)]
    scratch += [pltpu.VMEM(small.shape, f32)] * 2
    scratch += [pltpu.VMEM((count, EXTRA, width), f32), pltpu.VMEM((count, EXTRA, width), bf16)]
    flops = 24 * every * width * units
    copies = 5 * count + 6 + 2 + 2
    outs = kernel(body, outs, scratch, copies, flops, *operands, scalar=me)
    return outs[:count], outs[count:]


def weight_grads(expert, blocks, factors, away=None):
    bf16 = jnp.bfloat16
    parts, count, width = len(blocks), len(blocks[0]), blocks[0][0].shape[1]
    each = factors[0][0].shape[0]
    tok_count, every, units = each // count, each * parts, factors[0][0].shape[1] // 2
    extra = 0 if away is None else 1

    def body(*refs):
        b_refs, refs = refs[: parts * count], refs[parts * count :]
        f_refs, refs = refs[: 2 * parts], refs[2 * parts :]
        away_refs, out_refs, refs = refs[:extra], refs[extra : 3 * extra + 1], refs[3 * extra + 1 :]
        x_buf, c_buf, weighted_buf, factor_buf, *bufs, sems = refs
        away_bufs, out_bufs = bufs[:extra], bufs[extra:]
        fetch = Fetch(sems)
        names = range(parts * count)
        for i in names:
            at = pl.ds(i * tok_count, tok_count)
            fetch.start(("x", i), b_refs[i].at[pl.ds(0, tok_count)], x_buf.at[at])
        for p in range(parts):
            at = pl.ds(p * each, each)
            lanes = pl.ds(2 * expert * units, 2 * units)
            fetch.start(("f", p), f_refs[2 * p + 1].at[:, lanes], factor_buf.at[at])
        if extra:
            fetch.start("away", away_refs[0], away_bufs[0])
        for p in range(parts):
            at = pl.ds(p * each, each)
            lanes = pl.ds(expert * units, units)
            fetch.start(("w", p), f_refs[2 * p].at[:, lanes], weighted_buf.at[at])
        for i in names:
            at = pl.ds(i * tok_count, tok_count)
            fetch.start(("c", i), b_refs[i].at[pl.ds(tok_count, tok_count)], c_buf.at[at])
        fetch.wait(*[("x", i) for i in names], *[("f", p) for p in range(parts)])
        for number in range(3):
            if number < 2:
                left, right = x_buf, factor_buf[:, number * units : (number + 1) * units]
                columns, into = slice(number * units, (number + 1) * units), slice(0, width)
            else:
                fetch.wait(*[("c", i) for i in names], *[("w", p) for p in range(parts)])
                left, right = weighted_buf, c_buf[...]
                columns, into = slice(0, width), slice(width, width + units)
            for start in range(0, into.stop - into.start, units):
                value = dot(left[:, start : start + units], right, ((0,), (0,)))
                at = slice(into.start + start, into.start + start + units)
                if not extra:
                    out_bufs[0][at, columns] = value.astype(bf16)
                else:
                    fetch.wait("away")
                    value = value + away_bufs[0][at, columns].astype(jnp.float32)
                    out_bufs[number][start : start + units, :] = value.astype(bf16)
                    block = out_bufs[number].at[start : start + units]
                    target = out_refs[number].at[start : start + units]
                    fetch.start(("out", number, start), block, target)
            if not extra and number:
                at = pl.ds(into.start, into.stop - into.start)
                fetch.start(("out", number), out_bufs[0].at[at], out_refs[0].at[at])
        fetch.wait_all()

    flops = 6 * every * width * units
    operands = (*[b for part in blocks for b in part], *[f for part in factors for f in part])
    scratch = [pltpu.VMEM((every, width), bf16)] * 2
    scratch += [pltpu.VMEM((every, units), bf16), pltpu.VMEM((every, 2 * units), bf16)]
    packed = shape(width + units, width, bf16)
    if away is None:
        outs = [packed]
        scratch += [pltpu.VMEM(packed.shape, bf16)]
    else:
        operands += (away,)
        outs = [shape(width, units, bf16)] * 2 + [shape(units, width, bf16)]
        scratch += [pltpu.VMEM(v.shape, bf16) for v in (packed, *outs)]
    copies = 2 * parts * count + 2 * parts + 1 + 2 * -(-width // units) + 1
    outs = kernel(body, outs, scratch, copies, flops, *operands)
    return outs if extra else outs[0]


def paired(latent_in, routes, combine_weights, cotangent, w_gate, w_up, w_down):
    f32 = jnp.float32
    devices_ep, tok_count, width = lax.axis_size("ep"), *latent_in.shape
    me = lax.axis_index("ep")
    mid = tok_count // 2
    experts = jnp.arange(devices_ep, dtype=jnp.int32)
    own = (w_gate[0], w_up[0], w_down[0])

    chosen = routes[None, :, :] == experts[:, None, None]
    share = jnp.sum(jnp.where(chosen, combine_weights[None, :, :], 0.0), axis=2)
    lines = jnp.stack(pieces(share)).reshape(-1, width)
    lines = jnp.pad(lines, ((0, EXTRA - lines.shape[0]), (0, 0)))
    a0 = jnp.concatenate([latent_in[:mid], cotangent[:mid], lines], axis=0)
    b0 = jnp.concatenate([latent_in[mid:], cotangent[mid:]], axis=0)
    a0, b0, own = fence(a0, b0, own)

    a4, a2, a1, b4 = swap(a0, SIDE), swap(a0, FAR), swap(a0, NEAR), swap(b0, SIDE)
    gate_w = swap(own[0], CORE)
    a0, b0, a1, a2, a4, b4, gate_w, own = fence(a0, b0, a1, a2, a4, b4, gate_w, own)
    a6, a5, b2, a3 = swap(a2, SIDE), swap(a1, SIDE), swap(b0, FAR), swap(a2, NEAR)
    up_w = swap(own[1], CORE)
    a0, b0, a3, a5, a6, b2, up_w, own = fence(a0, b0, a3, a5, a6, b2, up_w, own)
    a7, b6, b1, b3 = swap(a3, SIDE), swap(b2, SIDE), swap(b0, NEAR), swap(b2, NEAR)
    down_w = swap(own[2], CORE)
    a0, b0, a7, b1, b3, b6, down_w, own = fence(a0, b0, a7, b1, b3, b6, down_w, own)
    b5, b7 = swap(b1, SIDE), swap(b3, SIDE)
    weights, me = (own, (gate_w, up_w, down_w)), me.astype(jnp.int32).reshape(1)
    a = [a0, a1, a2, a3, a4, a5, a6, a7]
    q, (*a_factors, shares, inners) = both_ways(0, a, weights, me)
    q, shares, inners, b5, b7 = fence(q, shares, inners, b5, b7)
    q7, q5 = swap(q[7], SIDE), swap(q[5], SIDE)
    b = [b0, b1, b2, b3, b4, b5, b6, b7]
    p, b_factors = both_ways(1, b, weights, me, (shares, inners))
    p, q, q7, q5, b_factors = fence(p, q, q7, q5, b_factors)
    factors = (a_factors, b_factors)
    q3, q1 = narrow(added(q[3], q7)), narrow(added(q[1], q5))
    q3, q1, p, q = fence(q3, q1, p, q)
    q6, p7, q3, q1 = swap(q[6], SIDE), swap(p[7], SIDE), swap(q3, NEAR), swap(q1, NEAR)
    away = weight_grads(1, (a, b), factors)
    p, q, q6, p7, q3, q1, away = fence(p, q, q6, p7, q3, q1, away)
    q2, p3 = narrow(added(q[2], q6) + q3.astype(f32)), narrow(added(p[3], p7))
    q2, p3, p, q, away = fence(q2, p3, p, q, away)
    p6, p5, q2, p3 = swap(p[6], SIDE), swap(p[5], SIDE), swap(q2, FAR), swap(p3, NEAR)
    away = swap(away, CORE)
    p, q, p6, p5, q2, p3, away = fence(p, q, p6, p5, q2, p3, away)
    p2, p1 = narrow(added(p[2], p6) + p3.astype(f32)), narrow(added(p[1], p5))
    p2, p1, p, q, away = fence(p2, p1, p, q, away)
    p4, q4, p2, p1 = swap(p[4], SIDE), swap(q[4], SIDE), swap(p2, FAR), swap(p1, NEAR)
    grad_w = weight_grads(0, (a, b), factors, away)
    p4, q4, p2, p1, grad_w = fence(p4, q4, p2, p1, grad_w)

    q = added(q[0], q4) + added(q1, q2)
    p = added(p[0], p4) + added(p1, p2)
    combined = narrow(jnp.concatenate([q[:mid], p[:mid]], axis=0))
    grad_latent = narrow(jnp.concatenate([q[mid : 2 * mid], p[mid : 2 * mid]], axis=0))
    inner = p[2 * mid :].reshape(-1, devices_ep, tok_count)[:3].sum(axis=0)
    grad_combine = jnp.sum(jnp.where(chosen, inner[:, :, None], 0.0), axis=0)
    return (combined, grad_latent, grad_combine, *[v[None] for v in grad_w])


def local(latent_in, routes, combine_weights, cotangent, w_gate, w_up, w_down):
    plan = paired if w_gate.shape[0] == 1 and lax.axis_size("ep") == 2 * len(REACH) else exchanged
    return plan(latent_in, routes, combine_weights, cotangent, w_gate, w_up, w_down)


def solution(mesh):
    return jax.shard_map(
        local,
        mesh=mesh,
        in_specs=(
            P(("grp", "ep"), None),
            P(("grp", "ep"), None),
            P(("grp", "ep"), None),
            P(("grp", "ep"), None),
            P("ep", None, None),
            P("ep", None, None),
            P("ep", None, None),
        ),
        out_specs=(
            P(("grp", "ep"), None),
            P(("grp", "ep"), None),
            P(("grp", "ep"), None),
            P(("grp", "ep"), None, None),
            P(("grp", "ep"), None, None),
            P(("grp", "ep"), None, None),
        ),
        check_vma=False,
    )
```

```python
import jax
import jax.numpy as jnp
from jax import lax
from jax.experimental import pallas as pl
from jax.experimental.pallas import tpu as pltpu
from jax.sharding import PartitionSpec as P


def assign_slots(route_rows, expert_count):
    flat_ids = route_rows.reshape(-1)
    onehot = (flat_ids[:, None] == jnp.arange(expert_count, dtype=jnp.int32)[None, :]).astype(
        jnp.int32
    )
    ranks = jnp.cumsum(onehot, axis=0) - 1
    return (flat_ids, jnp.sum(onehot * ranks, axis=1))


def expert_forward(rows, gate_w, up_w, down_w):
    gate_pre = jnp.einsum("erl,elf->erf", rows, gate_w, preferred_element_type=jnp.float32)
    up_pre = jnp.einsum("erl,elf->erf", rows, up_w, preferred_element_type=jnp.float32)
    sigma = jax.nn.sigmoid(gate_pre)
    silu_val = gate_pre * sigma
    hidden = (silu_val * up_pre).astype(jnp.bfloat16)
    expert_out = jnp.einsum(
        "erf,efl->erl", hidden, down_w, preferred_element_type=jnp.float32
    ).astype(jnp.bfloat16)
    return (expert_out, (gate_pre, up_pre, sigma, silu_val, hidden))


def expert_backward(rows, grad_out, saved, gate_w, up_w, down_w):
    gate_pre, up_pre, sigma, silu_val, hidden = saved
    grad_down = jnp.einsum(
        "erf,erl->efl", hidden, grad_out, preferred_element_type=jnp.float32
    ).astype(jnp.bfloat16)
    grad_hidden = jnp.einsum("erl,efl->erf", grad_out, down_w, preferred_element_type=jnp.float32)
    grad_gate = (grad_hidden * up_pre * sigma * (1.0 + gate_pre * (1.0 - sigma))).astype(
        jnp.bfloat16
    )
    grad_up = (grad_hidden * silu_val).astype(jnp.bfloat16)
    grad_gw = jnp.einsum(
        "erl,erf->elf", rows, grad_gate, preferred_element_type=jnp.float32
    ).astype(jnp.bfloat16)
    grad_uw = jnp.einsum("erl,erf->elf", rows, grad_up, preferred_element_type=jnp.float32).astype(
        jnp.bfloat16
    )
    grad_rows = (
        jnp.einsum("erf,elf->erl", grad_gate, gate_w, preferred_element_type=jnp.float32)
        + jnp.einsum("erf,elf->erl", grad_up, up_w, preferred_element_type=jnp.float32)
    ).astype(jnp.bfloat16)
    return (grad_rows, grad_gw, grad_uw, grad_down)


def exchanged(latent_in, routes, combine_weights, cotangent, w_gate, w_up, w_down):
    devices_ep = lax.axis_size("ep")
    local_experts = w_gate.shape[0]
    expert_count = local_experts * devices_ep
    tok_count = latent_in.shape[0]
    top_count = routes.shape[1]
    width = latent_in.shape[1]
    capacity = tok_count * top_count * 3 // (2 * expert_count)
    expert_ids, slot_ids = assign_slots(routes, expert_count)
    position = expert_ids * capacity + slot_ids
    repeated = jnp.repeat(latent_in, top_count, axis=0)
    weighted = (combine_weights[:, :, None] * cotangent.astype(jnp.float32)[:, None, :]).astype(
        jnp.bfloat16
    )
    send_rows = jnp.zeros((expert_count * capacity, width), jnp.bfloat16).at[position].set(repeated)
    send_rows = send_rows.reshape(expert_count, capacity, width)
    send_cot = (
        jnp.zeros((expert_count * capacity, width), jnp.bfloat16)
        .at[position]
        .set(weighted.reshape(-1, width))
    )
    send_cot = send_cot.reshape(expert_count, capacity, width)

    def to_local(received):
        shaped = received.reshape(devices_ep, local_experts, capacity, width)
        return shaped.transpose(1, 0, 2, 3).reshape(local_experts, devices_ep * capacity, width)

    def to_home(local_rows):
        shaped = local_rows.reshape(local_experts, devices_ep, capacity, width)
        return shaped.transpose(1, 0, 2, 3).reshape(expert_count, capacity, width)

    got_rows = lax.all_to_all(send_rows, "ep", split_axis=0, concat_axis=0, tiled=True)
    rows_local = to_local(got_rows)
    expert_out, saved = expert_forward(rows_local, w_gate, w_up, w_down)
    back_out = lax.all_to_all(to_home(expert_out), "ep", split_axis=0, concat_axis=0, tiled=True)
    got_cot = lax.all_to_all(send_cot, "ep", split_axis=0, concat_axis=0, tiled=True)
    grad_rows, grad_gw, grad_uw, grad_down = expert_backward(
        rows_local, to_local(got_cot), saved, w_gate, w_up, w_down
    )
    back_grad = lax.all_to_all(to_home(grad_rows), "ep", split_axis=0, concat_axis=0, tiled=True)
    out_rows = (
        back_out.reshape(-1, width)[position]
        .reshape(tok_count, top_count, width)
        .astype(jnp.float32)
    )
    grad_back = (
        back_grad.reshape(-1, width)[position]
        .reshape(tok_count, top_count, width)
        .astype(jnp.float32)
    )
    combined = jnp.sum(combine_weights[:, :, None] * out_rows, axis=1).astype(jnp.bfloat16)
    grad_combine = jnp.sum(cotangent.astype(jnp.float32)[:, None, :] * out_rows, axis=2)
    grad_latent = jnp.sum(grad_back, axis=1).astype(jnp.bfloat16)
    return (combined, grad_latent, grad_combine, grad_gw, grad_uw, grad_down)


def dot(a, b, dims):
    return lax.dot_general(a, b, (dims, ((), ())), preferred_element_type=jnp.float32)


def swap(value, bit):
    pairs = [(i, i ^ bit) for i in range(lax.axis_size("ep"))]
    return lax.ppermute(value, "ep", pairs)


CORE, SIDE, NEAR, FAR = 1, 2, 4, 8
REACH = (0, NEAR, FAR, NEAR | FAR, SIDE, SIDE | NEAR, SIDE | FAR, SIDE | NEAR | FAR)


def fence(*values):
    return lax.optimization_barrier(values)


def added(a, b):
    return a.astype(jnp.float32) + b.astype(jnp.float32)


def narrow(value):
    return value.astype(jnp.bfloat16)


MIB = 1 << 20


class Fetch:
    def __init__(self, sems):
        self.sems, self.waiting = sems, {}

    def start(self, name, source, target):
        copy = pltpu.make_async_copy(source, target, self.sems.at[len(self.waiting)])
        copy.start()
        self.waiting[name] = [copy, False]

    def wait(self, *names):
        for name in names:
            if not self.waiting[name][1]:
                self.waiting[name][0].wait()
                self.waiting[name][1] = True

    def wait_all(self):
        self.wait(*self.waiting)


def kernel(body, outs, scratch, copies, flops, *operands, scalar=None):
    moved = sum(v.size * v.dtype.itemsize for v in (*operands, *outs))
    in_specs = [pl.BlockSpec(memory_space=pl.ANY)] * len(operands)
    if scalar is not None:
        operands = (scalar, *operands)
        in_specs = [pl.BlockSpec(memory_space=pltpu.SMEM), *in_specs]
    return pl.pallas_call(
        body,
        out_shape=outs,
        in_specs=in_specs,
        out_specs=[pl.BlockSpec(memory_space=pl.ANY)] * len(outs),
        scratch_shapes=[*scratch, pltpu.SemaphoreType.DMA((copies,))],
        compiler_params=pltpu.CompilerParams(vmem_limit_bytes=56 * MIB),
        cost_estimate=pl.CostEstimate(flops=flops, bytes_accessed=moved, transcendentals=0),
    )(*operands)


def shape(rows, columns, dtype):
    return jax.ShapeDtypeStruct((rows, columns), dtype)


def pieces(value):
    first = narrow(value)
    value = value - first.astype(jnp.float32)
    second = narrow(value)
    return first, second, narrow(value - second.astype(jnp.float32))


EXTRA = 16


def both_ways(number, blocks, weights, me, before=None):
    bf16, f32 = jnp.bfloat16, jnp.float32
    count, width = len(blocks), blocks[0].shape[1]
    units, last = weights[0][0].shape[1], before is not None
    tok_count = (blocks[0].shape[0] - (0 if last else EXTRA)) // 2
    every, size = count * tok_count, 2 * tok_count
    lanes = 128
    back = size + (EXTRA if last else 0)

    def body(me_ref, *refs):
        b_refs, w_refs, refs = refs[:count], refs[count : count + 6], refs[count + 6 :]
        before_refs, refs = (refs[:2], refs[2:]) if last else ((), refs)
        q_refs, refs = refs[:count], refs[count:]
        weighted_ref, factor_ref, refs = refs[0], refs[1], refs[2:]
        after_refs, refs = ((), refs) if last else (refs[:2], refs[2:])
        w_bufs, refs = refs[:6], refs[6:]
        x_buf, c_buf, y_buf, g_buf, weighted_buf, factor_buf, refs = *refs[:6], refs[6:]
        share_buf, inner_buf, wide_buf, extra_buf, sems = refs
        fetch = Fetch(sems)
        me = me_ref[0]
        low = lax.rem(me, 8)
        for b in range(count):
            at = pl.ds(b * tok_count, tok_count)
            fetch.start(("x", b), b_refs[b].at[pl.ds(0, tok_count)], x_buf.at[at])
            if b == 0:
                fetch.start(("w", 0), w_refs[0], w_bufs[0])
        if last:
            fetch.start("share", before_refs[0], share_buf)
            fetch.start("inner", before_refs[1], inner_buf)
        else:
            for b in range(count):
                fetch.start(("s", b), b_refs[b].at[pl.ds(size, EXTRA)], extra_buf.at[b])
        for i in (1, 2):
            fetch.start(("w", i), w_refs[i], w_bufs[i])
        for b in range(count):
            at = pl.ds(b * tok_count, tok_count)
            fetch.start(("c", b), b_refs[b].at[pl.ds(tok_count, tok_count)], c_buf.at[at])
        for i in (3, 4, 5):
            fetch.start(("w", i), w_refs[i], w_bufs[i])

        def place(e):
            number = lax.rem(low + e, 2) + low - lax.rem(low, 2)
            return pl.ds(pl.multiple_of(number * lanes, lanes), lanes)

        upper = me >= 8
        if last:
            fetch.wait("share", "inner")
        else:
            inner_buf[...] = jnp.zeros((lanes, lanes), f32)
            share_buf[...] = jnp.zeros((lanes, lanes), f32)
            for b in range(count):
                fetch.wait(("s", b))
                wide_buf[b] = extra_buf[b].astype(f32)
            for e in range(2):
                for b in range(count):
                    tile = wide_buf[b, :, place(e)]
                    sums = [tile[r : r + 1] + tile[r + 2 : r + 3] + tile[r + 4 : r + 5] for r in (0, 1)]
                    row = e * count + b
                    share_buf[row : row + 1, :] = jnp.where(upper, sums[1], sums[0])
            share_buf[...] = share_buf[...].T

        half = slice(number * tok_count, (number + 1) * tok_count)
        fetch.wait(*[("x", b) for b in range(count)])
        x, y, g = x_buf[...], 0.0, 0.0
        for e in range(2):
            gate_w, up_w, down_w = w_bufs[3 * e : 3 * e + 3]
            columns = slice(e * units, (e + 1) * units)
            fetch.wait(("w", 3 * e))
            gate = dot(x, gate_w[...], ((1,), (0,)))
            fetch.wait(("w", 3 * e + 1))
            up = dot(x, up_w[...], ((1,), (0,)))
            sigma = jax.nn.sigmoid(gate)
            silu_val = gate * sigma
            hidden = silu_val * up
            part = [share_buf[half, e * count + b : e * count + b + 1] for b in range(count)]
            part = jnp.concatenate(part, axis=0)
            weighted = (part * hidden).astype(bf16)
            weighted_buf[:, columns] = weighted
            fetch.wait(("w", 3 * e + 2))
            if e == 0:
                fetch.wait(*[("c", b) for b in range(count)])
            plain = dot(c_buf[...], down_w[...], ((1,), (1,)))
            y = y + dot(weighted, down_w[...], ((1,), (0,)))
            inner = jnp.sum(hidden * plain, axis=1, keepdims=True)
            for b in range(count):
                value = inner[b * tok_count : (b + 1) * tok_count]
                inner_buf[half, e * count + b : e * count + b + 1] = value
            grad_hidden = part * plain
            grad_gate = (grad_hidden * up * (sigma * (1.0 + gate * (1.0 - sigma)))).astype(bf16)
            grad_up = (grad_hidden * silu_val).astype(bf16)
            factor_buf[:, 2 * e * units : (2 * e + 1) * units] = grad_gate
            factor_buf[:, (2 * e + 1) * units : (2 * e + 2) * units] = grad_up
            g = g + dot(grad_gate, gate_w[...], ((1,), (1,)))
            g = g + dot(grad_up, up_w[...], ((1,), (1,)))
        y_buf[...] = y.astype(bf16)
        g_buf[...] = g.astype(bf16)
        for b in range(count):
            at = pl.ds(b * tok_count, tok_count)
            fetch.start(("y", b), y_buf.at[at], q_refs[b].at[pl.ds(0, tok_count)])
            fetch.start(("g", b), g_buf.at[at], q_refs[b].at[pl.ds(tok_count, tok_count)])
        fetch.start("weighted", weighted_buf, weighted_ref)
        fetch.start("factor", factor_buf, factor_ref)
        if last:
            wide_buf[...] = jnp.zeros((count, EXTRA, width), f32)
            inner_buf[...] = inner_buf[...].T
            for e in range(2):
                for b in range(count):
                    row = e * count + b
                    value, lines = inner_buf[row : row + 1, :], []
                    for _ in range(3):
                        piece = value.astype(bf16).astype(f32)
                        lines += [jnp.where(upper, 0.0, piece), jnp.where(upper, piece, 0.0)]
                        value = value - piece
                    lines += [jnp.zeros((2, lanes), f32)]
                    wide_buf[b, 0:8, place(e)] = jnp.concatenate(lines, axis=0)
            for b in range(count):
                extra_buf[b] = wide_buf[b].astype(bf16)
                fetch.start(("i", b), extra_buf.at[b], q_refs[b].at[pl.ds(size, EXTRA)])
        else:
            fetch.start("share", share_buf, after_refs[0])
            fetch.start("inner", inner_buf, after_refs[1])
        fetch.wait_all()

    outs = [shape(back, width, bf16)] * count
    outs += [shape(every, 2 * units, bf16), shape(every, 4 * units, bf16)]
    small = shape(lanes, lanes, f32)
    operands = (*blocks, *weights[0], *weights[1])
    if last:
        operands += before
    else:
        outs += [small, small]
    scratch = [pltpu.VMEM(w.shape, bf16) for w in (*weights[0], *weights[1])]
    scratch += [pltpu.VMEM((every, width), bf16)] * 4
    scratch += [pltpu.VMEM((every, 2 * units), bf16), pltpu.VMEM((every, 4 * units), bf16)]
    scratch += [pltpu.VMEM(small.shape, f32)] * 2
    scratch += [pltpu.VMEM((count, EXTRA, width), f32), pltpu.VMEM((count, EXTRA, width), bf16)]
    flops = 24 * every * width * units
    copies = 5 * count + 6 + 2 + 2
    outs = kernel(body, outs, scratch, copies, flops, *operands, scalar=me)
    return outs[:count], outs[count:]


def weight_grads(expert, blocks, factors, away=None):
    bf16 = jnp.bfloat16
    parts, count, width = len(blocks), len(blocks[0]), blocks[0][0].shape[1]
    each = factors[0][0].shape[0]
    tok_count, every, units = each // count, each * parts, factors[0][0].shape[1] // 2
    extra = 0 if away is None else 1

    def body(*refs):
        b_refs, refs = refs[: parts * count], refs[parts * count :]
        f_refs, refs = refs[: 2 * parts], refs[2 * parts :]
        away_refs, out_refs, refs = refs[:extra], refs[extra : 3 * extra + 1], refs[3 * extra + 1 :]
        x_buf, c_buf, weighted_buf, factor_buf, *bufs, sems = refs
        away_bufs, out_bufs = bufs[:extra], bufs[extra:]
        fetch = Fetch(sems)
        names = range(parts * count)
        for i in names:
            at = pl.ds(i * tok_count, tok_count)
            fetch.start(("x", i), b_refs[i].at[pl.ds(0, tok_count)], x_buf.at[at])
        for p in range(parts):
            at = pl.ds(p * each, each)
            lanes = pl.ds(2 * expert * units, 2 * units)
            fetch.start(("f", p), f_refs[2 * p + 1].at[:, lanes], factor_buf.at[at])
        if extra:
            fetch.start("away", away_refs[0], away_bufs[0])
        for p in range(parts):
            at = pl.ds(p * each, each)
            lanes = pl.ds(expert * units, units)
            fetch.start(("w", p), f_refs[2 * p].at[:, lanes], weighted_buf.at[at])
        for i in names:
            at = pl.ds(i * tok_count, tok_count)
            fetch.start(("c", i), b_refs[i].at[pl.ds(tok_count, tok_count)], c_buf.at[at])
        fetch.wait(*[("x", i) for i in names], *[("f", p) for p in range(parts)])
        for number in range(3):
            if number < 2:
                left, right = x_buf, factor_buf[:, number * units : (number + 1) * units]
                columns, into = slice(number * units, (number + 1) * units), slice(0, width)
            else:
                fetch.wait(*[("c", i) for i in names], *[("w", p) for p in range(parts)])
                left, right = weighted_buf, c_buf[...]
                columns, into = slice(0, width), slice(width, width + units)
            for start in range(0, into.stop - into.start, units):
                value = dot(left[:, start : start + units], right, ((0,), (0,)))
                at = slice(into.start + start, into.start + start + units)
                if not extra:
                    out_bufs[0][at, columns] = value.astype(bf16)
                else:
                    fetch.wait("away")
                    value = value + away_bufs[0][at, columns].astype(jnp.float32)
                    out_bufs[number][start : start + units, :] = value.astype(bf16)
                    block = out_bufs[number].at[start : start + units]
                    target = out_refs[number].at[start : start + units]
                    fetch.start(("out", number, start), block, target)
            if not extra and number:
                at = pl.ds(into.start, into.stop - into.start)
                fetch.start(("out", number), out_bufs[0].at[at], out_refs[0].at[at])
        fetch.wait_all()

    flops = 6 * every * width * units
    operands = (*[b for part in blocks for b in part], *[f for part in factors for f in part])
    scratch = [pltpu.VMEM((every, width), bf16)] * 2
    scratch += [pltpu.VMEM((every, units), bf16), pltpu.VMEM((every, 2 * units), bf16)]
    packed = shape(width + units, width, bf16)
    if away is None:
        outs = [packed]
        scratch += [pltpu.VMEM(packed.shape, bf16)]
    else:
        operands += (away,)
        outs = [shape(width, units, bf16)] * 2 + [shape(units, width, bf16)]
        scratch += [pltpu.VMEM(v.shape, bf16) for v in (packed, *outs)]
    copies = 2 * parts * count + 2 * parts + 1 + 2 * -(-width // units) + 1
    outs = kernel(body, outs, scratch, copies, flops, *operands)
    return outs if extra else outs[0]


def paired(latent_in, routes, combine_weights, cotangent, w_gate, w_up, w_down):
    f32 = jnp.float32
    devices_ep, tok_count, width = lax.axis_size("ep"), *latent_in.shape
    me = lax.axis_index("ep")
    mid = tok_count // 2
    experts = jnp.arange(devices_ep, dtype=jnp.int32)
    own = (w_gate[0], w_up[0], w_down[0])

    chosen = routes[None, :, :] == experts[:, None, None]
    share = jnp.sum(jnp.where(chosen, combine_weights[None, :, :], 0.0), axis=2)
    lines = jnp.stack(pieces(share)).reshape(-1, width)
    lines = jnp.pad(lines, ((0, EXTRA - lines.shape[0]), (0, 0)))
    a0 = jnp.concatenate([latent_in[:mid], cotangent[:mid], lines], axis=0)
    b0 = jnp.concatenate([latent_in[mid:], cotangent[mid:]], axis=0)
    a0, b0, own = fence(a0, b0, own)

    a4, a2, a1, b4 = swap(a0, SIDE), swap(a0, FAR), swap(a0, NEAR), swap(b0, SIDE)
    gate_w = swap(own[0], CORE)
    a2, a4, b4, a1, gate_w, a0, b0, own = fence(a2, a4, b4, a1, gate_w, a0, b0, own)
    a6, a5, b2, a3 = swap(a2, SIDE), swap(a1, SIDE), swap(b0, FAR), swap(a2, NEAR)
    up_w = swap(own[1], CORE)
    b2, a5, a6, a3, up_w, a0, b0, own = fence(b2, a5, a6, a3, up_w, a0, b0, own)
    a7, b6, b1, b3 = swap(a3, SIDE), swap(b2, SIDE), swap(b0, NEAR), swap(b2, NEAR)
    down_w = swap(own[2], CORE)
    a7, b6, b3, b1, down_w, a0, b0, own = fence(a7, b6, b3, b1, down_w, a0, b0, own)
    b5, b7 = swap(b1, SIDE), swap(b3, SIDE)
    weights, me = (own, (gate_w, up_w, down_w)), me.astype(jnp.int32).reshape(1)
    a = [a0, a1, a2, a3, a4, a5, a6, a7]
    q, (*a_factors, shares, inners) = both_ways(0, a, weights, me)
    q, shares, inners, b5, b7 = fence(q, shares, inners, b5, b7)
    q7, q5 = swap(q[7], SIDE), swap(q[5], SIDE)
    b = [b0, b1, b2, b3, b4, b5, b6, b7]
    p, b_factors = both_ways(1, b, weights, me, (shares, inners))
    p, q, q7, q5, b_factors = fence(p, q, q7, q5, b_factors)
    factors = (a_factors, b_factors)
    q3, q1 = narrow(added(q[3], q7)), narrow(added(q[1], q5))
    q3, q1, p, q = fence(q3, q1, p, q)
    q6, p7, q3, q1 = swap(q[6], SIDE), swap(p[7], SIDE), swap(q3, NEAR), swap(q1, NEAR)
    away = weight_grads(1, (a, b), factors)
    q6, p7, q3, q1, away, p, q = fence(q6, p7, q3, q1, away, p, q)
    q2, p3 = narrow(added(q[2], q6) + q3.astype(f32)), narrow(added(p[3], p7))
    q2, p3, p, q, away = fence(q2, p3, p, q, away)
    p6, p5, q2, p3 = swap(p[6], SIDE), swap(p[5], SIDE), swap(q2, FAR), swap(p3, NEAR)
    away = swap(away, CORE)
    q2, p6, p5, p3, away, p, q = fence(q2, p6, p5, p3, away, p, q)
    p2, p1 = narrow(added(p[2], p6) + p3.astype(f32)), narrow(added(p[1], p5))
    p2, p1, p, q, away = fence(p2, p1, p, q, away)
    p4, q4, p2, p1 = swap(p[4], SIDE), swap(q[4], SIDE), swap(p2, FAR), swap(p1, NEAR)
    grad_w = weight_grads(0, (a, b), factors, away)
    p2, p4, q4, p1, grad_w = fence(p2, p4, q4, p1, grad_w)

    q = added(q[0], q4) + added(q1, q2)
    p = added(p[0], p4) + added(p1, p2)
    combined = narrow(jnp.concatenate([q[:mid], p[:mid]], axis=0))
    grad_latent = narrow(jnp.concatenate([q[mid : 2 * mid], p[mid : 2 * mid]], axis=0))
    inner = p[2 * mid :].reshape(-1, devices_ep, tok_count)[:3].sum(axis=0)
    grad_combine = jnp.sum(jnp.where(chosen, inner[:, :, None], 0.0), axis=0)
    return (combined, grad_latent, grad_combine, *[v[None] for v in grad_w])


def local(latent_in, routes, combine_weights, cotangent, w_gate, w_up, w_down):
    plan = paired if w_gate.shape[0] == 1 and lax.axis_size("ep") == 2 * len(REACH) else exchanged
    return plan(latent_in, routes, combine_weights, cotangent, w_gate, w_up, w_down)


def solution(mesh):
    return jax.shard_map(
        local,
        mesh=mesh,
        in_specs=(
            P(("grp", "ep"), None),
            P(("grp", "ep"), None),
            P(("grp", "ep"), None),
            P(("grp", "ep"), None),
            P("ep", None, None),
            P("ep", None, None),
            P("ep", None, None),
        ),
        out_specs=(
            P(("grp", "ep"), None),
            P(("grp", "ep"), None),
            P(("grp", "ep"), None),
            P(("grp", "ep"), None, None),
            P(("grp", "ep"), None, None),
            P(("grp", "ep"), None, None),
        ),
        check_vma=False,
    )
```

```python
import jax
import jax.numpy as jnp
from jax import lax
from jax.experimental import pallas as pl
from jax.experimental.pallas import tpu as pltpu
from jax.sharding import PartitionSpec as P


def assign_slots(route_rows, expert_count):
    flat_ids = route_rows.reshape(-1)
    onehot = (flat_ids[:, None] == jnp.arange(expert_count, dtype=jnp.int32)[None, :]).astype(
        jnp.int32
    )
    ranks = jnp.cumsum(onehot, axis=0) - 1
    return (flat_ids, jnp.sum(onehot * ranks, axis=1))


def expert_forward(rows, gate_w, up_w, down_w):
    gate_pre = jnp.einsum("erl,elf->erf", rows, gate_w, preferred_element_type=jnp.float32)
    up_pre = jnp.einsum("erl,elf->erf", rows, up_w, preferred_element_type=jnp.float32)
    sigma = jax.nn.sigmoid(gate_pre)
    silu_val = gate_pre * sigma
    hidden = (silu_val * up_pre).astype(jnp.bfloat16)
    expert_out = jnp.einsum(
        "erf,efl->erl", hidden, down_w, preferred_element_type=jnp.float32
    ).astype(jnp.bfloat16)
    return (expert_out, (gate_pre, up_pre, sigma, silu_val, hidden))


def expert_backward(rows, grad_out, saved, gate_w, up_w, down_w):
    gate_pre, up_pre, sigma, silu_val, hidden = saved
    grad_down = jnp.einsum(
        "erf,erl->efl", hidden, grad_out, preferred_element_type=jnp.float32
    ).astype(jnp.bfloat16)
    grad_hidden = jnp.einsum("erl,efl->erf", grad_out, down_w, preferred_element_type=jnp.float32)
    grad_gate = (grad_hidden * up_pre * sigma * (1.0 + gate_pre * (1.0 - sigma))).astype(
        jnp.bfloat16
    )
    grad_up = (grad_hidden * silu_val).astype(jnp.bfloat16)
    grad_gw = jnp.einsum(
        "erl,erf->elf", rows, grad_gate, preferred_element_type=jnp.float32
    ).astype(jnp.bfloat16)
    grad_uw = jnp.einsum("erl,erf->elf", rows, grad_up, preferred_element_type=jnp.float32).astype(
        jnp.bfloat16
    )
    grad_rows = (
        jnp.einsum("erf,elf->erl", grad_gate, gate_w, preferred_element_type=jnp.float32)
        + jnp.einsum("erf,elf->erl", grad_up, up_w, preferred_element_type=jnp.float32)
    ).astype(jnp.bfloat16)
    return (grad_rows, grad_gw, grad_uw, grad_down)


def exchanged(latent_in, routes, combine_weights, cotangent, w_gate, w_up, w_down):
    devices_ep = lax.axis_size("ep")
    local_experts = w_gate.shape[0]
    expert_count = local_experts * devices_ep
    tok_count = latent_in.shape[0]
    top_count = routes.shape[1]
    width = latent_in.shape[1]
    capacity = tok_count * top_count * 3 // (2 * expert_count)
    expert_ids, slot_ids = assign_slots(routes, expert_count)
    position = expert_ids * capacity + slot_ids
    repeated = jnp.repeat(latent_in, top_count, axis=0)
    weighted = (combine_weights[:, :, None] * cotangent.astype(jnp.float32)[:, None, :]).astype(
        jnp.bfloat16
    )
    send_rows = jnp.zeros((expert_count * capacity, width), jnp.bfloat16).at[position].set(repeated)
    send_rows = send_rows.reshape(expert_count, capacity, width)
    send_cot = (
        jnp.zeros((expert_count * capacity, width), jnp.bfloat16)
        .at[position]
        .set(weighted.reshape(-1, width))
    )
    send_cot = send_cot.reshape(expert_count, capacity, width)

    def to_local(received):
        shaped = received.reshape(devices_ep, local_experts, capacity, width)
        return shaped.transpose(1, 0, 2, 3).reshape(local_experts, devices_ep * capacity, width)

    def to_home(local_rows):
        shaped = local_rows.reshape(local_experts, devices_ep, capacity, width)
        return shaped.transpose(1, 0, 2, 3).reshape(expert_count, capacity, width)

    got_rows = lax.all_to_all(send_rows, "ep", split_axis=0, concat_axis=0, tiled=True)
    rows_local = to_local(got_rows)
    expert_out, saved = expert_forward(rows_local, w_gate, w_up, w_down)
    back_out = lax.all_to_all(to_home(expert_out), "ep", split_axis=0, concat_axis=0, tiled=True)
    got_cot = lax.all_to_all(send_cot, "ep", split_axis=0, concat_axis=0, tiled=True)
    grad_rows, grad_gw, grad_uw, grad_down = expert_backward(
        rows_local, to_local(got_cot), saved, w_gate, w_up, w_down
    )
    back_grad = lax.all_to_all(to_home(grad_rows), "ep", split_axis=0, concat_axis=0, tiled=True)
    out_rows = (
        back_out.reshape(-1, width)[position]
        .reshape(tok_count, top_count, width)
        .astype(jnp.float32)
    )
    grad_back = (
        back_grad.reshape(-1, width)[position]
        .reshape(tok_count, top_count, width)
        .astype(jnp.float32)
    )
    combined = jnp.sum(combine_weights[:, :, None] * out_rows, axis=1).astype(jnp.bfloat16)
    grad_combine = jnp.sum(cotangent.astype(jnp.float32)[:, None, :] * out_rows, axis=2)
    grad_latent = jnp.sum(grad_back, axis=1).astype(jnp.bfloat16)
    return (combined, grad_latent, grad_combine, grad_gw, grad_uw, grad_down)


def dot(a, b, dims):
    return lax.dot_general(a, b, (dims, ((), ())), preferred_element_type=jnp.float32)


def swap(value, bit):
    pairs = [(i, i ^ bit) for i in range(lax.axis_size("ep"))]
    return lax.ppermute(value, "ep", pairs)


CORE, SIDE, NEAR, FAR = 1, 2, 4, 8
REACH = (0, NEAR, FAR, NEAR | FAR, SIDE, SIDE | NEAR, SIDE | FAR, SIDE | NEAR | FAR)


def fence(*values):
    return lax.optimization_barrier(values)


def added(a, b):
    return a.astype(jnp.float32) + b.astype(jnp.float32)


def narrow(value):
    return value.astype(jnp.bfloat16)


MIB = 1 << 20


class Fetch:
    def __init__(self, sems):
        self.sems, self.waiting = sems, {}

    def start(self, name, source, target):
        copy = pltpu.make_async_copy(source, target, self.sems.at[len(self.waiting)])
        copy.start()
        self.waiting[name] = [copy, False]

    def wait(self, *names):
        for name in names:
            if not self.waiting[name][1]:
                self.waiting[name][0].wait()
                self.waiting[name][1] = True

    def wait_all(self):
        self.wait(*self.waiting)


def kernel(body, outs, scratch, copies, flops, *operands, scalar=None):
    moved = sum(v.size * v.dtype.itemsize for v in (*operands, *outs))
    in_specs = [pl.BlockSpec(memory_space=pl.ANY)] * len(operands)
    if scalar is not None:
        operands = (scalar, *operands)
        in_specs = [pl.BlockSpec(memory_space=pltpu.SMEM), *in_specs]
    return pl.pallas_call(
        body,
        out_shape=outs,
        in_specs=in_specs,
        out_specs=[pl.BlockSpec(memory_space=pl.ANY)] * len(outs),
        scratch_shapes=[*scratch, pltpu.SemaphoreType.DMA((copies,))],
        compiler_params=pltpu.CompilerParams(vmem_limit_bytes=56 * MIB),
        cost_estimate=pl.CostEstimate(flops=flops, bytes_accessed=moved, transcendentals=0),
    )(*operands)


def shape(rows, columns, dtype):
    return jax.ShapeDtypeStruct((rows, columns), dtype)


def pieces(value):
    first = narrow(value)
    value = value - first.astype(jnp.float32)
    second = narrow(value)
    return first, second, narrow(value - second.astype(jnp.float32))


EXTRA = 16


def both_ways(number, blocks, weights, me, before=None):
    bf16, f32 = jnp.bfloat16, jnp.float32
    count, width = len(blocks), blocks[0].shape[1]
    units, last = weights[0][0].shape[1], before is not None
    tok_count = (blocks[0].shape[0] - (0 if last else EXTRA)) // 2
    every, size = count * tok_count, 2 * tok_count
    lanes = 128
    back = size + (EXTRA if last else 0)

    def body(me_ref, *refs):
        b_refs, w_refs, refs = refs[:count], refs[count : count + 6], refs[count + 6 :]
        before_refs, refs = (refs[:2], refs[2:]) if last else ((), refs)
        q_refs, refs = refs[:count], refs[count:]
        weighted_ref, factor_ref, refs = refs[0], refs[1], refs[2:]
        after_refs, refs = ((), refs) if last else (refs[:2], refs[2:])
        wide_w, down_w, refs = refs[0], refs[1], refs[2:]
        x_buf, c_buf, y_buf, g_buf, weighted_buf, factor_buf, refs = *refs[:6], refs[6:]
        share_buf, inner_buf, wide_buf, extra_buf, sems = refs
        fetch = Fetch(sems)
        w_bufs = []
        for e in range(2):
            for i in (2 * e, 2 * e + 1):
                w_bufs.append(wide_w.at[:, pl.ds(i * units, units)])
            w_bufs.append(down_w.at[pl.ds(e * units, units)])
        me = me_ref[0]
        low = lax.rem(me, 8)
        for b in range(count):
            at = pl.ds(b * tok_count, tok_count)
            fetch.start(("x", b), b_refs[b].at[pl.ds(0, tok_count)], x_buf.at[at])
            if b == 0:
                fetch.start(("w", 0), w_refs[0], w_bufs[0])
        if last:
            fetch.start("share", before_refs[0], share_buf)
            fetch.start("inner", before_refs[1], inner_buf)
        else:
            for b in range(count):
                fetch.start(("s", b), b_refs[b].at[pl.ds(size, EXTRA)], extra_buf.at[b])
        for i in (1, 2):
            fetch.start(("w", i), w_refs[i], w_bufs[i])
        for b in range(count):
            at = pl.ds(b * tok_count, tok_count)
            fetch.start(("c", b), b_refs[b].at[pl.ds(tok_count, tok_count)], c_buf.at[at])
        for i in (3, 4, 5):
            fetch.start(("w", i), w_refs[i], w_bufs[i])

        def place(e):
            number = lax.rem(low + e, 2) + low - lax.rem(low, 2)
            return pl.ds(pl.multiple_of(number * lanes, lanes), lanes)

        upper = me >= 8
        if last:
            fetch.wait("share", "inner")
        else:
            inner_buf[...] = jnp.zeros((lanes, lanes), f32)
            share_buf[...] = jnp.zeros((lanes, lanes), f32)
            for b in range(count):
                fetch.wait(("s", b))
                wide_buf[b] = extra_buf[b].astype(f32)
            for e in range(2):
                for b in range(count):
                    tile = wide_buf[b, :, place(e)]
                    sums = [tile[r : r + 1] + tile[r + 2 : r + 3] + tile[r + 4 : r + 5] for r in (0, 1)]
                    row = e * count + b
                    share_buf[row : row + 1, :] = jnp.where(upper, sums[1], sums[0])
            share_buf[...] = share_buf[...].T

        half = slice(number * tok_count, (number + 1) * tok_count)
        fetch.wait(*[("x", b) for b in range(count)])
        x = x_buf[...]
        for e in range(2):
            columns = slice(e * units, (e + 1) * units)
            fetch.wait(("w", 3 * e))
            gate = dot(x, wide_w[:, 2 * e * units : (2 * e + 1) * units], ((1,), (0,)))
            fetch.wait(("w", 3 * e + 1))
            up = dot(x, wide_w[:, (2 * e + 1) * units : (2 * e + 2) * units], ((1,), (0,)))
            fetch.wait(("w", 3 * e + 2))
            if e == 0:
                fetch.wait(*[("c", b) for b in range(count)])
            plain = dot(c_buf[...], down_w[columns, :], ((1,), (1,)))
            sigma = jax.nn.sigmoid(gate)
            silu_val = gate * sigma
            hidden = silu_val * up
            part = [share_buf[half, e * count + b : e * count + b + 1] for b in range(count)]
            part = jnp.concatenate(part, axis=0)
            weighted_buf[:, columns] = (part * hidden).astype(bf16)
            inner = jnp.sum(hidden * plain, axis=1, keepdims=True)
            for b in range(count):
                value = inner[b * tok_count : (b + 1) * tok_count]
                inner_buf[half, e * count + b : e * count + b + 1] = value
            grad_hidden = part * plain
            grad_gate = (grad_hidden * up * (sigma * (1.0 + gate * (1.0 - sigma)))).astype(bf16)
            grad_up = (grad_hidden * silu_val).astype(bf16)
            factor_buf[:, 2 * e * units : (2 * e + 1) * units] = grad_gate
            factor_buf[:, (2 * e + 1) * units : (2 * e + 2) * units] = grad_up
        fetch.start("weighted", weighted_buf, weighted_ref)
        fetch.start("factor", factor_buf, factor_ref)
        y_buf[...] = dot(weighted_buf[...], down_w[...], ((1,), (0,))).astype(bf16)
        for b in range(count):
            at = pl.ds(b * tok_count, tok_count)
            fetch.start(("y", b), y_buf.at[at], q_refs[b].at[pl.ds(0, tok_count)])
        g_buf[...] = dot(factor_buf[...], wide_w[...], ((1,), (1,))).astype(bf16)
        for b in range(count):
            at = pl.ds(b * tok_count, tok_count)
            fetch.start(("g", b), g_buf.at[at], q_refs[b].at[pl.ds(tok_count, tok_count)])
        if last:
            wide_buf[...] = jnp.zeros((count, EXTRA, width), f32)
            inner_buf[...] = inner_buf[...].T
            for e in range(2):
                for b in range(count):
                    row = e * count + b
                    value, lines = inner_buf[row : row + 1, :], []
                    for _ in range(3):
                        piece = value.astype(bf16).astype(f32)
                        lines += [jnp.where(upper, 0.0, piece), jnp.where(upper, piece, 0.0)]
                        value = value - piece
                    lines += [jnp.zeros((2, lanes), f32)]
                    wide_buf[b, 0:8, place(e)] = jnp.concatenate(lines, axis=0)
            for b in range(count):
                extra_buf[b] = wide_buf[b].astype(bf16)
                fetch.start(("i", b), extra_buf.at[b], q_refs[b].at[pl.ds(size, EXTRA)])
        else:
            fetch.start("share", share_buf, after_refs[0])
            fetch.start("inner", inner_buf, after_refs[1])
        fetch.wait_all()

    outs = [shape(back, width, bf16)] * count
    outs += [shape(every, 2 * units, bf16), shape(every, 4 * units, bf16)]
    small = shape(lanes, lanes, f32)
    operands = (*blocks, *weights[0], *weights[1])
    if last:
        operands += before
    else:
        outs += [small, small]
    scratch = [pltpu.VMEM((width, 4 * units), bf16), pltpu.VMEM((2 * units, width), bf16)]
    scratch += [pltpu.VMEM((every, width), bf16)] * 4
    scratch += [pltpu.VMEM((every, 2 * units), bf16), pltpu.VMEM((every, 4 * units), bf16)]
    scratch += [pltpu.VMEM(small.shape, f32)] * 2
    scratch += [pltpu.VMEM((count, EXTRA, width), f32), pltpu.VMEM((count, EXTRA, width), bf16)]
    flops = 24 * every * width * units
    copies = 5 * count + 6 + 2 + 2
    outs = kernel(body, outs, scratch, copies, flops, *operands, scalar=me)
    return outs[:count], outs[count:]


def weight_grads(expert, blocks, factors, away=None):
    bf16 = jnp.bfloat16
    parts, count, width = len(blocks), len(blocks[0]), blocks[0][0].shape[1]
    each = factors[0][0].shape[0]
    tok_count, every, units = each // count, each * parts, factors[0][0].shape[1] // 2
    extra = 0 if away is None else 1

    def body(*refs):
        b_refs, refs = refs[: parts * count], refs[parts * count :]
        f_refs, refs = refs[: 2 * parts], refs[2 * parts :]
        away_refs, out_refs, refs = refs[:extra], refs[extra : 3 * extra + 1], refs[3 * extra + 1 :]
        x_buf, c_buf, weighted_buf, factor_buf, *bufs, sems = refs
        away_bufs, out_bufs = bufs[:extra], bufs[extra:]
        fetch = Fetch(sems)
        names = range(parts * count)
        for i in names:
            at = pl.ds(i * tok_count, tok_count)
            fetch.start(("x", i), b_refs[i].at[pl.ds(0, tok_count)], x_buf.at[at])
        for p in range(parts):
            at = pl.ds(p * each, each)
            lanes = pl.ds(2 * expert * units, 2 * units)
            fetch.start(("f", p), f_refs[2 * p + 1].at[:, lanes], factor_buf.at[at])
        if extra:
            fetch.start("away", away_refs[0], away_bufs[0])
        for p in range(parts):
            at = pl.ds(p * each, each)
            lanes = pl.ds(expert * units, units)
            fetch.start(("w", p), f_refs[2 * p].at[:, lanes], weighted_buf.at[at])
        for i in names:
            at = pl.ds(i * tok_count, tok_count)
            fetch.start(("c", i), b_refs[i].at[pl.ds(tok_count, tok_count)], c_buf.at[at])
        fetch.wait(*[("x", i) for i in names], *[("f", p) for p in range(parts)])
        for number in range(3):
            if number < 2:
                left, right = x_buf, factor_buf[:, number * units : (number + 1) * units]
                columns, into = slice(number * units, (number + 1) * units), slice(0, width)
            else:
                fetch.wait(*[("c", i) for i in names], *[("w", p) for p in range(parts)])
                left, right = weighted_buf, c_buf[...]
                columns, into = slice(0, width), slice(width, width + units)
            for start in range(0, into.stop - into.start, units):
                value = dot(left[:, start : start + units], right, ((0,), (0,)))
                at = slice(into.start + start, into.start + start + units)
                if not extra:
                    out_bufs[0][at, columns] = value.astype(bf16)
                else:
                    fetch.wait("away")
                    value = value + away_bufs[0][at, columns].astype(jnp.float32)
                    out_bufs[number][start : start + units, :] = value.astype(bf16)
                    block = out_bufs[number].at[start : start + units]
                    target = out_refs[number].at[start : start + units]
                    fetch.start(("out", number, start), block, target)
            if not extra and number:
                at = pl.ds(into.start, into.stop - into.start)
                fetch.start(("out", number), out_bufs[0].at[at], out_refs[0].at[at])
        fetch.wait_all()

    flops = 6 * every * width * units
    operands = (*[b for part in blocks for b in part], *[f for part in factors for f in part])
    scratch = [pltpu.VMEM((every, width), bf16)] * 2
    scratch += [pltpu.VMEM((every, units), bf16), pltpu.VMEM((every, 2 * units), bf16)]
    packed = shape(width + units, width, bf16)
    if away is None:
        outs = [packed]
        scratch += [pltpu.VMEM(packed.shape, bf16)]
    else:
        operands += (away,)
        outs = [shape(width, units, bf16)] * 2 + [shape(units, width, bf16)]
        scratch += [pltpu.VMEM(v.shape, bf16) for v in (packed, *outs)]
    copies = 2 * parts * count + 2 * parts + 1 + 2 * -(-width // units) + 1
    outs = kernel(body, outs, scratch, copies, flops, *operands)
    return outs if extra else outs[0]


def paired(latent_in, routes, combine_weights, cotangent, w_gate, w_up, w_down):
    f32 = jnp.float32
    devices_ep, tok_count, width = lax.axis_size("ep"), *latent_in.shape
    me = lax.axis_index("ep")
    mid = tok_count // 2
    experts = jnp.arange(devices_ep, dtype=jnp.int32)
    own = (w_gate[0], w_up[0], w_down[0])

    chosen = routes[None, :, :] == experts[:, None, None]
    share = jnp.sum(jnp.where(chosen, combine_weights[None, :, :], 0.0), axis=2)
    lines = jnp.stack(pieces(share)).reshape(-1, width)
    lines = jnp.pad(lines, ((0, EXTRA - lines.shape[0]), (0, 0)))
    a0 = jnp.concatenate([latent_in[:mid], cotangent[:mid], lines], axis=0)
    b0 = jnp.concatenate([latent_in[mid:], cotangent[mid:]], axis=0)
    a0, b0, own = fence(a0, b0, own)

    a4, a2, a1, b4 = swap(a0, SIDE), swap(a0, FAR), swap(a0, NEAR), swap(b0, SIDE)
    gate_w = swap(own[0], CORE)
    a2, a4, b4, a1, gate_w, a0, b0, own = fence(a2, a4, b4, a1, gate_w, a0, b0, own)
    a6, a5, b2, a3 = swap(a2, SIDE), swap(a1, SIDE), swap(b0, FAR), swap(a2, NEAR)
    up_w = swap(own[1], CORE)
    b2, a5, a6, a3, up_w, a0, b0, own = fence(b2, a5, a6, a3, up_w, a0, b0, own)
    a7, b6, b1, b3 = swap(a3, SIDE), swap(b2, SIDE), swap(b0, NEAR), swap(b2, NEAR)
    down_w = swap(own[2], CORE)
    a7, b6, b3, b1, down_w, a0, b0, own = fence(a7, b6, b3, b1, down_w, a0, b0, own)
    b5, b7 = swap(b1, SIDE), swap(b6, NEAR)
    weights, me = (own, (gate_w, up_w, down_w)), me.astype(jnp.int32).reshape(1)
    a = [a0, a1, a2, a3, a4, a5, a6, a7]
    q, (*a_factors, shares, inners) = both_ways(0, a, weights, me)
    q, shares, inners, b5, b7 = fence(q, shares, inners, b5, b7)
    q5, q7, q3 = swap(q[5], SIDE), swap(q[7], NEAR), swap(q[3], NEAR)
    b = [b0, b1, b2, b3, b4, b5, b6, b7]
    p, b_factors = both_ways(1, b, weights, me, (shares, inners))
    q5, q7, q3, p, q, b_factors = fence(q5, q7, q3, p, q, b_factors)
    factors = (a_factors, b_factors)
    q6, q2, q1 = narrow(added(q[6], q7)), added(q[2], q3), narrow(added(q[1], q5))
    q6, q2, q1, p, q = fence(q6, q2, q1, p, q)
    q6, p7, q1 = swap(q6, SIDE), swap(p[7], SIDE), swap(q1, NEAR)
    away = weight_grads(1, (a, b), factors)
    q6, p7, q1, q2, away, p, q = fence(q6, p7, q1, q2, away, p, q)
    q2, p3 = narrow(q2 + q6.astype(f32)), narrow(added(p[3], p7))
    q2, p3, p, q, away = fence(q2, p3, p, q, away)
    p6, p5, q2, p3 = swap(p[6], SIDE), swap(p[5], SIDE), swap(q2, FAR), swap(p3, NEAR)
    away = swap(away, CORE)
    q2, p6, p5, p3, away, p, q = fence(q2, p6, p5, p3, away, p, q)
    p2, p1 = narrow(added(p[2], p6) + p3.astype(f32)), narrow(added(p[1], p5))
    p2, p1, p, q, away = fence(p2, p1, p, q, away)
    p4, q4, p2, p1 = swap(p[4], SIDE), swap(q[4], SIDE), swap(p2, FAR), swap(p1, NEAR)
    grad_w = weight_grads(0, (a, b), factors, away)
    p2, p4, q4, p1, grad_w = fence(p2, p4, q4, p1, grad_w)

    q = added(q[0], q4) + added(q1, q2)
    p = added(p[0], p4) + added(p1, p2)
    combined = narrow(jnp.concatenate([q[:mid], p[:mid]], axis=0))
    grad_latent = narrow(jnp.concatenate([q[mid : 2 * mid], p[mid : 2 * mid]], axis=0))
    inner = p[2 * mid :].reshape(-1, devices_ep, tok_count)[:3].sum(axis=0)
    grad_combine = jnp.sum(jnp.where(chosen, inner[:, :, None], 0.0), axis=0)
    return (combined, grad_latent, grad_combine, *[v[None] for v in grad_w])


def local(latent_in, routes, combine_weights, cotangent, w_gate, w_up, w_down):
    plan = paired if w_gate.shape[0] == 1 and lax.axis_size("ep") == 2 * len(REACH) else exchanged
    return plan(latent_in, routes, combine_weights, cotangent, w_gate, w_up, w_down)


def solution(mesh):
    return jax.shard_map(
        local,
        mesh=mesh,
        in_specs=(
            P(("grp", "ep"), None),
            P(("grp", "ep"), None),
            P(("grp", "ep"), None),
            P(("grp", "ep"), None),
            P("ep", None, None),
            P("ep", None, None),
            P("ep", None, None),
        ),
        out_specs=(
            P(("grp", "ep"), None),
            P(("grp", "ep"), None),
            P(("grp", "ep"), None),
            P(("grp", "ep"), None, None),
            P(("grp", "ep"), None, None),
            P(("grp", "ep"), None, None),
        ),
        check_vma=False,
    )
```

```python
import jax
import jax.numpy as jnp
from jax import lax
from jax.experimental import pallas as pl
from jax.experimental.pallas import tpu as pltpu
from jax.sharding import PartitionSpec as P


def assign_slots(route_rows, expert_count):
    flat_ids = route_rows.reshape(-1)
    onehot = (flat_ids[:, None] == jnp.arange(expert_count, dtype=jnp.int32)[None, :]).astype(
        jnp.int32
    )
    ranks = jnp.cumsum(onehot, axis=0) - 1
    return (flat_ids, jnp.sum(onehot * ranks, axis=1))


def expert_forward(rows, gate_w, up_w, down_w):
    gate_pre = jnp.einsum("erl,elf->erf", rows, gate_w, preferred_element_type=jnp.float32)
    up_pre = jnp.einsum("erl,elf->erf", rows, up_w, preferred_element_type=jnp.float32)
    sigma = jax.nn.sigmoid(gate_pre)
    silu_val = gate_pre * sigma
    hidden = (silu_val * up_pre).astype(jnp.bfloat16)
    expert_out = jnp.einsum(
        "erf,efl->erl", hidden, down_w, preferred_element_type=jnp.float32
    ).astype(jnp.bfloat16)
    return (expert_out, (gate_pre, up_pre, sigma, silu_val, hidden))


def expert_backward(rows, grad_out, saved, gate_w, up_w, down_w):
    gate_pre, up_pre, sigma, silu_val, hidden = saved
    grad_down = jnp.einsum(
        "erf,erl->efl", hidden, grad_out, preferred_element_type=jnp.float32
    ).astype(jnp.bfloat16)
    grad_hidden = jnp.einsum("erl,efl->erf", grad_out, down_w, preferred_element_type=jnp.float32)
    grad_gate = (grad_hidden * up_pre * sigma * (1.0 + gate_pre * (1.0 - sigma))).astype(
        jnp.bfloat16
    )
    grad_up = (grad_hidden * silu_val).astype(jnp.bfloat16)
    grad_gw = jnp.einsum(
        "erl,erf->elf", rows, grad_gate, preferred_element_type=jnp.float32
    ).astype(jnp.bfloat16)
    grad_uw = jnp.einsum("erl,erf->elf", rows, grad_up, preferred_element_type=jnp.float32).astype(
        jnp.bfloat16
    )
    grad_rows = (
        jnp.einsum("erf,elf->erl", grad_gate, gate_w, preferred_element_type=jnp.float32)
        + jnp.einsum("erf,elf->erl", grad_up, up_w, preferred_element_type=jnp.float32)
    ).astype(jnp.bfloat16)
    return (grad_rows, grad_gw, grad_uw, grad_down)


def exchanged(latent_in, routes, combine_weights, cotangent, w_gate, w_up, w_down):
    devices_ep = lax.axis_size("ep")
    local_experts = w_gate.shape[0]
    expert_count = local_experts * devices_ep
    tok_count = latent_in.shape[0]
    top_count = routes.shape[1]
    width = latent_in.shape[1]
    capacity = tok_count * top_count * 3 // (2 * expert_count)
    expert_ids, slot_ids = assign_slots(routes, expert_count)
    position = expert_ids * capacity + slot_ids
    repeated = jnp.repeat(latent_in, top_count, axis=0)
    weighted = (combine_weights[:, :, None] * cotangent.astype(jnp.float32)[:, None, :]).astype(
        jnp.bfloat16
    )
    send_rows = jnp.zeros((expert_count * capacity, width), jnp.bfloat16).at[position].set(repeated)
    send_rows = send_rows.reshape(expert_count, capacity, width)
    send_cot = (
        jnp.zeros((expert_count * capacity, width), jnp.bfloat16)
        .at[position]
        .set(weighted.reshape(-1, width))
    )
    send_cot = send_cot.reshape(expert_count, capacity, width)

    def to_local(received):
        shaped = received.reshape(devices_ep, local_experts, capacity, width)
        return shaped.transpose(1, 0, 2, 3).reshape(local_experts, devices_ep * capacity, width)

    def to_home(local_rows):
        shaped = local_rows.reshape(local_experts, devices_ep, capacity, width)
        return shaped.transpose(1, 0, 2, 3).reshape(expert_count, capacity, width)

    got_rows = lax.all_to_all(send_rows, "ep", split_axis=0, concat_axis=0, tiled=True)
    rows_local = to_local(got_rows)
    expert_out, saved = expert_forward(rows_local, w_gate, w_up, w_down)
    back_out = lax.all_to_all(to_home(expert_out), "ep", split_axis=0, concat_axis=0, tiled=True)
    got_cot = lax.all_to_all(send_cot, "ep", split_axis=0, concat_axis=0, tiled=True)
    grad_rows, grad_gw, grad_uw, grad_down = expert_backward(
        rows_local, to_local(got_cot), saved, w_gate, w_up, w_down
    )
    back_grad = lax.all_to_all(to_home(grad_rows), "ep", split_axis=0, concat_axis=0, tiled=True)
    out_rows = (
        back_out.reshape(-1, width)[position]
        .reshape(tok_count, top_count, width)
        .astype(jnp.float32)
    )
    grad_back = (
        back_grad.reshape(-1, width)[position]
        .reshape(tok_count, top_count, width)
        .astype(jnp.float32)
    )
    combined = jnp.sum(combine_weights[:, :, None] * out_rows, axis=1).astype(jnp.bfloat16)
    grad_combine = jnp.sum(cotangent.astype(jnp.float32)[:, None, :] * out_rows, axis=2)
    grad_latent = jnp.sum(grad_back, axis=1).astype(jnp.bfloat16)
    return (combined, grad_latent, grad_combine, grad_gw, grad_uw, grad_down)


def dot(a, b, dims):
    return lax.dot_general(a, b, (dims, ((), ())), preferred_element_type=jnp.float32)


def swap(value, bit):
    pairs = [(i, i ^ bit) for i in range(lax.axis_size("ep"))]
    return lax.ppermute(value, "ep", pairs)


CORE, SIDE, NEAR, FAR = 1, 2, 4, 8
REACH = (0, NEAR, FAR, NEAR | FAR, SIDE, SIDE | NEAR, SIDE | FAR, SIDE | NEAR | FAR)


def fence(*values):
    return lax.optimization_barrier(values)


def added(a, b):
    return a.astype(jnp.float32) + b.astype(jnp.float32)


def narrow(value):
    return value.astype(jnp.bfloat16)


MIB = 1 << 20


class Fetch:
    def __init__(self, sems):
        self.sems, self.waiting = sems, {}

    def start(self, name, source, target):
        copy = pltpu.make_async_copy(source, target, self.sems.at[len(self.waiting)])
        copy.start()
        self.waiting[name] = [copy, False]

    def wait(self, *names):
        for name in names:
            if not self.waiting[name][1]:
                self.waiting[name][0].wait()
                self.waiting[name][1] = True

    def wait_all(self):
        self.wait(*self.waiting)


def kernel(body, outs, scratch, copies, flops, *operands, scalar=None):
    moved = sum(v.size * v.dtype.itemsize for v in (*operands, *outs))
    in_specs = [pl.BlockSpec(memory_space=pl.ANY)] * len(operands)
    if scalar is not None:
        operands = (scalar, *operands)
        in_specs = [pl.BlockSpec(memory_space=pltpu.SMEM), *in_specs]
    return pl.pallas_call(
        body,
        out_shape=outs,
        in_specs=in_specs,
        out_specs=[pl.BlockSpec(memory_space=pl.ANY)] * len(outs),
        scratch_shapes=[*scratch, pltpu.SemaphoreType.DMA((copies,))],
        compiler_params=pltpu.CompilerParams(vmem_limit_bytes=56 * MIB),
        cost_estimate=pl.CostEstimate(flops=flops, bytes_accessed=moved, transcendentals=0),
    )(*operands)


def shape(rows, columns, dtype):
    return jax.ShapeDtypeStruct((rows, columns), dtype)


def pieces(value):
    first = narrow(value)
    value = value - first.astype(jnp.float32)
    second = narrow(value)
    return first, second, narrow(value - second.astype(jnp.float32))


EXTRA = 16


def both_ways(number, blocks, weights, me, before=None):
    bf16, f32 = jnp.bfloat16, jnp.float32
    count, width = len(blocks), blocks[0].shape[1]
    units, last = weights[0][0].shape[1], before is not None
    tok_count = (blocks[0].shape[0] - (0 if last else EXTRA)) // 2
    every, size = count * tok_count, 2 * tok_count
    lanes = 128
    back = size + (EXTRA if last else 0)

    def body(me_ref, *refs):
        b_refs, w_refs, refs = refs[:count], refs[count : count + 6], refs[count + 6 :]
        before_refs, refs = (refs[:2], refs[2:]) if last else ((), refs)
        q_refs, refs = refs[:count], refs[count:]
        weighted_ref, factor_ref, refs = refs[0], refs[1], refs[2:]
        after_refs, refs = ((), refs) if last else (refs[:2], refs[2:])
        wide_w, down_w, refs = refs[0], refs[1], refs[2:]
        x_buf, c_buf, y_buf, g_buf, weighted_buf, factor_buf, refs = *refs[:6], refs[6:]
        share_buf, inner_buf, wide_buf, extra_buf, sems = refs
        fetch = Fetch(sems)
        w_bufs = []
        for e in range(2):
            for i in (2 * e, 2 * e + 1):
                w_bufs.append(wide_w.at[:, pl.ds(i * units, units)])
            w_bufs.append(down_w.at[pl.ds(e * units, units)])
        me = me_ref[0]
        low = lax.rem(me, 8)
        for b in range(count):
            at = pl.ds(b * tok_count, tok_count)
            fetch.start(("x", b), b_refs[b].at[pl.ds(0, tok_count)], x_buf.at[at])
            if b == 0:
                fetch.start(("w", 0), w_refs[0], w_bufs[0])
        if last:
            fetch.start("share", before_refs[0], share_buf)
            fetch.start("inner", before_refs[1], inner_buf)
        else:
            for b in range(count):
                fetch.start(("s", b), b_refs[b].at[pl.ds(size, EXTRA)], extra_buf.at[b])
        for i in (1, 2):
            fetch.start(("w", i), w_refs[i], w_bufs[i])
        for b in range(count):
            at = pl.ds(b * tok_count, tok_count)
            fetch.start(("c", b), b_refs[b].at[pl.ds(tok_count, tok_count)], c_buf.at[at])
        for i in (3, 4, 5):
            fetch.start(("w", i), w_refs[i], w_bufs[i])

        def place(e):
            number = lax.rem(low + e, 2) + low - lax.rem(low, 2)
            return pl.ds(pl.multiple_of(number * lanes, lanes), lanes)

        upper = me >= 8
        if last:
            fetch.wait("share", "inner")
        else:
            inner_buf[...] = jnp.zeros((lanes, lanes), f32)
            share_buf[...] = jnp.zeros((lanes, lanes), f32)
            for b in range(count):
                fetch.wait(("s", b))
                wide_buf[b] = extra_buf[b].astype(f32)
            for e in range(2):
                for b in range(count):
                    tile = wide_buf[b, :, place(e)]
                    sums = [tile[r : r + 1] + tile[r + 2 : r + 3] + tile[r + 4 : r + 5] for r in (0, 1)]
                    row = e * count + b
                    share_buf[row : row + 1, :] = jnp.where(upper, sums[1], sums[0])
            share_buf[...] = share_buf[...].T

        half = slice(number * tok_count, (number + 1) * tok_count)
        fetch.wait(*[("x", b) for b in range(count)])
        x = x_buf[...]
        for e in range(2):
            columns = slice(e * units, (e + 1) * units)
            fetch.wait(("w", 3 * e))
            gate = dot(x, wide_w[:, 2 * e * units : (2 * e + 1) * units], ((1,), (0,)))
            fetch.wait(("w", 3 * e + 1))
            up = dot(x, wide_w[:, (2 * e + 1) * units : (2 * e + 2) * units], ((1,), (0,)))
            fetch.wait(("w", 3 * e + 2))
            if e == 0:
                fetch.wait(*[("c", b) for b in range(count)])
            plain = dot(c_buf[...], down_w[columns, :], ((1,), (1,)))
            sigma = jax.nn.sigmoid(gate)
            silu_val = gate * sigma
            hidden = silu_val * up
            part = [share_buf[half, e * count + b : e * count + b + 1] for b in range(count)]
            part = jnp.concatenate(part, axis=0)
            weighted_buf[:, columns] = (part * hidden).astype(bf16)
            inner = jnp.sum(hidden * plain, axis=1, keepdims=True)
            for b in range(count):
                value = inner[b * tok_count : (b + 1) * tok_count]
                inner_buf[half, e * count + b : e * count + b + 1] = value
            grad_hidden = part * plain
            grad_gate = (grad_hidden * up * (sigma * (1.0 + gate * (1.0 - sigma)))).astype(bf16)
            grad_up = (grad_hidden * silu_val).astype(bf16)
            factor_buf[:, 2 * e * units : (2 * e + 1) * units] = grad_gate
            factor_buf[:, (2 * e + 1) * units : (2 * e + 2) * units] = grad_up
        fetch.start("weighted", weighted_buf, weighted_ref)
        fetch.start("factor", factor_buf, factor_ref)
        y_buf[...] = dot(weighted_buf[...], down_w[...], ((1,), (0,))).astype(bf16)
        for b in range(count):
            at = pl.ds(b * tok_count, tok_count)
            fetch.start(("y", b), y_buf.at[at], q_refs[b].at[pl.ds(0, tok_count)])
        g_buf[...] = dot(factor_buf[...], wide_w[...], ((1,), (1,))).astype(bf16)
        for b in range(count):
            at = pl.ds(b * tok_count, tok_count)
            fetch.start(("g", b), g_buf.at[at], q_refs[b].at[pl.ds(tok_count, tok_count)])
        if last:
            wide_buf[...] = jnp.zeros((count, EXTRA, width), f32)
            inner_buf[...] = inner_buf[...].T
            for e in range(2):
                for b in range(count):
                    row = e * count + b
                    value, lines = inner_buf[row : row + 1, :], []
                    for _ in range(3):
                        piece = value.astype(bf16).astype(f32)
                        lines += [jnp.where(upper, 0.0, piece), jnp.where(upper, piece, 0.0)]
                        value = value - piece
                    lines += [jnp.zeros((2, lanes), f32)]
                    wide_buf[b, 0:8, place(e)] = jnp.concatenate(lines, axis=0)
            for b in range(count):
                extra_buf[b] = wide_buf[b].astype(bf16)
                fetch.start(("i", b), extra_buf.at[b], q_refs[b].at[pl.ds(size, EXTRA)])
        else:
            fetch.start("share", share_buf, after_refs[0])
            fetch.start("inner", inner_buf, after_refs[1])
        fetch.wait_all()

    outs = [shape(back, width, bf16)] * count
    outs += [shape(every, 2 * units, bf16), shape(every, 4 * units, bf16)]
    small = shape(lanes, lanes, f32)
    operands = (*blocks, *weights[0], *weights[1])
    if last:
        operands += before
    else:
        outs += [small, small]
    scratch = [pltpu.VMEM((width, 4 * units), bf16), pltpu.VMEM((2 * units, width), bf16)]
    scratch += [pltpu.VMEM((every, width), bf16)] * 4
    scratch += [pltpu.VMEM((every, 2 * units), bf16), pltpu.VMEM((every, 4 * units), bf16)]
    scratch += [pltpu.VMEM(small.shape, f32)] * 2
    scratch += [pltpu.VMEM((count, EXTRA, width), f32), pltpu.VMEM((count, EXTRA, width), bf16)]
    flops = 24 * every * width * units
    copies = 5 * count + 6 + 2 + 2
    outs = kernel(body, outs, scratch, copies, flops, *operands, scalar=me)
    return outs[:count], outs[count:]


def weight_grads(expert, blocks, factors, away=None):
    bf16 = jnp.bfloat16
    parts, count, width = len(blocks), len(blocks[0]), blocks[0][0].shape[1]
    each = factors[0][0].shape[0]
    tok_count, every, units = each // count, each * parts, factors[0][0].shape[1] // 2
    extra = 0 if away is None else 1

    def body(*refs):
        b_refs, refs = refs[: parts * count], refs[parts * count :]
        f_refs, refs = refs[: 2 * parts], refs[2 * parts :]
        away_refs, out_refs, refs = refs[:extra], refs[extra : 3 * extra + 1], refs[3 * extra + 1 :]
        x_buf, c_buf, weighted_buf, factor_buf, *bufs, sems = refs
        away_bufs, out_bufs = bufs[:extra], bufs[extra:]
        fetch = Fetch(sems)
        names = range(parts * count)
        for i in names:
            at = pl.ds(i * tok_count, tok_count)
            fetch.start(("x", i), b_refs[i].at[pl.ds(0, tok_count)], x_buf.at[at])
        for p in range(parts):
            at = pl.ds(p * each, each)
            lanes = pl.ds(2 * expert * units, 2 * units)
            fetch.start(("f", p), f_refs[2 * p + 1].at[:, lanes], factor_buf.at[at])
        if extra:
            fetch.start("away", away_refs[0], away_bufs[0])
        for p in range(parts):
            at = pl.ds(p * each, each)
            lanes = pl.ds(expert * units, units)
            fetch.start(("w", p), f_refs[2 * p].at[:, lanes], weighted_buf.at[at])
        for i in names:
            at = pl.ds(i * tok_count, tok_count)
            fetch.start(("c", i), b_refs[i].at[pl.ds(tok_count, tok_count)], c_buf.at[at])
        fetch.wait(*[("x", i) for i in names], *[("f", p) for p in range(parts)])
        for number in range(3):
            if number < 2:
                left, right = x_buf, factor_buf[:, number * units : (number + 1) * units]
                columns, into = slice(number * units, (number + 1) * units), slice(0, width)
            else:
                fetch.wait(*[("c", i) for i in names], *[("w", p) for p in range(parts)])
                left, right = weighted_buf, c_buf[...]
                columns, into = slice(0, width), slice(width, width + units)
            for start in range(0, into.stop - into.start, units):
                value = dot(left[:, start : start + units], right, ((0,), (0,)))
                at = slice(into.start + start, into.start + start + units)
                if not extra:
                    out_bufs[0][at, columns] = value.astype(bf16)
                else:
                    fetch.wait("away")
                    value = value + away_bufs[0][at, columns].astype(jnp.float32)
                    out_bufs[number][start : start + units, :] = value.astype(bf16)
                    block = out_bufs[number].at[start : start + units]
                    target = out_refs[number].at[start : start + units]
                    fetch.start(("out", number, start), block, target)
            if not extra and number:
                at = pl.ds(into.start, into.stop - into.start)
                fetch.start(("out", number), out_bufs[0].at[at], out_refs[0].at[at])
        fetch.wait_all()

    flops = 6 * every * width * units
    operands = (*[b for part in blocks for b in part], *[f for part in factors for f in part])
    scratch = [pltpu.VMEM((every, width), bf16)] * 2
    scratch += [pltpu.VMEM((every, units), bf16), pltpu.VMEM((every, 2 * units), bf16)]
    packed = shape(width + units, width, bf16)
    if away is None:
        outs = [packed]
        scratch += [pltpu.VMEM(packed.shape, bf16)]
    else:
        operands += (away,)
        outs = [shape(width, units, bf16)] * 2 + [shape(units, width, bf16)]
        scratch += [pltpu.VMEM(v.shape, bf16) for v in (packed, *outs)]
    copies = 2 * parts * count + 2 * parts + 1 + 2 * -(-width // units) + 1
    outs = kernel(body, outs, scratch, copies, flops, *operands)
    return outs if extra else outs[0]


def paired(latent_in, routes, combine_weights, cotangent, w_gate, w_up, w_down):
    f32 = jnp.float32
    devices_ep, tok_count, width = lax.axis_size("ep"), *latent_in.shape
    me = lax.axis_index("ep")
    mid = tok_count // 2
    experts = jnp.arange(devices_ep, dtype=jnp.int32)
    own = (w_gate[0], w_up[0], w_down[0])

    chosen = routes[None, :, :] == experts[:, None, None]
    share = jnp.sum(jnp.where(chosen, combine_weights[None, :, :], 0.0), axis=2)
    lines = jnp.stack(pieces(share)).reshape(-1, width)
    lines = jnp.pad(lines, ((0, EXTRA - lines.shape[0]), (0, 0)))
    a0 = jnp.concatenate([latent_in[:mid], cotangent[:mid], lines], axis=0)
    b0 = jnp.concatenate([latent_in[mid:], cotangent[mid:]], axis=0)
    gate_w, up_w, down_w = [swap(w, CORE) for w in own]
    a0, b0, gate_w, up_w, down_w, own = fence(a0, b0, gate_w, up_w, down_w, own)

    a2, a4, b4, a1 = swap(a0, FAR), swap(a0, SIDE), swap(b0, SIDE), swap(a0, NEAR)
    a2, a1, a4, b4, b0 = fence(a2, a1, a4, b4, b0)
    a5, a6, a3, b2 = swap(a1, SIDE), swap(a2, SIDE), swap(a2, NEAR), swap(b0, FAR)
    (a3,) = fence(a3)
    a7 = swap(a3, SIDE)
    b2, a5, a6 = fence(b2, a5, a6)
    b6, b1, b3 = swap(b2, SIDE), swap(b0, NEAR), swap(b2, NEAR)
    a7, b1, b6 = fence(a7, b1, b6)
    b5, b7 = swap(b1, SIDE), swap(b6, NEAR)
    weights, me = (own, (gate_w, up_w, down_w)), me.astype(jnp.int32).reshape(1)
    a = [a0, a1, a2, a3, a4, a5, a6, a7]
    q, (*a_factors, shares, inners) = both_ways(0, a, weights, me)
    q, shares, inners, b5, b7 = fence(q, shares, inners, b5, b7)
    q5, q7, q3, q4 = swap(q[5], SIDE), swap(q[7], NEAR), swap(q[3], NEAR), swap(q[4], SIDE)
    b = [b0, b1, b2, b3, b4, b5, b6, b7]
    p, b_factors = both_ways(1, b, weights, me, (shares, inners))
    q5, q7, q3, q4, p, q, b_factors = fence(q5, q7, q3, q4, p, q, b_factors)
    factors = (a_factors, b_factors)
    q6, q2, q1 = narrow(added(q[6], q7)), added(q[2], q3), narrow(added(q[1], q5))
    q6, q2, q1, p, q = fence(q6, q2, q1, p, q)
    q6, p7, q1 = swap(q6, SIDE), swap(p[7], SIDE), swap(q1, NEAR)
    away = weight_grads(1, (a, b), factors)
    q6, p7, q1, q2, away, p, q = fence(q6, p7, q1, q2, away, p, q)
    q2, p3 = narrow(q2 + q6.astype(f32)), narrow(added(p[3], p7))
    q2, p3, p, q, away = fence(q2, p3, p, q, away)
    p6, p5, q2, p3 = swap(p[6], SIDE), swap(p[5], SIDE), swap(q2, FAR), swap(p3, NEAR)
    away = swap(away, CORE)
    q2, p6, p5, p3, away, p, q = fence(q2, p6, p5, p3, away, p, q)
    p2, p1 = narrow(added(p[2], p6) + p3.astype(f32)), narrow(added(p[1], p5))
    p2, p1, p, q, away = fence(p2, p1, p, q, away)
    p4, p2, p1 = swap(p[4], SIDE), swap(p2, FAR), swap(p1, NEAR)
    grad_w = weight_grads(0, (a, b), factors, away)
    p2, p4, p1, grad_w = fence(p2, p4, p1, grad_w)

    q = added(q[0], q4) + added(q1, q2)
    p = added(p[0], p4) + added(p1, p2)
    combined = narrow(jnp.concatenate([q[:mid], p[:mid]], axis=0))
    grad_latent = narrow(jnp.concatenate([q[mid : 2 * mid], p[mid : 2 * mid]], axis=0))
    inner = p[2 * mid :].reshape(-1, devices_ep, tok_count)[:3].sum(axis=0)
    grad_combine = jnp.sum(jnp.where(chosen, inner[:, :, None], 0.0), axis=0)
    return (combined, grad_latent, grad_combine, *[v[None] for v in grad_w])


def local(latent_in, routes, combine_weights, cotangent, w_gate, w_up, w_down):
    plan = paired if w_gate.shape[0] == 1 and lax.axis_size("ep") == 2 * len(REACH) else exchanged
    return plan(latent_in, routes, combine_weights, cotangent, w_gate, w_up, w_down)


def solution(mesh):
    return jax.shard_map(
        local,
        mesh=mesh,
        in_specs=(
            P(("grp", "ep"), None),
            P(("grp", "ep"), None),
            P(("grp", "ep"), None),
            P(("grp", "ep"), None),
            P("ep", None, None),
            P("ep", None, None),
            P("ep", None, None),
        ),
        out_specs=(
            P(("grp", "ep"), None),
            P(("grp", "ep"), None),
            P(("grp", "ep"), None),
            P(("grp", "ep"), None, None),
            P(("grp", "ep"), None, None),
            P(("grp", "ep"), None, None),
        ),
        check_vma=False,
    )
```

```python
import jax
import jax.numpy as jnp
from jax import lax
from jax.experimental import pallas as pl
from jax.experimental.pallas import tpu as pltpu
from jax.sharding import PartitionSpec as P


def assign_slots(route_rows, expert_count):
    flat_ids = route_rows.reshape(-1)
    onehot = (flat_ids[:, None] == jnp.arange(expert_count, dtype=jnp.int32)[None, :]).astype(
        jnp.int32
    )
    ranks = jnp.cumsum(onehot, axis=0) - 1
    return (flat_ids, jnp.sum(onehot * ranks, axis=1))


def expert_forward(rows, gate_w, up_w, down_w):
    gate_pre = jnp.einsum("erl,elf->erf", rows, gate_w, preferred_element_type=jnp.float32)
    up_pre = jnp.einsum("erl,elf->erf", rows, up_w, preferred_element_type=jnp.float32)
    sigma = jax.nn.sigmoid(gate_pre)
    silu_val = gate_pre * sigma
    hidden = (silu_val * up_pre).astype(jnp.bfloat16)
    expert_out = jnp.einsum(
        "erf,efl->erl", hidden, down_w, preferred_element_type=jnp.float32
    ).astype(jnp.bfloat16)
    return (expert_out, (gate_pre, up_pre, sigma, silu_val, hidden))


def expert_backward(rows, grad_out, saved, gate_w, up_w, down_w):
    gate_pre, up_pre, sigma, silu_val, hidden = saved
    grad_down = jnp.einsum(
        "erf,erl->efl", hidden, grad_out, preferred_element_type=jnp.float32
    ).astype(jnp.bfloat16)
    grad_hidden = jnp.einsum("erl,efl->erf", grad_out, down_w, preferred_element_type=jnp.float32)
    grad_gate = (grad_hidden * up_pre * sigma * (1.0 + gate_pre * (1.0 - sigma))).astype(
        jnp.bfloat16
    )
    grad_up = (grad_hidden * silu_val).astype(jnp.bfloat16)
    grad_gw = jnp.einsum(
        "erl,erf->elf", rows, grad_gate, preferred_element_type=jnp.float32
    ).astype(jnp.bfloat16)
    grad_uw = jnp.einsum("erl,erf->elf", rows, grad_up, preferred_element_type=jnp.float32).astype(
        jnp.bfloat16
    )
    grad_rows = (
        jnp.einsum("erf,elf->erl", grad_gate, gate_w, preferred_element_type=jnp.float32)
        + jnp.einsum("erf,elf->erl", grad_up, up_w, preferred_element_type=jnp.float32)
    ).astype(jnp.bfloat16)
    return (grad_rows, grad_gw, grad_uw, grad_down)


def exchanged(latent_in, routes, combine_weights, cotangent, w_gate, w_up, w_down):
    devices_ep = lax.axis_size("ep")
    local_experts = w_gate.shape[0]
    expert_count = local_experts * devices_ep
    tok_count = latent_in.shape[0]
    top_count = routes.shape[1]
    width = latent_in.shape[1]
    capacity = tok_count * top_count * 3 // (2 * expert_count)
    expert_ids, slot_ids = assign_slots(routes, expert_count)
    position = expert_ids * capacity + slot_ids
    repeated = jnp.repeat(latent_in, top_count, axis=0)
    weighted = (combine_weights[:, :, None] * cotangent.astype(jnp.float32)[:, None, :]).astype(
        jnp.bfloat16
    )
    send_rows = jnp.zeros((expert_count * capacity, width), jnp.bfloat16).at[position].set(repeated)
    send_rows = send_rows.reshape(expert_count, capacity, width)
    send_cot = (
        jnp.zeros((expert_count * capacity, width), jnp.bfloat16)
        .at[position]
        .set(weighted.reshape(-1, width))
    )
    send_cot = send_cot.reshape(expert_count, capacity, width)

    def to_local(received):
        shaped = received.reshape(devices_ep, local_experts, capacity, width)
        return shaped.transpose(1, 0, 2, 3).reshape(local_experts, devices_ep * capacity, width)

    def to_home(local_rows):
        shaped = local_rows.reshape(local_experts, devices_ep, capacity, width)
        return shaped.transpose(1, 0, 2, 3).reshape(expert_count, capacity, width)

    got_rows = lax.all_to_all(send_rows, "ep", split_axis=0, concat_axis=0, tiled=True)
    rows_local = to_local(got_rows)
    expert_out, saved = expert_forward(rows_local, w_gate, w_up, w_down)
    back_out = lax.all_to_all(to_home(expert_out), "ep", split_axis=0, concat_axis=0, tiled=True)
    got_cot = lax.all_to_all(send_cot, "ep", split_axis=0, concat_axis=0, tiled=True)
    grad_rows, grad_gw, grad_uw, grad_down = expert_backward(
        rows_local, to_local(got_cot), saved, w_gate, w_up, w_down
    )
    back_grad = lax.all_to_all(to_home(grad_rows), "ep", split_axis=0, concat_axis=0, tiled=True)
    out_rows = (
        back_out.reshape(-1, width)[position]
        .reshape(tok_count, top_count, width)
        .astype(jnp.float32)
    )
    grad_back = (
        back_grad.reshape(-1, width)[position]
        .reshape(tok_count, top_count, width)
        .astype(jnp.float32)
    )
    combined = jnp.sum(combine_weights[:, :, None] * out_rows, axis=1).astype(jnp.bfloat16)
    grad_combine = jnp.sum(cotangent.astype(jnp.float32)[:, None, :] * out_rows, axis=2)
    grad_latent = jnp.sum(grad_back, axis=1).astype(jnp.bfloat16)
    return (combined, grad_latent, grad_combine, grad_gw, grad_uw, grad_down)


def dot(a, b, dims):
    return lax.dot_general(a, b, (dims, ((), ())), preferred_element_type=jnp.float32)


def swap(value, bit):
    pairs = [(i, i ^ bit) for i in range(lax.axis_size("ep"))]
    return lax.ppermute(value, "ep", pairs)


CORE, SIDE, NEAR, FAR = 1, 2, 4, 8
REACH = (0, NEAR, FAR, NEAR | FAR, SIDE, SIDE | NEAR, SIDE | FAR, SIDE | NEAR | FAR)


def fence(*values):
    return lax.optimization_barrier(values)


def added(a, b):
    return a.astype(jnp.float32) + b.astype(jnp.float32)


def narrow(value):
    return value.astype(jnp.bfloat16)


MIB = 1 << 20


class Fetch:
    def __init__(self, sems):
        self.sems, self.waiting = sems, {}

    def start(self, name, source, target):
        copy = pltpu.make_async_copy(source, target, self.sems.at[len(self.waiting)])
        copy.start()
        self.waiting[name] = [copy, False]

    def wait(self, *names):
        for name in names:
            if not self.waiting[name][1]:
                self.waiting[name][0].wait()
                self.waiting[name][1] = True

    def wait_all(self):
        self.wait(*self.waiting)


def kernel(body, outs, scratch, copies, flops, *operands, scalar=None):
    moved = sum(v.size * v.dtype.itemsize for v in (*operands, *outs))
    in_specs = [pl.BlockSpec(memory_space=pl.ANY)] * len(operands)
    if scalar is not None:
        operands = (scalar, *operands)
        in_specs = [pl.BlockSpec(memory_space=pltpu.SMEM), *in_specs]
    return pl.pallas_call(
        body,
        out_shape=outs,
        in_specs=in_specs,
        out_specs=[pl.BlockSpec(memory_space=pl.ANY)] * len(outs),
        scratch_shapes=[*scratch, pltpu.SemaphoreType.DMA((copies,))],
        compiler_params=pltpu.CompilerParams(vmem_limit_bytes=56 * MIB),
        cost_estimate=pl.CostEstimate(flops=flops, bytes_accessed=moved, transcendentals=0),
    )(*operands)


def shape(rows, columns, dtype):
    return jax.ShapeDtypeStruct((rows, columns), dtype)


def pieces(value):
    first = narrow(value)
    value = value - first.astype(jnp.float32)
    second = narrow(value)
    return first, second, narrow(value - second.astype(jnp.float32))


EXTRA = 16


def both_ways(number, blocks, weights, me, before=None):
    bf16, f32 = jnp.bfloat16, jnp.float32
    count, width = len(blocks), blocks[0].shape[1]
    units, last = weights[0][0].shape[1], before is not None
    tok_count = (blocks[0].shape[0] - (0 if last else EXTRA)) // 2
    every, size = count * tok_count, 2 * tok_count
    lanes = 128
    back = size + (EXTRA if last else 0)
    layout = [[b] for b in range(count)] if last else [[0], [1], [2], [4], [5], [6], [7, 3]]
    place_of = {b: (i, j * back) for i, held in enumerate(layout) for j, b in enumerate(held)}

    def body(me_ref, *refs):
        b_refs, w_refs, refs = refs[:count], refs[count : count + 6], refs[count + 6 :]
        before_refs, refs = (refs[:2], refs[2:]) if last else ((), refs)
        q_refs, refs = refs[: len(layout)], refs[len(layout) :]
        weighted_ref, factor_ref, refs = refs[0], refs[1], refs[2:]
        after_refs, refs = ((), refs) if last else (refs[:2], refs[2:])
        wide_w, down_w, refs = refs[0], refs[1], refs[2:]
        x_buf, c_buf, y_buf, g_buf, weighted_buf, factor_buf, refs = *refs[:6], refs[6:]
        share_buf, inner_buf, wide_buf, extra_buf, sems = refs
        fetch = Fetch(sems)
        w_bufs = []
        for e in range(2):
            for i in (2 * e, 2 * e + 1):
                w_bufs.append(wide_w.at[:, pl.ds(i * units, units)])
            w_bufs.append(down_w.at[pl.ds(e * units, units)])
        me = me_ref[0]
        low = lax.rem(me, 8)
        for b in range(count):
            at = pl.ds(b * tok_count, tok_count)
            fetch.start(("x", b), b_refs[b].at[pl.ds(0, tok_count)], x_buf.at[at])
            if b == 0:
                fetch.start(("w", 0), w_refs[0], w_bufs[0])
        if last:
            fetch.start("share", before_refs[0], share_buf)
            fetch.start("inner", before_refs[1], inner_buf)
        else:
            for b in range(count):
                fetch.start(("s", b), b_refs[b].at[pl.ds(size, EXTRA)], extra_buf.at[b])
        for i in (1, 2):
            fetch.start(("w", i), w_refs[i], w_bufs[i])
        for b in range(count):
            at = pl.ds(b * tok_count, tok_count)
            fetch.start(("c", b), b_refs[b].at[pl.ds(tok_count, tok_count)], c_buf.at[at])
        for i in (3, 4, 5):
            fetch.start(("w", i), w_refs[i], w_bufs[i])

        def returned(b, first, rows):
            ref, offset = place_of[b]
            return q_refs[ref].at[pl.ds(offset + first, rows)]

        def place(e):
            number = lax.rem(low + e, 2) + low - lax.rem(low, 2)
            return pl.ds(pl.multiple_of(number * lanes, lanes), lanes)

        upper = me >= 8
        if last:
            fetch.wait("share", "inner")
        else:
            inner_buf[...] = jnp.zeros((lanes, lanes), f32)
            share_buf[...] = jnp.zeros((lanes, lanes), f32)
            for b in range(count):
                fetch.wait(("s", b))
                wide_buf[b] = extra_buf[b].astype(f32)
            for e in range(2):
                for b in range(count):
                    tile = wide_buf[b, :, place(e)]
                    sums = [tile[r : r + 1] + tile[r + 2 : r + 3] + tile[r + 4 : r + 5] for r in (0, 1)]
                    row = e * count + b
                    share_buf[row : row + 1, :] = jnp.where(upper, sums[1], sums[0])
            share_buf[...] = share_buf[...].T

        half = slice(number * tok_count, (number + 1) * tok_count)
        fetch.wait(*[("x", b) for b in range(count)])
        x = x_buf[...]
        for e in range(2):
            columns = slice(e * units, (e + 1) * units)
            fetch.wait(("w", 3 * e))
            gate = dot(x, wide_w[:, 2 * e * units : (2 * e + 1) * units], ((1,), (0,)))
            fetch.wait(("w", 3 * e + 1))
            up = dot(x, wide_w[:, (2 * e + 1) * units : (2 * e + 2) * units], ((1,), (0,)))
            fetch.wait(("w", 3 * e + 2))
            if e == 0:
                fetch.wait(*[("c", b) for b in range(count)])
            plain = dot(c_buf[...], down_w[columns, :], ((1,), (1,)))
            sigma = jax.nn.sigmoid(gate)
            silu_val = gate * sigma
            hidden = silu_val * up
            part = [share_buf[half, e * count + b : e * count + b + 1] for b in range(count)]
            part = jnp.concatenate(part, axis=0)
            weighted_buf[:, columns] = (part * hidden).astype(bf16)
            inner = jnp.sum(hidden * plain, axis=1, keepdims=True)
            for b in range(count):
                value = inner[b * tok_count : (b + 1) * tok_count]
                inner_buf[half, e * count + b : e * count + b + 1] = value
            grad_hidden = part * plain
            grad_gate = (grad_hidden * up * (sigma * (1.0 + gate * (1.0 - sigma)))).astype(bf16)
            grad_up = (grad_hidden * silu_val).astype(bf16)
            factor_buf[:, 2 * e * units : (2 * e + 1) * units] = grad_gate
            factor_buf[:, (2 * e + 1) * units : (2 * e + 2) * units] = grad_up
        fetch.start("weighted", weighted_buf, weighted_ref)
        fetch.start("factor", factor_buf, factor_ref)
        y_buf[...] = dot(weighted_buf[...], down_w[...], ((1,), (0,))).astype(bf16)
        for b in range(count):
            at = pl.ds(b * tok_count, tok_count)
            fetch.start(("y", b), y_buf.at[at], returned(b, 0, tok_count))
        g_buf[...] = dot(factor_buf[...], wide_w[...], ((1,), (1,))).astype(bf16)
        for b in range(count):
            at = pl.ds(b * tok_count, tok_count)
            fetch.start(("g", b), g_buf.at[at], returned(b, tok_count, tok_count))
        if last:
            wide_buf[...] = jnp.zeros((count, EXTRA, width), f32)
            inner_buf[...] = inner_buf[...].T
            for e in range(2):
                for b in range(count):
                    row = e * count + b
                    value, lines = inner_buf[row : row + 1, :], []
                    for _ in range(3):
                        piece = value.astype(bf16).astype(f32)
                        lines += [jnp.where(upper, 0.0, piece), jnp.where(upper, piece, 0.0)]
                        value = value - piece
                    lines += [jnp.zeros((2, lanes), f32)]
                    wide_buf[b, 0:8, place(e)] = jnp.concatenate(lines, axis=0)
            for b in range(count):
                extra_buf[b] = wide_buf[b].astype(bf16)
                fetch.start(("i", b), extra_buf.at[b], returned(b, size, EXTRA))
        else:
            fetch.start("share", share_buf, after_refs[0])
            fetch.start("inner", inner_buf, after_refs[1])
        fetch.wait_all()

    outs = [shape(len(held) * back, width, bf16) for held in layout]
    outs += [shape(every, 2 * units, bf16), shape(every, 4 * units, bf16)]
    small = shape(lanes, lanes, f32)
    operands = (*blocks, *weights[0], *weights[1])
    if last:
        operands += before
    else:
        outs += [small, small]
    scratch = [pltpu.VMEM((width, 4 * units), bf16), pltpu.VMEM((2 * units, width), bf16)]
    scratch += [pltpu.VMEM((every, width), bf16)] * 4
    scratch += [pltpu.VMEM((every, 2 * units), bf16), pltpu.VMEM((every, 4 * units), bf16)]
    scratch += [pltpu.VMEM(small.shape, f32)] * 2
    scratch += [pltpu.VMEM((count, EXTRA, width), f32), pltpu.VMEM((count, EXTRA, width), bf16)]
    flops = 24 * every * width * units
    copies = 5 * count + 6 + 2 + 2
    outs = kernel(body, outs, scratch, copies, flops, *operands, scalar=me)
    return outs[: len(layout)], outs[len(layout) :]


def weight_grads(expert, blocks, factors, away=None):
    bf16 = jnp.bfloat16
    parts, count, width = len(blocks), len(blocks[0]), blocks[0][0].shape[1]
    each = factors[0][0].shape[0]
    tok_count, every, units = each // count, each * parts, factors[0][0].shape[1] // 2
    extra = 0 if away is None else 1

    def body(*refs):
        b_refs, refs = refs[: parts * count], refs[parts * count :]
        f_refs, refs = refs[: 2 * parts], refs[2 * parts :]
        away_refs, out_refs, refs = refs[:extra], refs[extra : 3 * extra + 1], refs[3 * extra + 1 :]
        x_buf, c_buf, weighted_buf, factor_buf, *bufs, sems = refs
        away_bufs, out_bufs = bufs[:extra], bufs[extra:]
        fetch = Fetch(sems)
        names = range(parts * count)
        for i in names:
            at = pl.ds(i * tok_count, tok_count)
            fetch.start(("x", i), b_refs[i].at[pl.ds(0, tok_count)], x_buf.at[at])
        for p in range(parts):
            at = pl.ds(p * each, each)
            lanes = pl.ds(2 * expert * units, 2 * units)
            fetch.start(("f", p), f_refs[2 * p + 1].at[:, lanes], factor_buf.at[at])
        if extra:
            fetch.start("away", away_refs[0], away_bufs[0])
        for p in range(parts):
            at = pl.ds(p * each, each)
            lanes = pl.ds(expert * units, units)
            fetch.start(("w", p), f_refs[2 * p].at[:, lanes], weighted_buf.at[at])
        for i in names:
            at = pl.ds(i * tok_count, tok_count)
            fetch.start(("c", i), b_refs[i].at[pl.ds(tok_count, tok_count)], c_buf.at[at])
        fetch.wait(*[("x", i) for i in names], *[("f", p) for p in range(parts)])
        for number in range(3):
            if number < 2:
                left, right = x_buf, factor_buf[:, number * units : (number + 1) * units]
                columns, into = slice(number * units, (number + 1) * units), slice(0, width)
            else:
                fetch.wait(*[("c", i) for i in names], *[("w", p) for p in range(parts)])
                left, right = weighted_buf, c_buf[...]
                columns, into = slice(0, width), slice(width, width + units)
            for start in range(0, into.stop - into.start, units):
                value = dot(left[:, start : start + units], right, ((0,), (0,)))
                at = slice(into.start + start, into.start + start + units)
                if not extra:
                    out_bufs[0][at, columns] = value.astype(bf16)
                else:
                    fetch.wait("away")
                    value = value + away_bufs[0][at, columns].astype(jnp.float32)
                    out_bufs[number][start : start + units, :] = value.astype(bf16)
                    block = out_bufs[number].at[start : start + units]
                    target = out_refs[number].at[start : start + units]
                    fetch.start(("out", number, start), block, target)
            if not extra and number:
                at = pl.ds(into.start, into.stop - into.start)
                fetch.start(("out", number), out_bufs[0].at[at], out_refs[0].at[at])
        fetch.wait_all()

    flops = 6 * every * width * units
    operands = (*[b for part in blocks for b in part], *[f for part in factors for f in part])
    scratch = [pltpu.VMEM((every, width), bf16)] * 2
    scratch += [pltpu.VMEM((every, units), bf16), pltpu.VMEM((every, 2 * units), bf16)]
    packed = shape(width + units, width, bf16)
    if away is None:
        outs = [packed]
        scratch += [pltpu.VMEM(packed.shape, bf16)]
    else:
        operands += (away,)
        outs = [shape(width, units, bf16)] * 2 + [shape(units, width, bf16)]
        scratch += [pltpu.VMEM(v.shape, bf16) for v in (packed, *outs)]
    copies = 2 * parts * count + 2 * parts + 1 + 2 * -(-width // units) + 1
    outs = kernel(body, outs, scratch, copies, flops, *operands)
    return outs if extra else outs[0]


def paired(latent_in, routes, combine_weights, cotangent, w_gate, w_up, w_down):
    f32 = jnp.float32
    devices_ep, tok_count, width = lax.axis_size("ep"), *latent_in.shape
    me = lax.axis_index("ep")
    mid = tok_count // 2
    experts = jnp.arange(devices_ep, dtype=jnp.int32)
    own = (w_gate[0], w_up[0], w_down[0])

    chosen = routes[None, :, :] == experts[:, None, None]
    share = jnp.sum(jnp.where(chosen, combine_weights[None, :, :], 0.0), axis=2)
    lines = jnp.stack(pieces(share)).reshape(-1, width)
    lines = jnp.pad(lines, ((0, EXTRA - lines.shape[0]), (0, 0)))
    a0 = jnp.concatenate([latent_in[:mid], cotangent[:mid], lines], axis=0)
    b0 = jnp.concatenate([latent_in[mid:], cotangent[mid:]], axis=0)
    gate_w = swap(own[0], CORE)
    a0, b0, gate_w, own = fence(a0, b0, gate_w, own)

    a2, a4, b4, a1 = swap(a0, FAR), swap(a0, SIDE), swap(b0, SIDE), swap(a0, NEAR)
    up_w = swap(own[1], CORE)
    a1, a4, a2, b4, up_w, b0, own = fence(a1, a4, a2, b4, up_w, b0, own)
    a5, a6, a3, b2 = swap(a1, SIDE), swap(a2, SIDE), swap(a2, NEAR), swap(b0, FAR)
    down_w = swap(own[2], CORE)
    (a3,) = fence(a3)
    a7 = swap(a3, SIDE)
    b2, a5, a6 = fence(b2, a5, a6)
    b6, b1, b3 = swap(b2, SIDE), swap(b0, NEAR), swap(b2, NEAR)
    a7, b1, b6 = fence(a7, b1, b6)
    b5, b7 = swap(b1, SIDE), swap(b6, NEAR)
    weights, me = (own, (gate_w, up_w, down_w)), me.astype(jnp.int32).reshape(1)
    a = [a0, a1, a2, a3, a4, a5, a6, a7]
    q, (*a_factors, shares, inners) = both_ways(0, a, weights, me)
    q0, q1, q2, q4, q5, q6, q73 = q
    q73, q5, shares, inners, b5, b7 = fence(q73, q5, shares, inners, b5, b7)
    r73, r5 = swap(q73, NEAR), swap(q5, SIDE)
    b = [b0, b1, b2, b3, b4, b5, b6, b7]
    p, b_factors = both_ways(1, b, weights, me, (shares, inners))
    p0, p1, p2, p3, p4, p5, p6, p7 = p
    r73, r5, q6, q4, p7, p6, p5, p4, b_factors = fence(r73, r5, q6, q4, p7, p6, p5, p4, b_factors)
    factors, size = (a_factors, b_factors), q6.shape[0]
    q6, q2, q1 = narrow(added(q6, r73[:size])), added(q2, r73[size:]), narrow(added(q1, r5))
    q6, p7, q1 = fence(q6, p7, q1)
    r6, r7, q1 = swap(q6, SIDE), swap(p7, SIDE), swap(q1, NEAR)
    away = weight_grads(1, (a, b), factors)
    r6, r7, q1, away, p6, p5 = fence(r6, r7, q1, away, p6, p5)
    q2, p3 = narrow(q2 + r6.astype(f32)), narrow(added(p3, r7))
    q2, p3, p6, p5, away = fence(q2, p3, p6, p5, away)
    q2, r6, r5, p3, away = (
        swap(q2, FAR), swap(p6, SIDE), swap(p5, SIDE), swap(p3, NEAR), swap(away, CORE),
    )
    q2, r6, r5, p3, away, q4, p4 = fence(q2, r6, r5, p3, away, q4, p4)
    p2, p1 = narrow(added(p2, r6) + p3.astype(f32)), narrow(added(p1, r5))
    p2, p1, p4, q4, away = fence(p2, p1, p4, q4, away)
    p2, p4, q4, p1 = swap(p2, FAR), swap(p4, SIDE), swap(q4, SIDE), swap(p1, NEAR)
    grad_w = weight_grads(0, (a, b), factors, away)
    p2, p4, q4, p1, grad_w = fence(p2, p4, q4, p1, grad_w)

    q = added(q0, q4) + added(q1, q2)
    p = added(p0, p4) + added(p1, p2)
    combined = narrow(jnp.concatenate([q[:mid], p[:mid]], axis=0))
    grad_latent = narrow(jnp.concatenate([q[mid : 2 * mid], p[mid : 2 * mid]], axis=0))
    inner = p[2 * mid :].reshape(-1, devices_ep, tok_count)[:3].sum(axis=0)
    grad_combine = jnp.sum(jnp.where(chosen, inner[:, :, None], 0.0), axis=0)
    return (combined, grad_latent, grad_combine, *[v[None] for v in grad_w])


def local(latent_in, routes, combine_weights, cotangent, w_gate, w_up, w_down):
    plan = paired if w_gate.shape[0] == 1 and lax.axis_size("ep") == 2 * len(REACH) else exchanged
    return plan(latent_in, routes, combine_weights, cotangent, w_gate, w_up, w_down)


def solution(mesh):
    return jax.shard_map(
        local,
        mesh=mesh,
        in_specs=(
            P(("grp", "ep"), None),
            P(("grp", "ep"), None),
            P(("grp", "ep"), None),
            P(("grp", "ep"), None),
            P("ep", None, None),
            P("ep", None, None),
            P("ep", None, None),
        ),
        out_specs=(
            P(("grp", "ep"), None),
            P(("grp", "ep"), None),
            P(("grp", "ep"), None),
            P(("grp", "ep"), None, None),
            P(("grp", "ep"), None, None),
            P(("grp", "ep"), None, None),
        ),
        check_vma=False,
    )
```

```python
import jax
import jax.numpy as jnp
from jax import lax
from jax.experimental import pallas as pl
from jax.experimental.pallas import tpu as pltpu
from jax.sharding import PartitionSpec as P


def assign_slots(route_rows, expert_count):
    flat_ids = route_rows.reshape(-1)
    onehot = (flat_ids[:, None] == jnp.arange(expert_count, dtype=jnp.int32)[None, :]).astype(
        jnp.int32
    )
    ranks = jnp.cumsum(onehot, axis=0) - 1
    return (flat_ids, jnp.sum(onehot * ranks, axis=1))


def expert_forward(rows, gate_w, up_w, down_w):
    gate_pre = jnp.einsum("erl,elf->erf", rows, gate_w, preferred_element_type=jnp.float32)
    up_pre = jnp.einsum("erl,elf->erf", rows, up_w, preferred_element_type=jnp.float32)
    sigma = jax.nn.sigmoid(gate_pre)
    silu_val = gate_pre * sigma
    hidden = (silu_val * up_pre).astype(jnp.bfloat16)
    expert_out = jnp.einsum(
        "erf,efl->erl", hidden, down_w, preferred_element_type=jnp.float32
    ).astype(jnp.bfloat16)
    return (expert_out, (gate_pre, up_pre, sigma, silu_val, hidden))


def expert_backward(rows, grad_out, saved, gate_w, up_w, down_w):
    gate_pre, up_pre, sigma, silu_val, hidden = saved
    grad_down = jnp.einsum(
        "erf,erl->efl", hidden, grad_out, preferred_element_type=jnp.float32
    ).astype(jnp.bfloat16)
    grad_hidden = jnp.einsum("erl,efl->erf", grad_out, down_w, preferred_element_type=jnp.float32)
    grad_gate = (grad_hidden * up_pre * sigma * (1.0 + gate_pre * (1.0 - sigma))).astype(
        jnp.bfloat16
    )
    grad_up = (grad_hidden * silu_val).astype(jnp.bfloat16)
    grad_gw = jnp.einsum(
        "erl,erf->elf", rows, grad_gate, preferred_element_type=jnp.float32
    ).astype(jnp.bfloat16)
    grad_uw = jnp.einsum("erl,erf->elf", rows, grad_up, preferred_element_type=jnp.float32).astype(
        jnp.bfloat16
    )
    grad_rows = (
        jnp.einsum("erf,elf->erl", grad_gate, gate_w, preferred_element_type=jnp.float32)
        + jnp.einsum("erf,elf->erl", grad_up, up_w, preferred_element_type=jnp.float32)
    ).astype(jnp.bfloat16)
    return (grad_rows, grad_gw, grad_uw, grad_down)


def exchanged(latent_in, routes, combine_weights, cotangent, w_gate, w_up, w_down):
    devices_ep = lax.axis_size("ep")
    local_experts = w_gate.shape[0]
    expert_count = local_experts * devices_ep
    tok_count = latent_in.shape[0]
    top_count = routes.shape[1]
    width = latent_in.shape[1]
    capacity = tok_count * top_count * 3 // (2 * expert_count)
    expert_ids, slot_ids = assign_slots(routes, expert_count)
    position = expert_ids * capacity + slot_ids
    repeated = jnp.repeat(latent_in, top_count, axis=0)
    weighted = (combine_weights[:, :, None] * cotangent.astype(jnp.float32)[:, None, :]).astype(
        jnp.bfloat16
    )
    send_rows = jnp.zeros((expert_count * capacity, width), jnp.bfloat16).at[position].set(repeated)
    send_rows = send_rows.reshape(expert_count, capacity, width)
    send_cot = (
        jnp.zeros((expert_count * capacity, width), jnp.bfloat16)
        .at[position]
        .set(weighted.reshape(-1, width))
    )
    send_cot = send_cot.reshape(expert_count, capacity, width)

    def to_local(received):
        shaped = received.reshape(devices_ep, local_experts, capacity, width)
        return shaped.transpose(1, 0, 2, 3).reshape(local_experts, devices_ep * capacity, width)

    def to_home(local_rows):
        shaped = local_rows.reshape(local_experts, devices_ep, capacity, width)
        return shaped.transpose(1, 0, 2, 3).reshape(expert_count, capacity, width)

    got_rows = lax.all_to_all(send_rows, "ep", split_axis=0, concat_axis=0, tiled=True)
    rows_local = to_local(got_rows)
    expert_out, saved = expert_forward(rows_local, w_gate, w_up, w_down)
    back_out = lax.all_to_all(to_home(expert_out), "ep", split_axis=0, concat_axis=0, tiled=True)
    got_cot = lax.all_to_all(send_cot, "ep", split_axis=0, concat_axis=0, tiled=True)
    grad_rows, grad_gw, grad_uw, grad_down = expert_backward(
        rows_local, to_local(got_cot), saved, w_gate, w_up, w_down
    )
    back_grad = lax.all_to_all(to_home(grad_rows), "ep", split_axis=0, concat_axis=0, tiled=True)
    out_rows = (
        back_out.reshape(-1, width)[position]
        .reshape(tok_count, top_count, width)
        .astype(jnp.float32)
    )
    grad_back = (
        back_grad.reshape(-1, width)[position]
        .reshape(tok_count, top_count, width)
        .astype(jnp.float32)
    )
    combined = jnp.sum(combine_weights[:, :, None] * out_rows, axis=1).astype(jnp.bfloat16)
    grad_combine = jnp.sum(cotangent.astype(jnp.float32)[:, None, :] * out_rows, axis=2)
    grad_latent = jnp.sum(grad_back, axis=1).astype(jnp.bfloat16)
    return (combined, grad_latent, grad_combine, grad_gw, grad_uw, grad_down)


def dot(a, b, dims):
    return lax.dot_general(a, b, (dims, ((), ())), preferred_element_type=jnp.float32)


def swap(value, bit):
    pairs = [(i, i ^ bit) for i in range(lax.axis_size("ep"))]
    return lax.ppermute(value, "ep", pairs)


CORE, SIDE, NEAR, FAR = 1, 2, 4, 8
REACH = (0, NEAR, FAR, NEAR | FAR, SIDE, SIDE | NEAR, SIDE | FAR, SIDE | NEAR | FAR)


def fence(*values):
    return lax.optimization_barrier(values)


def added(a, b):
    return a.astype(jnp.float32) + b.astype(jnp.float32)


def narrow(value):
    return value.astype(jnp.bfloat16)


MIB = 1 << 20


class Fetch:
    def __init__(self, sems):
        self.sems, self.waiting = sems, {}

    def start(self, name, source, target):
        copy = pltpu.make_async_copy(source, target, self.sems.at[len(self.waiting)])
        copy.start()
        self.waiting[name] = [copy, False]

    def wait(self, *names):
        for name in names:
            if not self.waiting[name][1]:
                self.waiting[name][0].wait()
                self.waiting[name][1] = True

    def wait_all(self):
        self.wait(*self.waiting)


def kernel(body, outs, scratch, copies, flops, *operands, scalar=None):
    moved = sum(v.size * v.dtype.itemsize for v in (*operands, *outs))
    in_specs = [pl.BlockSpec(memory_space=pl.ANY)] * len(operands)
    if scalar is not None:
        operands = (scalar, *operands)
        in_specs = [pl.BlockSpec(memory_space=pltpu.SMEM), *in_specs]
    return pl.pallas_call(
        body,
        out_shape=outs,
        in_specs=in_specs,
        out_specs=[pl.BlockSpec(memory_space=pl.ANY)] * len(outs),
        scratch_shapes=[*scratch, pltpu.SemaphoreType.DMA((copies,))],
        compiler_params=pltpu.CompilerParams(vmem_limit_bytes=56 * MIB),
        cost_estimate=pl.CostEstimate(flops=flops, bytes_accessed=moved, transcendentals=0),
    )(*operands)


def shape(rows, columns, dtype):
    return jax.ShapeDtypeStruct((rows, columns), dtype)


def pieces(value):
    first = narrow(value)
    value = value - first.astype(jnp.float32)
    second = narrow(value)
    return first, second, narrow(value - second.astype(jnp.float32))


EXTRA = 16


def both_ways(number, blocks, weights, me, before=None):
    bf16, f32 = jnp.bfloat16, jnp.float32
    count, width = len(blocks), blocks[0].shape[1]
    units, last = weights[0][0].shape[1], before is not None
    tok_count = (blocks[0].shape[0] - (0 if last else EXTRA)) // 2
    every, size = count * tok_count, 2 * tok_count
    lanes = 128
    back = size + (EXTRA if last else 0)
    layout = [[b] for b in range(count)] if last else [[0], [1], [2], [4], [5], [6], [7, 3]]
    place_of = {b: (i, j * back) for i, held in enumerate(layout) for j, b in enumerate(held)}

    def body(me_ref, *refs):
        b_refs, w_refs, refs = refs[:count], refs[count : count + 6], refs[count + 6 :]
        before_refs, refs = (refs[:2], refs[2:]) if last else ((), refs)
        q_refs, refs = refs[: len(layout)], refs[len(layout) :]
        weighted_ref, factor_ref, refs = refs[0], refs[1], refs[2:]
        after_refs, refs = ((), refs) if last else (refs[:2], refs[2:])
        wide_w, down_w, refs = refs[0], refs[1], refs[2:]
        x_buf, c_buf, y_buf, g_buf, weighted_buf, factor_buf, refs = *refs[:6], refs[6:]
        share_buf, inner_buf, wide_buf, extra_buf, sems = refs
        fetch = Fetch(sems)
        w_bufs = []
        for e in range(2):
            for i in (2 * e, 2 * e + 1):
                w_bufs.append(wide_w.at[:, pl.ds(i * units, units)])
            w_bufs.append(down_w.at[pl.ds(e * units, units)])
        me = me_ref[0]
        low = lax.rem(me, 8)
        for b in range(count):
            at = pl.ds(b * tok_count, tok_count)
            fetch.start(("x", b), b_refs[b].at[pl.ds(0, tok_count)], x_buf.at[at])
            if b == 0:
                fetch.start(("w", 0), w_refs[0], w_bufs[0])
        if last:
            fetch.start("share", before_refs[0], share_buf)
            fetch.start("inner", before_refs[1], inner_buf)
        else:
            for b in range(count):
                fetch.start(("s", b), b_refs[b].at[pl.ds(size, EXTRA)], extra_buf.at[b])
        for i in (1, 2):
            fetch.start(("w", i), w_refs[i], w_bufs[i])
        for b in range(count):
            at = pl.ds(b * tok_count, tok_count)
            fetch.start(("c", b), b_refs[b].at[pl.ds(tok_count, tok_count)], c_buf.at[at])
        for i in (3, 4, 5):
            fetch.start(("w", i), w_refs[i], w_bufs[i])

        def returned(b, first, rows):
            ref, offset = place_of[b]
            return q_refs[ref].at[pl.ds(offset + first, rows)]

        def place(e):
            number = lax.rem(low + e, 2) + low - lax.rem(low, 2)
            return pl.ds(pl.multiple_of(number * lanes, lanes), lanes)

        upper = me >= 8
        if last:
            fetch.wait("share", "inner")
        else:
            inner_buf[...] = jnp.zeros((lanes, lanes), f32)
            share_buf[...] = jnp.zeros((lanes, lanes), f32)
            for b in range(count):
                fetch.wait(("s", b))
                wide_buf[b] = extra_buf[b].astype(f32)
            for e in range(2):
                for b in range(count):
                    tile = wide_buf[b, :, place(e)]
                    sums = [tile[r : r + 1] + tile[r + 2 : r + 3] + tile[r + 4 : r + 5] for r in (0, 1)]
                    row = e * count + b
                    share_buf[row : row + 1, :] = jnp.where(upper, sums[1], sums[0])
            share_buf[...] = share_buf[...].T

        half = slice(number * tok_count, (number + 1) * tok_count)
        fetch.wait(*[("x", b) for b in range(count)])
        x = x_buf[...]
        for e in range(2):
            columns = slice(e * units, (e + 1) * units)
            fetch.wait(("w", 3 * e))
            gate = dot(x, wide_w[:, 2 * e * units : (2 * e + 1) * units], ((1,), (0,)))
            fetch.wait(("w", 3 * e + 1))
            up = dot(x, wide_w[:, (2 * e + 1) * units : (2 * e + 2) * units], ((1,), (0,)))
            fetch.wait(("w", 3 * e + 2))
            if e == 0:
                fetch.wait(*[("c", b) for b in range(count)])
            plain = dot(c_buf[...], down_w[columns, :], ((1,), (1,)))
            sigma = jax.nn.sigmoid(gate)
            silu_val = gate * sigma
            hidden = silu_val * up
            part = [share_buf[half, e * count + b : e * count + b + 1] for b in range(count)]
            part = jnp.concatenate(part, axis=0)
            weighted_buf[:, columns] = (part * hidden).astype(bf16)
            inner = jnp.sum(hidden * plain, axis=1, keepdims=True)
            for b in range(count):
                value = inner[b * tok_count : (b + 1) * tok_count]
                inner_buf[half, e * count + b : e * count + b + 1] = value
            grad_hidden = part * plain
            grad_gate = (grad_hidden * up * (sigma * (1.0 + gate * (1.0 - sigma)))).astype(bf16)
            grad_up = (grad_hidden * silu_val).astype(bf16)
            factor_buf[:, 2 * e * units : (2 * e + 1) * units] = grad_gate
            factor_buf[:, (2 * e + 1) * units : (2 * e + 2) * units] = grad_up
        fetch.start("weighted", weighted_buf, weighted_ref)
        fetch.start("factor", factor_buf, factor_ref)
        y_buf[...] = dot(weighted_buf[...], down_w[...], ((1,), (0,))).astype(bf16)
        for b in range(count):
            at = pl.ds(b * tok_count, tok_count)
            fetch.start(("y", b), y_buf.at[at], returned(b, 0, tok_count))
        g_buf[...] = dot(factor_buf[...], wide_w[...], ((1,), (1,))).astype(bf16)
        for b in range(count):
            at = pl.ds(b * tok_count, tok_count)
            fetch.start(("g", b), g_buf.at[at], returned(b, tok_count, tok_count))
        if last:
            wide_buf[...] = jnp.zeros((count, EXTRA, width), f32)
            inner_buf[...] = inner_buf[...].T
            for e in range(2):
                for b in range(count):
                    row = e * count + b
                    value, lines = inner_buf[row : row + 1, :], []
                    for _ in range(3):
                        piece = value.astype(bf16).astype(f32)
                        lines += [jnp.where(upper, 0.0, piece), jnp.where(upper, piece, 0.0)]
                        value = value - piece
                    lines += [jnp.zeros((2, lanes), f32)]
                    wide_buf[b, 0:8, place(e)] = jnp.concatenate(lines, axis=0)
            for b in range(count):
                extra_buf[b] = wide_buf[b].astype(bf16)
                fetch.start(("i", b), extra_buf.at[b], returned(b, size, EXTRA))
        else:
            fetch.start("share", share_buf, after_refs[0])
            fetch.start("inner", inner_buf, after_refs[1])
        fetch.wait_all()

    outs = [shape(len(held) * back, width, bf16) for held in layout]
    outs += [shape(every, 2 * units, bf16), shape(every, 4 * units, bf16)]
    small = shape(lanes, lanes, f32)
    operands = (*blocks, *weights[0], *weights[1])
    if last:
        operands += before
    else:
        outs += [small, small]
    scratch = [pltpu.VMEM((width, 4 * units), bf16), pltpu.VMEM((2 * units, width), bf16)]
    scratch += [pltpu.VMEM((every, width), bf16)] * 4
    scratch += [pltpu.VMEM((every, 2 * units), bf16), pltpu.VMEM((every, 4 * units), bf16)]
    scratch += [pltpu.VMEM(small.shape, f32)] * 2
    scratch += [pltpu.VMEM((count, EXTRA, width), f32), pltpu.VMEM((count, EXTRA, width), bf16)]
    flops = 24 * every * width * units
    copies = 5 * count + 6 + 2 + 2
    outs = kernel(body, outs, scratch, copies, flops, *operands, scalar=me)
    return outs[: len(layout)], outs[len(layout) :]


def weight_grads(expert, blocks, factors, away=None):
    bf16 = jnp.bfloat16
    parts, count, width = len(blocks), len(blocks[0]), blocks[0][0].shape[1]
    each = factors[0][0].shape[0]
    tok_count, every, units = each // count, each * parts, factors[0][0].shape[1] // 2
    extra = 0 if away is None else 1

    def body(*refs):
        b_refs, refs = refs[: parts * count], refs[parts * count :]
        f_refs, refs = refs[: 2 * parts], refs[2 * parts :]
        away_refs, out_refs, refs = refs[:extra], refs[extra : 3 * extra + 1], refs[3 * extra + 1 :]
        x_buf, c_buf, weighted_buf, factor_buf, *bufs, sems = refs
        away_bufs, out_bufs = bufs[:extra], bufs[extra:]
        fetch = Fetch(sems)
        names = range(parts * count)
        for i in names:
            at = pl.ds(i * tok_count, tok_count)
            fetch.start(("x", i), b_refs[i].at[pl.ds(0, tok_count)], x_buf.at[at])
        for p in range(parts):
            at = pl.ds(p * each, each)
            lanes = pl.ds(2 * expert * units, 2 * units)
            fetch.start(("f", p), f_refs[2 * p + 1].at[:, lanes], factor_buf.at[at])
        if extra:
            fetch.start("away", away_refs[0], away_bufs[0])
        for p in range(parts):
            at = pl.ds(p * each, each)
            lanes = pl.ds(expert * units, units)
            fetch.start(("w", p), f_refs[2 * p].at[:, lanes], weighted_buf.at[at])
        for i in names:
            at = pl.ds(i * tok_count, tok_count)
            fetch.start(("c", i), b_refs[i].at[pl.ds(tok_count, tok_count)], c_buf.at[at])
        fetch.wait(*[("x", i) for i in names], *[("f", p) for p in range(parts)])
        for number in range(3):
            if number < 2:
                left, right = x_buf, factor_buf[:, number * units : (number + 1) * units]
                columns, into = slice(number * units, (number + 1) * units), slice(0, width)
            else:
                fetch.wait(*[("c", i) for i in names], *[("w", p) for p in range(parts)])
                left, right = weighted_buf, c_buf[...]
                columns, into = slice(0, width), slice(width, width + units)
            for start in range(0, into.stop - into.start, units):
                value = dot(left[:, start : start + units], right, ((0,), (0,)))
                at = slice(into.start + start, into.start + start + units)
                if not extra:
                    out_bufs[0][at, columns] = value.astype(bf16)
                else:
                    fetch.wait("away")
                    value = value + away_bufs[0][at, columns].astype(jnp.float32)
                    out_bufs[number][start : start + units, :] = value.astype(bf16)
                    block = out_bufs[number].at[start : start + units]
                    target = out_refs[number].at[start : start + units]
                    fetch.start(("out", number, start), block, target)
            if not extra and number:
                at = pl.ds(into.start, into.stop - into.start)
                fetch.start(("out", number), out_bufs[0].at[at], out_refs[0].at[at])
        fetch.wait_all()

    flops = 6 * every * width * units
    operands = (*[b for part in blocks for b in part], *[f for part in factors for f in part])
    scratch = [pltpu.VMEM((every, width), bf16)] * 2
    scratch += [pltpu.VMEM((every, units), bf16), pltpu.VMEM((every, 2 * units), bf16)]
    packed = shape(width + units, width, bf16)
    if away is None:
        outs = [packed]
        scratch += [pltpu.VMEM(packed.shape, bf16)]
    else:
        operands += (away,)
        outs = [shape(width, units, bf16)] * 2 + [shape(units, width, bf16)]
        scratch += [pltpu.VMEM(v.shape, bf16) for v in (packed, *outs)]
    copies = 2 * parts * count + 2 * parts + 1 + 2 * -(-width // units) + 1
    outs = kernel(body, outs, scratch, copies, flops, *operands)
    return outs if extra else outs[0]


def paired(latent_in, routes, combine_weights, cotangent, w_gate, w_up, w_down):
    f32 = jnp.float32
    devices_ep, tok_count, width = lax.axis_size("ep"), *latent_in.shape
    me = lax.axis_index("ep")
    mid = tok_count // 2
    experts = jnp.arange(devices_ep, dtype=jnp.int32)
    own = (w_gate[0], w_up[0], w_down[0])

    chosen = routes[None, :, :] == experts[:, None, None]
    share = jnp.sum(jnp.where(chosen, combine_weights[None, :, :], 0.0), axis=2)
    lines = jnp.stack(pieces(share)).reshape(-1, width)
    lines = jnp.pad(lines, ((0, EXTRA - lines.shape[0]), (0, 0)))
    a0 = jnp.concatenate([latent_in[:mid], cotangent[:mid], lines], axis=0)
    b0 = jnp.concatenate([latent_in[mid:], cotangent[mid:]], axis=0)
    gate_w = swap(own[0], CORE)
    a0, b0, gate_w, own = fence(a0, b0, gate_w, own)

    a2, a4, b4, a1 = swap(a0, FAR), swap(a0, SIDE), swap(b0, SIDE), swap(a0, NEAR)
    up_w = swap(own[1], CORE)
    a1, a4, a2, b4, up_w, b0, own = fence(a1, a4, a2, b4, up_w, b0, own)
    a5, a6, a3, b2 = swap(a1, SIDE), swap(a2, SIDE), swap(a2, NEAR), swap(b0, FAR)
    down_w = swap(own[2], CORE)
    (a3,) = fence(a3)
    a7 = swap(a3, SIDE)
    b2, a5, a6 = fence(b2, a5, a6)
    b6, b1, b3 = swap(b2, SIDE), swap(b0, NEAR), swap(b2, NEAR)
    a7, b1, b6 = fence(a7, b1, b6)
    b5, b7 = swap(b1, SIDE), swap(b6, NEAR)
    weights, me = (own, (gate_w, up_w, down_w)), me.astype(jnp.int32).reshape(1)
    a = [a0, a1, a2, a3, a4, a5, a6, a7]
    q, (*a_factors, shares, inners) = both_ways(0, a, weights, me)
    q0, q1, q2, q4, q5, q6, q73 = q
    q73, q5, shares, inners, b5, b7 = fence(q73, q5, shares, inners, b5, b7)
    r73, r5 = swap(q73, NEAR), swap(q5, SIDE)
    b = [b0, b1, b2, b3, b4, b5, b6, b7]
    p, b_factors = both_ways(1, b, weights, me, (shares, inners))
    p0, p1, p2, p3, p4, p5, p6, p7 = p
    r73, r5, q6, q4, p7, p6, p5, p4, b_factors = fence(r73, r5, q6, q4, p7, p6, p5, p4, b_factors)
    factors, size = (a_factors, b_factors), q6.shape[0]
    q6, q2, q1 = narrow(added(q6, r73[:size])), added(q2, r73[size:]), narrow(added(q1, r5))
    q6, p7, q1 = fence(q6, p7, q1)
    r6, r7, q1 = swap(q6, SIDE), swap(p7, SIDE), swap(q1, NEAR)
    away = weight_grads(1, (a, b), factors)
    r6, away, p6, p5 = fence(r6, away, p6, p5)
    q2 = swap(narrow(q2 + r6.astype(f32)), FAR)
    r7, p6, p5, away = fence(r7, p6, p5, away)
    p3 = narrow(added(p3, r7))
    p3, p6, p5, away = fence(p3, p6, p5, away)
    r6, p3, r5, away = swap(p6, SIDE), swap(p3, NEAR), swap(p5, SIDE), swap(away, CORE)
    r6, p3, q4, p4 = fence(r6, p3, q4, p4)
    p2 = swap(narrow(added(p2, r6) + p3.astype(f32)), FAR)
    r5, away, p4, q4, q2 = fence(r5, away, p4, q4, q2)
    p1 = narrow(added(p1, r5))
    p1, p4, q4, away = fence(p1, p4, q4, away)
    p4, q4, p1 = swap(p4, SIDE), swap(q4, SIDE), swap(p1, NEAR)
    grad_w = weight_grads(0, (a, b), factors, away)
    p2, p4, q4, p1, grad_w = fence(p2, p4, q4, p1, grad_w)

    q = added(q0, q4) + added(q1, q2)
    p = added(p0, p4) + added(p1, p2)
    combined = narrow(jnp.concatenate([q[:mid], p[:mid]], axis=0))
    grad_latent = narrow(jnp.concatenate([q[mid : 2 * mid], p[mid : 2 * mid]], axis=0))
    inner = p[2 * mid :].reshape(-1, devices_ep, tok_count)[:3].sum(axis=0)
    grad_combine = jnp.sum(jnp.where(chosen, inner[:, :, None], 0.0), axis=0)
    return (combined, grad_latent, grad_combine, *[v[None] for v in grad_w])


def local(latent_in, routes, combine_weights, cotangent, w_gate, w_up, w_down):
    plan = paired if w_gate.shape[0] == 1 and lax.axis_size("ep") == 2 * len(REACH) else exchanged
    return plan(latent_in, routes, combine_weights, cotangent, w_gate, w_up, w_down)


def solution(mesh):
    return jax.shard_map(
        local,
        mesh=mesh,
        in_specs=(
            P(("grp", "ep"), None),
            P(("grp", "ep"), None),
            P(("grp", "ep"), None),
            P(("grp", "ep"), None),
            P("ep", None, None),
            P("ep", None, None),
            P("ep", None, None),
        ),
        out_specs=(
            P(("grp", "ep"), None),
            P(("grp", "ep"), None),
            P(("grp", "ep"), None),
            P(("grp", "ep"), None, None),
            P(("grp", "ep"), None, None),
            P(("grp", "ep"), None, None),
        ),
        check_vma=False,
    )
```

```python
import jax
import jax.numpy as jnp
from jax import lax
from jax.experimental import pallas as pl
from jax.experimental.pallas import tpu as pltpu
from jax.sharding import PartitionSpec as P


def assign_slots(route_rows, expert_count):
    flat_ids = route_rows.reshape(-1)
    onehot = (flat_ids[:, None] == jnp.arange(expert_count, dtype=jnp.int32)[None, :]).astype(
        jnp.int32
    )
    ranks = jnp.cumsum(onehot, axis=0) - 1
    return (flat_ids, jnp.sum(onehot * ranks, axis=1))


def expert_forward(rows, gate_w, up_w, down_w):
    gate_pre = jnp.einsum("erl,elf->erf", rows, gate_w, preferred_element_type=jnp.float32)
    up_pre = jnp.einsum("erl,elf->erf", rows, up_w, preferred_element_type=jnp.float32)
    sigma = jax.nn.sigmoid(gate_pre)
    silu_val = gate_pre * sigma
    hidden = (silu_val * up_pre).astype(jnp.bfloat16)
    expert_out = jnp.einsum(
        "erf,efl->erl", hidden, down_w, preferred_element_type=jnp.float32
    ).astype(jnp.bfloat16)
    return (expert_out, (gate_pre, up_pre, sigma, silu_val, hidden))


def expert_backward(rows, grad_out, saved, gate_w, up_w, down_w):
    gate_pre, up_pre, sigma, silu_val, hidden = saved
    grad_down = jnp.einsum(
        "erf,erl->efl", hidden, grad_out, preferred_element_type=jnp.float32
    ).astype(jnp.bfloat16)
    grad_hidden = jnp.einsum("erl,efl->erf", grad_out, down_w, preferred_element_type=jnp.float32)
    grad_gate = (grad_hidden * up_pre * sigma * (1.0 + gate_pre * (1.0 - sigma))).astype(
        jnp.bfloat16
    )
    grad_up = (grad_hidden * silu_val).astype(jnp.bfloat16)
    grad_gw = jnp.einsum(
        "erl,erf->elf", rows, grad_gate, preferred_element_type=jnp.float32
    ).astype(jnp.bfloat16)
    grad_uw = jnp.einsum("erl,erf->elf", rows, grad_up, preferred_element_type=jnp.float32).astype(
        jnp.bfloat16
    )
    grad_rows = (
        jnp.einsum("erf,elf->erl", grad_gate, gate_w, preferred_element_type=jnp.float32)
        + jnp.einsum("erf,elf->erl", grad_up, up_w, preferred_element_type=jnp.float32)
    ).astype(jnp.bfloat16)
    return (grad_rows, grad_gw, grad_uw, grad_down)


def exchanged(latent_in, routes, combine_weights, cotangent, w_gate, w_up, w_down):
    devices_ep = lax.axis_size("ep")
    local_experts = w_gate.shape[0]
    expert_count = local_experts * devices_ep
    tok_count = latent_in.shape[0]
    top_count = routes.shape[1]
    width = latent_in.shape[1]
    capacity = tok_count * top_count * 3 // (2 * expert_count)
    expert_ids, slot_ids = assign_slots(routes, expert_count)
    position = expert_ids * capacity + slot_ids
    repeated = jnp.repeat(latent_in, top_count, axis=0)
    weighted = (combine_weights[:, :, None] * cotangent.astype(jnp.float32)[:, None, :]).astype(
        jnp.bfloat16
    )
    send_rows = jnp.zeros((expert_count * capacity, width), jnp.bfloat16).at[position].set(repeated)
    send_rows = send_rows.reshape(expert_count, capacity, width)
    send_cot = (
        jnp.zeros((expert_count * capacity, width), jnp.bfloat16)
        .at[position]
        .set(weighted.reshape(-1, width))
    )
    send_cot = send_cot.reshape(expert_count, capacity, width)

    def to_local(received):
        shaped = received.reshape(devices_ep, local_experts, capacity, width)
        return shaped.transpose(1, 0, 2, 3).reshape(local_experts, devices_ep * capacity, width)

    def to_home(local_rows):
        shaped = local_rows.reshape(local_experts, devices_ep, capacity, width)
        return shaped.transpose(1, 0, 2, 3).reshape(expert_count, capacity, width)

    got_rows = lax.all_to_all(send_rows, "ep", split_axis=0, concat_axis=0, tiled=True)
    rows_local = to_local(got_rows)
    expert_out, saved = expert_forward(rows_local, w_gate, w_up, w_down)
    back_out = lax.all_to_all(to_home(expert_out), "ep", split_axis=0, concat_axis=0, tiled=True)
    got_cot = lax.all_to_all(send_cot, "ep", split_axis=0, concat_axis=0, tiled=True)
    grad_rows, grad_gw, grad_uw, grad_down = expert_backward(
        rows_local, to_local(got_cot), saved, w_gate, w_up, w_down
    )
    back_grad = lax.all_to_all(to_home(grad_rows), "ep", split_axis=0, concat_axis=0, tiled=True)
    out_rows = (
        back_out.reshape(-1, width)[position]
        .reshape(tok_count, top_count, width)
        .astype(jnp.float32)
    )
    grad_back = (
        back_grad.reshape(-1, width)[position]
        .reshape(tok_count, top_count, width)
        .astype(jnp.float32)
    )
    combined = jnp.sum(combine_weights[:, :, None] * out_rows, axis=1).astype(jnp.bfloat16)
    grad_combine = jnp.sum(cotangent.astype(jnp.float32)[:, None, :] * out_rows, axis=2)
    grad_latent = jnp.sum(grad_back, axis=1).astype(jnp.bfloat16)
    return (combined, grad_latent, grad_combine, grad_gw, grad_uw, grad_down)


def dot(a, b, dims):
    return lax.dot_general(a, b, (dims, ((), ())), preferred_element_type=jnp.float32)


def swap(value, bit):
    pairs = [(i, i ^ bit) for i in range(lax.axis_size("ep"))]
    return lax.ppermute(value, "ep", pairs)


CORE, SIDE, NEAR, FAR = 1, 2, 4, 8
REACH = (0, NEAR, FAR, NEAR | FAR, SIDE, SIDE | NEAR, SIDE | FAR, SIDE | NEAR | FAR)


def fence(*values):
    return lax.optimization_barrier(values)


def added(a, b):
    return a.astype(jnp.float32) + b.astype(jnp.float32)


def narrow(value):
    return value.astype(jnp.bfloat16)


MIB = 1 << 20


class Fetch:
    def __init__(self, sems):
        self.sems, self.waiting = sems, {}

    def start(self, name, source, target):
        copy = pltpu.make_async_copy(source, target, self.sems.at[len(self.waiting)])
        copy.start()
        self.waiting[name] = [copy, False]

    def wait(self, *names):
        for name in names:
            if not self.waiting[name][1]:
                self.waiting[name][0].wait()
                self.waiting[name][1] = True

    def wait_all(self):
        self.wait(*self.waiting)


def kernel(body, outs, scratch, copies, flops, *operands, scalar=None):
    moved = sum(v.size * v.dtype.itemsize for v in (*operands, *outs))
    in_specs = [pl.BlockSpec(memory_space=pl.ANY)] * len(operands)
    if scalar is not None:
        operands = (scalar, *operands)
        in_specs = [pl.BlockSpec(memory_space=pltpu.SMEM), *in_specs]
    return pl.pallas_call(
        body,
        out_shape=outs,
        in_specs=in_specs,
        out_specs=[pl.BlockSpec(memory_space=pl.ANY)] * len(outs),
        scratch_shapes=[*scratch, pltpu.SemaphoreType.DMA((copies,))],
        compiler_params=pltpu.CompilerParams(vmem_limit_bytes=56 * MIB),
        cost_estimate=pl.CostEstimate(flops=flops, bytes_accessed=moved, transcendentals=0),
    )(*operands)


def shape(rows, columns, dtype):
    return jax.ShapeDtypeStruct((rows, columns), dtype)


def pieces(value):
    first = narrow(value)
    value = value - first.astype(jnp.float32)
    second = narrow(value)
    return first, second, narrow(value - second.astype(jnp.float32))


EXTRA = 16


def both_ways(number, blocks, weights, me, before=None):
    bf16, f32 = jnp.bfloat16, jnp.float32
    count, width = len(blocks), blocks[0].shape[1]
    units, last = weights[0][0].shape[1], before is not None
    tok_count = (blocks[0].shape[0] - (0 if last else EXTRA)) // 2
    every, size = count * tok_count, 2 * tok_count
    lanes = 128
    back = size + (EXTRA if last else 0)
    layout = [[b] for b in range(count)] if last else [[0], [1], [2], [4], [5], [6], [7, 3]]
    place_of = {b: (i, j * back) for i, held in enumerate(layout) for j, b in enumerate(held)}

    def body(me_ref, *refs):
        b_refs, w_refs, refs = refs[:count], refs[count : count + 6], refs[count + 6 :]
        before_refs, refs = (refs[:2], refs[2:]) if last else ((), refs)
        q_refs, refs = refs[: len(layout)], refs[len(layout) :]
        weighted_ref, factor_ref, refs = refs[0], refs[1], refs[2:]
        after_refs, refs = ((), refs) if last else (refs[:2], refs[2:])
        wide_w, down_w, refs = refs[0], refs[1], refs[2:]
        x_buf, c_buf, y_buf, g_buf, weighted_buf, factor_buf, refs = *refs[:6], refs[6:]
        share_buf, inner_buf, wide_buf, extra_buf, sems = refs
        fetch = Fetch(sems)
        w_bufs = []
        for e in range(2):
            for i in (2 * e, 2 * e + 1):
                w_bufs.append(wide_w.at[:, pl.ds(i * units, units)])
            w_bufs.append(down_w.at[pl.ds(e * units, units)])
        me = me_ref[0]
        low = lax.rem(me, 8)
        for b in range(count):
            at = pl.ds(b * tok_count, tok_count)
            fetch.start(("x", b), b_refs[b].at[pl.ds(0, tok_count)], x_buf.at[at])
            if b == 0:
                fetch.start(("w", 0), w_refs[0], w_bufs[0])
        if last:
            fetch.start("share", before_refs[0], share_buf)
            fetch.start("inner", before_refs[1], inner_buf)
        else:
            for b in range(count):
                fetch.start(("s", b), b_refs[b].at[pl.ds(size, EXTRA)], extra_buf.at[b])
        for i in (1, 2):
            fetch.start(("w", i), w_refs[i], w_bufs[i])
        for b in range(count):
            at = pl.ds(b * tok_count, tok_count)
            fetch.start(("c", b), b_refs[b].at[pl.ds(tok_count, tok_count)], c_buf.at[at])
        for i in (3, 4, 5):
            fetch.start(("w", i), w_refs[i], w_bufs[i])

        def returned(b, first, rows):
            ref, offset = place_of[b]
            return q_refs[ref].at[pl.ds(offset + first, rows)]

        def place(e):
            number = lax.rem(low + e, 2) + low - lax.rem(low, 2)
            return pl.ds(pl.multiple_of(number * lanes, lanes), lanes)

        upper = me >= 8
        if last:
            fetch.wait("share", "inner")
        else:
            inner_buf[...] = jnp.zeros((lanes, lanes), f32)
            share_buf[...] = jnp.zeros((lanes, lanes), f32)
            for b in range(count):
                fetch.wait(("s", b))
                wide_buf[b] = extra_buf[b].astype(f32)
            for e in range(2):
                for b in range(count):
                    tile = wide_buf[b, :, place(e)]
                    sums = [tile[r : r + 1] + tile[r + 2 : r + 3] + tile[r + 4 : r + 5] for r in (0, 1)]
                    row = e * count + b
                    share_buf[row : row + 1, :] = jnp.where(upper, sums[1], sums[0])
            share_buf[...] = share_buf[...].T

        half = slice(number * tok_count, (number + 1) * tok_count)
        fetch.wait(*[("x", b) for b in range(count)])
        x = x_buf[...]
        for e in range(2):
            columns = slice(e * units, (e + 1) * units)
            fetch.wait(("w", 3 * e))
            gate = dot(x, wide_w[:, 2 * e * units : (2 * e + 1) * units], ((1,), (0,)))
            fetch.wait(("w", 3 * e + 1))
            up = dot(x, wide_w[:, (2 * e + 1) * units : (2 * e + 2) * units], ((1,), (0,)))
            fetch.wait(("w", 3 * e + 2))
            if e == 0:
                fetch.wait(*[("c", b) for b in range(count)])
            plain = dot(c_buf[...], down_w[columns, :], ((1,), (1,)))
            sigma = jax.nn.sigmoid(gate)
            silu_val = gate * sigma
            hidden = silu_val * up
            part = [share_buf[half, e * count + b : e * count + b + 1] for b in range(count)]
            part = jnp.concatenate(part, axis=0)
            weighted_buf[:, columns] = (part * hidden).astype(bf16)
            inner = jnp.sum(hidden * plain, axis=1, keepdims=True)
            for b in range(count):
                value = inner[b * tok_count : (b + 1) * tok_count]
                inner_buf[half, e * count + b : e * count + b + 1] = value
            grad_hidden = part * plain
            grad_gate = (grad_hidden * up * (sigma * (1.0 + gate * (1.0 - sigma)))).astype(bf16)
            grad_up = (grad_hidden * silu_val).astype(bf16)
            factor_buf[:, 2 * e * units : (2 * e + 1) * units] = grad_gate
            factor_buf[:, (2 * e + 1) * units : (2 * e + 2) * units] = grad_up
        fetch.start("weighted", weighted_buf, weighted_ref)
        fetch.start("factor", factor_buf, factor_ref)
        y_buf[...] = dot(weighted_buf[...], down_w[...], ((1,), (0,))).astype(bf16)
        for b in range(count):
            at = pl.ds(b * tok_count, tok_count)
            fetch.start(("y", b), y_buf.at[at], returned(b, 0, tok_count))
        g_buf[...] = dot(factor_buf[...], wide_w[...], ((1,), (1,))).astype(bf16)
        for b in range(count):
            at = pl.ds(b * tok_count, tok_count)
            fetch.start(("g", b), g_buf.at[at], returned(b, tok_count, tok_count))
        if last:
            wide_buf[...] = jnp.zeros((count, EXTRA, width), f32)
            inner_buf[...] = inner_buf[...].T
            for e in range(2):
                for b in range(count):
                    row = e * count + b
                    value, lines = inner_buf[row : row + 1, :], []
                    for _ in range(3):
                        piece = value.astype(bf16).astype(f32)
                        lines += [jnp.where(upper, 0.0, piece), jnp.where(upper, piece, 0.0)]
                        value = value - piece
                    lines += [jnp.zeros((2, lanes), f32)]
                    wide_buf[b, 0:8, place(e)] = jnp.concatenate(lines, axis=0)
            for b in range(count):
                extra_buf[b] = wide_buf[b].astype(bf16)
                fetch.start(("i", b), extra_buf.at[b], returned(b, size, EXTRA))
        else:
            fetch.start("share", share_buf, after_refs[0])
            fetch.start("inner", inner_buf, after_refs[1])
        fetch.wait_all()

    outs = [shape(len(held) * back, width, bf16) for held in layout]
    outs += [shape(every, 2 * units, bf16), shape(every, 4 * units, bf16)]
    small = shape(lanes, lanes, f32)
    operands = (*blocks, *weights[0], *weights[1])
    if last:
        operands += before
    else:
        outs += [small, small]
    scratch = [pltpu.VMEM((width, 4 * units), bf16), pltpu.VMEM((2 * units, width), bf16)]
    scratch += [pltpu.VMEM((every, width), bf16)] * 4
    scratch += [pltpu.VMEM((every, 2 * units), bf16), pltpu.VMEM((every, 4 * units), bf16)]
    scratch += [pltpu.VMEM(small.shape, f32)] * 2
    scratch += [pltpu.VMEM((count, EXTRA, width), f32), pltpu.VMEM((count, EXTRA, width), bf16)]
    flops = 24 * every * width * units
    copies = 5 * count + 6 + 2 + 2
    outs = kernel(body, outs, scratch, copies, flops, *operands, scalar=me)
    return outs[: len(layout)], outs[len(layout) :]


def weight_grads(expert, blocks, factors, away=None):
    bf16 = jnp.bfloat16
    parts, count, width = len(blocks), len(blocks[0]), blocks[0][0].shape[1]
    each = factors[0][0].shape[0]
    tok_count, every, units = each // count, each * parts, factors[0][0].shape[1] // 2
    extra = 0 if away is None else 1

    def body(*refs):
        b_refs, refs = refs[: parts * count], refs[parts * count :]
        f_refs, refs = refs[: 2 * parts], refs[2 * parts :]
        away_refs, out_refs, refs = refs[:extra], refs[extra : 3 * extra + 1], refs[3 * extra + 1 :]
        x_buf, c_buf, weighted_buf, factor_buf, *bufs, sems = refs
        away_bufs, out_bufs = bufs[:extra], bufs[extra:]
        fetch = Fetch(sems)
        names = range(parts * count)
        for i in names:
            at = pl.ds(i * tok_count, tok_count)
            fetch.start(("x", i), b_refs[i].at[pl.ds(0, tok_count)], x_buf.at[at])
        for p in range(parts):
            at = pl.ds(p * each, each)
            lanes = pl.ds(2 * expert * units, 2 * units)
            fetch.start(("f", p), f_refs[2 * p + 1].at[:, lanes], factor_buf.at[at])
        if extra:
            fetch.start("away", away_refs[0], away_bufs[0])
        for p in range(parts):
            at = pl.ds(p * each, each)
            lanes = pl.ds(expert * units, units)
            fetch.start(("w", p), f_refs[2 * p].at[:, lanes], weighted_buf.at[at])
        for i in names:
            at = pl.ds(i * tok_count, tok_count)
            fetch.start(("c", i), b_refs[i].at[pl.ds(tok_count, tok_count)], c_buf.at[at])
        fetch.wait(*[("x", i) for i in names], *[("f", p) for p in range(parts)])
        for number in range(3):
            if number < 2:
                left, right = x_buf, factor_buf[:, number * units : (number + 1) * units]
                columns, into = slice(number * units, (number + 1) * units), slice(0, width)
            else:
                fetch.wait(*[("c", i) for i in names], *[("w", p) for p in range(parts)])
                left, right = weighted_buf, c_buf[...]
                columns, into = slice(0, width), slice(width, width + units)
            for start in range(0, into.stop - into.start, units):
                value = dot(left[:, start : start + units], right, ((0,), (0,)))
                at = slice(into.start + start, into.start + start + units)
                if not extra:
                    out_bufs[0][at, columns] = value.astype(bf16)
                else:
                    fetch.wait("away")
                    value = value + away_bufs[0][at, columns].astype(jnp.float32)
                    out_bufs[number][start : start + units, :] = value.astype(bf16)
                    block = out_bufs[number].at[start : start + units]
                    target = out_refs[number].at[start : start + units]
                    fetch.start(("out", number, start), block, target)
            if not extra and number:
                at = pl.ds(into.start, into.stop - into.start)
                fetch.start(("out", number), out_bufs[0].at[at], out_refs[0].at[at])
        fetch.wait_all()

    flops = 6 * every * width * units
    operands = (*[b for part in blocks for b in part], *[f for part in factors for f in part])
    scratch = [pltpu.VMEM((every, width), bf16)] * 2
    scratch += [pltpu.VMEM((every, units), bf16), pltpu.VMEM((every, 2 * units), bf16)]
    packed = shape(width + units, width, bf16)
    if away is None:
        outs = [packed]
        scratch += [pltpu.VMEM(packed.shape, bf16)]
    else:
        operands += (away,)
        outs = [shape(width, units, bf16)] * 2 + [shape(units, width, bf16)]
        scratch += [pltpu.VMEM(v.shape, bf16) for v in (packed, *outs)]
    copies = 2 * parts * count + 2 * parts + 1 + 2 * -(-width // units) + 1
    outs = kernel(body, outs, scratch, copies, flops, *operands)
    return outs if extra else outs[0]


def paired(latent_in, routes, combine_weights, cotangent, w_gate, w_up, w_down):
    f32 = jnp.float32
    devices_ep, tok_count, width = lax.axis_size("ep"), *latent_in.shape
    me = lax.axis_index("ep")
    mid = tok_count // 2
    experts = jnp.arange(devices_ep, dtype=jnp.int32)
    own = (w_gate[0], w_up[0], w_down[0])

    chosen = routes[None, :, :] == experts[:, None, None]
    share = jnp.sum(jnp.where(chosen, combine_weights[None, :, :], 0.0), axis=2)
    lines = jnp.stack(pieces(share)).reshape(-1, width)
    lines = jnp.pad(lines, ((0, EXTRA - lines.shape[0]), (0, 0)))
    a0 = jnp.concatenate([latent_in[:mid], cotangent[:mid], lines], axis=0)
    b0 = jnp.concatenate([latent_in[mid:], cotangent[mid:]], axis=0)
    gate_w = swap(own[0], CORE)
    a0, b0, gate_w, own = fence(a0, b0, gate_w, own)

    a2, a4, b4, a1 = swap(a0, FAR), swap(a0, SIDE), swap(b0, SIDE), swap(a0, NEAR)
    up_w = swap(own[1], CORE)
    a1, a4, a2, b4, up_w, b0, own = fence(a1, a4, a2, b4, up_w, b0, own)
    a5, a6, a3, b2 = swap(a1, SIDE), swap(a2, SIDE), swap(a2, NEAR), swap(b0, FAR)
    down_w = swap(own[2], CORE)
    (a3,) = fence(a3)
    a7 = swap(a3, SIDE)
    b2, a5, a6 = fence(b2, a5, a6)
    b6, b1, b3 = swap(b2, SIDE), swap(b0, NEAR), swap(b2, NEAR)
    a7, b1, b6 = fence(a7, b1, b6)
    b5, b7 = swap(b1, SIDE), swap(b6, NEAR)
    weights, me = (own, (gate_w, up_w, down_w)), me.astype(jnp.int32).reshape(1)
    a = [a0, a1, a2, a3, a4, a5, a6, a7]
    q, (*a_factors, shares, inners) = both_ways(0, a, weights, me)
    q0, q1, q2, q4, q5, q6, q73 = q
    q73, q5, q4, shares, inners, b5, b7 = fence(q73, q5, q4, shares, inners, b5, b7)
    r73, r5, q4 = swap(q73, NEAR), swap(q5, SIDE), swap(q4, SIDE)
    b = [b0, b1, b2, b3, b4, b5, b6, b7]
    p, b_factors = both_ways(1, b, weights, me, (shares, inners))
    p0, p1, p2, p3, p4, p5, p6, p7 = p
    r73, r5, q6, q4, p7, p6, p5, p4, b_factors = fence(r73, r5, q6, q4, p7, p6, p5, p4, b_factors)
    factors, size = (a_factors, b_factors), q6.shape[0]
    q6, q2, q1 = narrow(added(q6, r73[:size])), added(q2, r73[size:]), narrow(added(q1, r5))
    q6, p7, q1 = fence(q6, p7, q1)
    r6, r7, q1 = swap(q6, SIDE), swap(p7, SIDE), swap(q1, NEAR)
    away = weight_grads(1, (a, b), factors)
    r6, q1, away, p6, p5 = fence(r6, q1, away, p6, p5)
    q2 = swap(narrow(q2 + r6.astype(f32)), FAR)
    r7, p6, p5, away = fence(r7, p6, p5, away)
    p3 = narrow(added(p3, r7))
    p3, p6, p5, away = fence(p3, p6, p5, away)
    r6, p3, r5, away = swap(p6, SIDE), swap(p3, NEAR), swap(p5, SIDE), swap(away, CORE)
    r6, p3, p4 = fence(r6, p3, p4)
    p2 = swap(narrow(added(p2, r6) + p3.astype(f32)), FAR)
    r5, away, p4, q2 = fence(r5, away, p4, q2)
    p1 = narrow(added(p1, r5))
    p1, p4, away = fence(p1, p4, away)
    p4, p1 = swap(p4, SIDE), swap(p1, NEAR)
    grad_w = weight_grads(0, (a, b), factors, away)
    p2, p4, p1, grad_w = fence(p2, p4, p1, grad_w)

    q = added(q0, q4) + added(q1, q2)
    p = added(p0, p4) + added(p1, p2)
    combined = narrow(jnp.concatenate([q[:mid], p[:mid]], axis=0))
    grad_latent = narrow(jnp.concatenate([q[mid : 2 * mid], p[mid : 2 * mid]], axis=0))
    inner = p[2 * mid :].reshape(-1, devices_ep, tok_count)[:3].sum(axis=0)
    grad_combine = jnp.sum(jnp.where(chosen, inner[:, :, None], 0.0), axis=0)
    return (combined, grad_latent, grad_combine, *[v[None] for v in grad_w])


def local(latent_in, routes, combine_weights, cotangent, w_gate, w_up, w_down):
    plan = paired if w_gate.shape[0] == 1 and lax.axis_size("ep") == 2 * len(REACH) else exchanged
    return plan(latent_in, routes, combine_weights, cotangent, w_gate, w_up, w_down)


def solution(mesh):
    return jax.shard_map(
        local,
        mesh=mesh,
        in_specs=(
            P(("grp", "ep"), None),
            P(("grp", "ep"), None),
            P(("grp", "ep"), None),
            P(("grp", "ep"), None),
            P("ep", None, None),
            P("ep", None, None),
            P("ep", None, None),
        ),
        out_specs=(
            P(("grp", "ep"), None),
            P(("grp", "ep"), None),
            P(("grp", "ep"), None),
            P(("grp", "ep"), None, None),
            P(("grp", "ep"), None, None),
            P(("grp", "ep"), None, None),
        ),
        check_vma=False,
    )
```

```python
import jax
import jax.numpy as jnp
from jax import lax
from jax.experimental import pallas as pl
from jax.experimental.pallas import tpu as pltpu
from jax.sharding import PartitionSpec as P


def assign_slots(route_rows, expert_count):
    flat_ids = route_rows.reshape(-1)
    onehot = (flat_ids[:, None] == jnp.arange(expert_count, dtype=jnp.int32)[None, :]).astype(
        jnp.int32
    )
    ranks = jnp.cumsum(onehot, axis=0) - 1
    return (flat_ids, jnp.sum(onehot * ranks, axis=1))


def expert_forward(rows, gate_w, up_w, down_w):
    gate_pre = jnp.einsum("erl,elf->erf", rows, gate_w, preferred_element_type=jnp.float32)
    up_pre = jnp.einsum("erl,elf->erf", rows, up_w, preferred_element_type=jnp.float32)
    sigma = jax.nn.sigmoid(gate_pre)
    silu_val = gate_pre * sigma
    hidden = (silu_val * up_pre).astype(jnp.bfloat16)
    expert_out = jnp.einsum(
        "erf,efl->erl", hidden, down_w, preferred_element_type=jnp.float32
    ).astype(jnp.bfloat16)
    return (expert_out, (gate_pre, up_pre, sigma, silu_val, hidden))


def expert_backward(rows, grad_out, saved, gate_w, up_w, down_w):
    gate_pre, up_pre, sigma, silu_val, hidden = saved
    grad_down = jnp.einsum(
        "erf,erl->efl", hidden, grad_out, preferred_element_type=jnp.float32
    ).astype(jnp.bfloat16)
    grad_hidden = jnp.einsum("erl,efl->erf", grad_out, down_w, preferred_element_type=jnp.float32)
    grad_gate = (grad_hidden * up_pre * sigma * (1.0 + gate_pre * (1.0 - sigma))).astype(
        jnp.bfloat16
    )
    grad_up = (grad_hidden * silu_val).astype(jnp.bfloat16)
    grad_gw = jnp.einsum(
        "erl,erf->elf", rows, grad_gate, preferred_element_type=jnp.float32
    ).astype(jnp.bfloat16)
    grad_uw = jnp.einsum("erl,erf->elf", rows, grad_up, preferred_element_type=jnp.float32).astype(
        jnp.bfloat16
    )
    grad_rows = (
        jnp.einsum("erf,elf->erl", grad_gate, gate_w, preferred_element_type=jnp.float32)
        + jnp.einsum("erf,elf->erl", grad_up, up_w, preferred_element_type=jnp.float32)
    ).astype(jnp.bfloat16)
    return (grad_rows, grad_gw, grad_uw, grad_down)


def exchanged(latent_in, routes, combine_weights, cotangent, w_gate, w_up, w_down):
    devices_ep = lax.axis_size("ep")
    local_experts = w_gate.shape[0]
    expert_count = local_experts * devices_ep
    tok_count = latent_in.shape[0]
    top_count = routes.shape[1]
    width = latent_in.shape[1]
    capacity = tok_count * top_count * 3 // (2 * expert_count)
    expert_ids, slot_ids = assign_slots(routes, expert_count)
    position = expert_ids * capacity + slot_ids
    repeated = jnp.repeat(latent_in, top_count, axis=0)
    weighted = (combine_weights[:, :, None] * cotangent.astype(jnp.float32)[:, None, :]).astype(
        jnp.bfloat16
    )
    send_rows = jnp.zeros((expert_count * capacity, width), jnp.bfloat16).at[position].set(repeated)
    send_rows = send_rows.reshape(expert_count, capacity, width)
    send_cot = (
        jnp.zeros((expert_count * capacity, width), jnp.bfloat16)
        .at[position]
        .set(weighted.reshape(-1, width))
    )
    send_cot = send_cot.reshape(expert_count, capacity, width)

    def to_local(received):
        shaped = received.reshape(devices_ep, local_experts, capacity, width)
        return shaped.transpose(1, 0, 2, 3).reshape(local_experts, devices_ep * capacity, width)

    def to_home(local_rows):
        shaped = local_rows.reshape(local_experts, devices_ep, capacity, width)
        return shaped.transpose(1, 0, 2, 3).reshape(expert_count, capacity, width)

    got_rows = lax.all_to_all(send_rows, "ep", split_axis=0, concat_axis=0, tiled=True)
    rows_local = to_local(got_rows)
    expert_out, saved = expert_forward(rows_local, w_gate, w_up, w_down)
    back_out = lax.all_to_all(to_home(expert_out), "ep", split_axis=0, concat_axis=0, tiled=True)
    got_cot = lax.all_to_all(send_cot, "ep", split_axis=0, concat_axis=0, tiled=True)
    grad_rows, grad_gw, grad_uw, grad_down = expert_backward(
        rows_local, to_local(got_cot), saved, w_gate, w_up, w_down
    )
    back_grad = lax.all_to_all(to_home(grad_rows), "ep", split_axis=0, concat_axis=0, tiled=True)
    out_rows = (
        back_out.reshape(-1, width)[position]
        .reshape(tok_count, top_count, width)
        .astype(jnp.float32)
    )
    grad_back = (
        back_grad.reshape(-1, width)[position]
        .reshape(tok_count, top_count, width)
        .astype(jnp.float32)
    )
    combined = jnp.sum(combine_weights[:, :, None] * out_rows, axis=1).astype(jnp.bfloat16)
    grad_combine = jnp.sum(cotangent.astype(jnp.float32)[:, None, :] * out_rows, axis=2)
    grad_latent = jnp.sum(grad_back, axis=1).astype(jnp.bfloat16)
    return (combined, grad_latent, grad_combine, grad_gw, grad_uw, grad_down)


def dot(a, b, dims):
    return lax.dot_general(a, b, (dims, ((), ())), preferred_element_type=jnp.float32)


def swap(value, bit):
    pairs = [(i, i ^ bit) for i in range(lax.axis_size("ep"))]
    return lax.ppermute(value, "ep", pairs)


CORE, SIDE, NEAR, FAR = 1, 2, 4, 8
REACH = (0, NEAR, FAR, NEAR | FAR, SIDE, SIDE | NEAR, SIDE | FAR, SIDE | NEAR | FAR)


def fence(*values):
    return lax.optimization_barrier(values)


def added(a, b):
    return a.astype(jnp.float32) + b.astype(jnp.float32)


def narrow(value):
    return value.astype(jnp.bfloat16)


MIB = 1 << 20


class Fetch:
    def __init__(self, sems):
        self.sems, self.waiting = sems, {}

    def start(self, name, source, target):
        copy = pltpu.make_async_copy(source, target, self.sems.at[len(self.waiting)])
        copy.start()
        self.waiting[name] = [copy, False]

    def wait(self, *names):
        for name in names:
            if not self.waiting[name][1]:
                self.waiting[name][0].wait()
                self.waiting[name][1] = True

    def wait_all(self):
        self.wait(*self.waiting)


def kernel(body, outs, scratch, copies, flops, *operands, scalar=None):
    moved = sum(v.size * v.dtype.itemsize for v in (*operands, *outs))
    in_specs = [pl.BlockSpec(memory_space=pl.ANY)] * len(operands)
    if scalar is not None:
        operands = (scalar, *operands)
        in_specs = [pl.BlockSpec(memory_space=pltpu.SMEM), *in_specs]
    return pl.pallas_call(
        body,
        out_shape=outs,
        in_specs=in_specs,
        out_specs=[pl.BlockSpec(memory_space=pl.ANY)] * len(outs),
        scratch_shapes=[*scratch, pltpu.SemaphoreType.DMA((copies,))],
        compiler_params=pltpu.CompilerParams(vmem_limit_bytes=56 * MIB),
        cost_estimate=pl.CostEstimate(flops=flops, bytes_accessed=moved, transcendentals=0),
    )(*operands)


def shape(rows, columns, dtype):
    return jax.ShapeDtypeStruct((rows, columns), dtype)


def pieces(value):
    first = narrow(value)
    value = value - first.astype(jnp.float32)
    second = narrow(value)
    return first, second, narrow(value - second.astype(jnp.float32))


EXTRA = 16


def both_ways(number, blocks, weights, me, before=None):
    bf16, f32 = jnp.bfloat16, jnp.float32
    count, width = len(blocks), blocks[0].shape[1]
    units, last = weights[0][0].shape[1], before is not None
    tok_count = (blocks[0].shape[0] - (0 if last else EXTRA)) // 2
    every, size = count * tok_count, 2 * tok_count
    lanes = 128
    back = size + (EXTRA if last else 0)
    layout = [[0], [1], [2], [4], [5], [6], [7, 3]]
    place_of = {b: (i, j * back) for i, held in enumerate(layout) for j, b in enumerate(held)}

    def body(me_ref, *refs):
        b_refs, w_refs, refs = refs[:count], refs[count : count + 6], refs[count + 6 :]
        before_refs, refs = (refs[:2], refs[2:]) if last else ((), refs)
        q_refs, refs = refs[: len(layout)], refs[len(layout) :]
        weighted_ref, factor_ref, refs = refs[0], refs[1], refs[2:]
        after_refs, refs = ((), refs) if last else (refs[:2], refs[2:])
        wide_w, down_w, refs = refs[0], refs[1], refs[2:]
        x_buf, c_buf, y_buf, g_buf, weighted_buf, factor_buf, refs = *refs[:6], refs[6:]
        share_buf, inner_buf, wide_buf, extra_buf, sems = refs
        fetch = Fetch(sems)
        w_bufs = []
        for e in range(2):
            for i in (2 * e, 2 * e + 1):
                w_bufs.append(wide_w.at[:, pl.ds(i * units, units)])
            w_bufs.append(down_w.at[pl.ds(e * units, units)])
        me = me_ref[0]
        low = lax.rem(me, 8)
        for b in range(count):
            at = pl.ds(b * tok_count, tok_count)
            fetch.start(("x", b), b_refs[b].at[pl.ds(0, tok_count)], x_buf.at[at])
            if b == 0:
                fetch.start(("w", 0), w_refs[0], w_bufs[0])
        if last:
            fetch.start("share", before_refs[0], share_buf)
            fetch.start("inner", before_refs[1], inner_buf)
        else:
            for b in range(count):
                fetch.start(("s", b), b_refs[b].at[pl.ds(size, EXTRA)], extra_buf.at[b])
        for i in (1, 2):
            fetch.start(("w", i), w_refs[i], w_bufs[i])
        for b in range(count):
            at = pl.ds(b * tok_count, tok_count)
            fetch.start(("c", b), b_refs[b].at[pl.ds(tok_count, tok_count)], c_buf.at[at])
        for i in (3, 4, 5):
            fetch.start(("w", i), w_refs[i], w_bufs[i])

        def returned(b, first, rows):
            ref, offset = place_of[b]
            return q_refs[ref].at[pl.ds(offset + first, rows)]

        def place(e):
            number = lax.rem(low + e, 2) + low - lax.rem(low, 2)
            return pl.ds(pl.multiple_of(number * lanes, lanes), lanes)

        upper = me >= 8
        if last:
            fetch.wait("share", "inner")
        else:
            inner_buf[...] = jnp.zeros((lanes, lanes), f32)
            share_buf[...] = jnp.zeros((lanes, lanes), f32)
            for b in range(count):
                fetch.wait(("s", b))
                wide_buf[b] = extra_buf[b].astype(f32)
            for e in range(2):
                for b in range(count):
                    tile = wide_buf[b, :, place(e)]
                    sums = [tile[r : r + 1] + tile[r + 2 : r + 3] + tile[r + 4 : r + 5] for r in (0, 1)]
                    row = e * count + b
                    share_buf[row : row + 1, :] = jnp.where(upper, sums[1], sums[0])
            share_buf[...] = share_buf[...].T

        half = slice(number * tok_count, (number + 1) * tok_count)
        fetch.wait(*[("x", b) for b in range(count)])
        x = x_buf[...]
        for e in range(2):
            columns = slice(e * units, (e + 1) * units)
            fetch.wait(("w", 3 * e))
            gate = dot(x, wide_w[:, 2 * e * units : (2 * e + 1) * units], ((1,), (0,)))
            fetch.wait(("w", 3 * e + 1))
            up = dot(x, wide_w[:, (2 * e + 1) * units : (2 * e + 2) * units], ((1,), (0,)))
            fetch.wait(("w", 3 * e + 2))
            if e == 0:
                fetch.wait(*[("c", b) for b in range(count)])
            plain = dot(c_buf[...], down_w[columns, :], ((1,), (1,)))
            sigma = jax.nn.sigmoid(gate)
            silu_val = gate * sigma
            hidden = silu_val * up
            part = [share_buf[half, e * count + b : e * count + b + 1] for b in range(count)]
            part = jnp.concatenate(part, axis=0)
            weighted_buf[:, columns] = (part * hidden).astype(bf16)
            inner = jnp.sum(hidden * plain, axis=1, keepdims=True)
            for b in range(count):
                value = inner[b * tok_count : (b + 1) * tok_count]
                inner_buf[half, e * count + b : e * count + b + 1] = value
            grad_hidden = part * plain
            grad_gate = (grad_hidden * up * (sigma * (1.0 + gate * (1.0 - sigma)))).astype(bf16)
            grad_up = (grad_hidden * silu_val).astype(bf16)
            factor_buf[:, 2 * e * units : (2 * e + 1) * units] = grad_gate
            factor_buf[:, (2 * e + 1) * units : (2 * e + 2) * units] = grad_up
        fetch.start("weighted", weighted_buf, weighted_ref)
        fetch.start("factor", factor_buf, factor_ref)
        y_buf[...] = dot(weighted_buf[...], down_w[...], ((1,), (0,))).astype(bf16)
        for b in range(count):
            at = pl.ds(b * tok_count, tok_count)
            fetch.start(("y", b), y_buf.at[at], returned(b, 0, tok_count))
        g_buf[...] = dot(factor_buf[...], wide_w[...], ((1,), (1,))).astype(bf16)
        for b in range(count):
            at = pl.ds(b * tok_count, tok_count)
            fetch.start(("g", b), g_buf.at[at], returned(b, tok_count, tok_count))
        if last:
            wide_buf[...] = jnp.zeros((count, EXTRA, width), f32)
            inner_buf[...] = inner_buf[...].T
            for e in range(2):
                for b in range(count):
                    row = e * count + b
                    value, lines = inner_buf[row : row + 1, :], []
                    for _ in range(3):
                        piece = value.astype(bf16).astype(f32)
                        lines += [jnp.where(upper, 0.0, piece), jnp.where(upper, piece, 0.0)]
                        value = value - piece
                    lines += [jnp.zeros((2, lanes), f32)]
                    wide_buf[b, 0:8, place(e)] = jnp.concatenate(lines, axis=0)
            for b in range(count):
                extra_buf[b] = wide_buf[b].astype(bf16)
                fetch.start(("i", b), extra_buf.at[b], returned(b, size, EXTRA))
        else:
            fetch.start("share", share_buf, after_refs[0])
            fetch.start("inner", inner_buf, after_refs[1])
        fetch.wait_all()

    outs = [shape(len(held) * back, width, bf16) for held in layout]
    outs += [shape(every, 2 * units, bf16), shape(every, 4 * units, bf16)]
    small = shape(lanes, lanes, f32)
    operands = (*blocks, *weights[0], *weights[1])
    if last:
        operands += before
    else:
        outs += [small, small]
    scratch = [pltpu.VMEM((width, 4 * units), bf16), pltpu.VMEM((2 * units, width), bf16)]
    scratch += [pltpu.VMEM((every, width), bf16)] * 4
    scratch += [pltpu.VMEM((every, 2 * units), bf16), pltpu.VMEM((every, 4 * units), bf16)]
    scratch += [pltpu.VMEM(small.shape, f32)] * 2
    scratch += [pltpu.VMEM((count, EXTRA, width), f32), pltpu.VMEM((count, EXTRA, width), bf16)]
    flops = 24 * every * width * units
    copies = 5 * count + 6 + 2 + 2
    outs = kernel(body, outs, scratch, copies, flops, *operands, scalar=me)
    return outs[: len(layout)], outs[len(layout) :]


def weight_grads(expert, blocks, factors, away=None):
    bf16 = jnp.bfloat16
    parts, count, width = len(blocks), len(blocks[0]), blocks[0][0].shape[1]
    each = factors[0][0].shape[0]
    tok_count, every, units = each // count, each * parts, factors[0][0].shape[1] // 2
    extra = 0 if away is None else 1

    def body(*refs):
        b_refs, refs = refs[: parts * count], refs[parts * count :]
        f_refs, refs = refs[: 2 * parts], refs[2 * parts :]
        away_refs, out_refs, refs = refs[:extra], refs[extra : 3 * extra + 1], refs[3 * extra + 1 :]
        x_buf, c_buf, weighted_buf, factor_buf, *bufs, sems = refs
        away_bufs, out_bufs = bufs[:extra], bufs[extra:]
        fetch = Fetch(sems)
        names = range(parts * count)
        for i in names:
            at = pl.ds(i * tok_count, tok_count)
            fetch.start(("x", i), b_refs[i].at[pl.ds(0, tok_count)], x_buf.at[at])
        for p in range(parts):
            at = pl.ds(p * each, each)
            lanes = pl.ds(2 * expert * units, 2 * units)
            fetch.start(("f", p), f_refs[2 * p + 1].at[:, lanes], factor_buf.at[at])
        if extra:
            fetch.start("away", away_refs[0], away_bufs[0])
        for p in range(parts):
            at = pl.ds(p * each, each)
            lanes = pl.ds(expert * units, units)
            fetch.start(("w", p), f_refs[2 * p].at[:, lanes], weighted_buf.at[at])
        for i in names:
            at = pl.ds(i * tok_count, tok_count)
            fetch.start(("c", i), b_refs[i].at[pl.ds(tok_count, tok_count)], c_buf.at[at])
        fetch.wait(*[("x", i) for i in names], *[("f", p) for p in range(parts)])
        for number in range(3):
            if number < 2:
                left, right = x_buf, factor_buf[:, number * units : (number + 1) * units]
                columns, into = slice(number * units, (number + 1) * units), slice(0, width)
            else:
                fetch.wait(*[("c", i) for i in names], *[("w", p) for p in range(parts)])
                left, right = weighted_buf, c_buf[...]
                columns, into = slice(0, width), slice(width, width + units)
            for start in range(0, into.stop - into.start, units):
                value = dot(left[:, start : start + units], right, ((0,), (0,)))
                at = slice(into.start + start, into.start + start + units)
                if not extra:
                    out_bufs[0][at, columns] = value.astype(bf16)
                else:
                    fetch.wait("away")
                    value = value + away_bufs[0][at, columns].astype(jnp.float32)
                    out_bufs[number][start : start + units, :] = value.astype(bf16)
                    block = out_bufs[number].at[start : start + units]
                    target = out_refs[number].at[start : start + units]
                    fetch.start(("out", number, start), block, target)
            if not extra and number:
                at = pl.ds(into.start, into.stop - into.start)
                fetch.start(("out", number), out_bufs[0].at[at], out_refs[0].at[at])
        fetch.wait_all()

    flops = 6 * every * width * units
    operands = (*[b for part in blocks for b in part], *[f for part in factors for f in part])
    scratch = [pltpu.VMEM((every, width), bf16)] * 2
    scratch += [pltpu.VMEM((every, units), bf16), pltpu.VMEM((every, 2 * units), bf16)]
    packed = shape(width + units, width, bf16)
    if away is None:
        outs = [packed]
        scratch += [pltpu.VMEM(packed.shape, bf16)]
    else:
        operands += (away,)
        outs = [shape(width, units, bf16)] * 2 + [shape(units, width, bf16)]
        scratch += [pltpu.VMEM(v.shape, bf16) for v in (packed, *outs)]
    copies = 2 * parts * count + 2 * parts + 1 + 2 * -(-width // units) + 1
    outs = kernel(body, outs, scratch, copies, flops, *operands)
    return outs if extra else outs[0]


def paired(latent_in, routes, combine_weights, cotangent, w_gate, w_up, w_down):
    f32 = jnp.float32
    devices_ep, tok_count, width = lax.axis_size("ep"), *latent_in.shape
    me = lax.axis_index("ep")
    mid = tok_count // 2
    experts = jnp.arange(devices_ep, dtype=jnp.int32)
    own = (w_gate[0], w_up[0], w_down[0])

    chosen = routes[None, :, :] == experts[:, None, None]
    share = jnp.sum(jnp.where(chosen, combine_weights[None, :, :], 0.0), axis=2)
    lines = jnp.stack(pieces(share)).reshape(-1, width)
    lines = jnp.pad(lines, ((0, EXTRA - lines.shape[0]), (0, 0)))
    a0 = jnp.concatenate([latent_in[:mid], cotangent[:mid], lines], axis=0)
    b0 = jnp.concatenate([latent_in[mid:], cotangent[mid:]], axis=0)
    gate_w = swap(own[0], CORE)
    a0, b0, gate_w, own = fence(a0, b0, gate_w, own)

    a2, a4, b4, a1 = swap(a0, FAR), swap(a0, SIDE), swap(b0, SIDE), swap(a0, NEAR)
    up_w = swap(own[1], CORE)
    a1, a4, a2, b4, up_w, b0, own = fence(a1, a4, a2, b4, up_w, b0, own)
    a5, a6, a3, b2 = swap(a1, SIDE), swap(a2, SIDE), swap(a2, NEAR), swap(b0, FAR)
    down_w = swap(own[2], CORE)
    (a3,) = fence(a3)
    a7 = swap(a3, SIDE)
    b2, a5, a6 = fence(b2, a5, a6)
    b6, b1, b3 = swap(b2, SIDE), swap(b0, NEAR), swap(b2, NEAR)
    a7, b1, b6 = fence(a7, b1, b6)
    b5, b7 = swap(b1, SIDE), swap(b6, NEAR)
    weights, me = (own, (gate_w, up_w, down_w)), me.astype(jnp.int32).reshape(1)
    a = [a0, a1, a2, a3, a4, a5, a6, a7]
    q, (*a_factors, shares, inners) = both_ways(0, a, weights, me)
    q0, q1, q2, q4, q5, q6, q73 = q
    q73, q5, shares, inners, b5, b7 = fence(q73, q5, shares, inners, b5, b7)
    r73, r5 = swap(q73, NEAR), swap(q5, SIDE)
    b = [b0, b1, b2, b3, b4, b5, b6, b7]
    p, b_factors = both_ways(1, b, weights, me, (shares, inners))
    p0, p1, p2, p4, p5, p6, p73 = p
    r73, r5, q6, q4, p73, p6, p5, p4, b_factors = fence(r73, r5, q6, q4, p73, p6, p5, p4, b_factors)
    factors, size = (a_factors, b_factors), q6.shape[0]
    q6, q2, q1 = narrow(added(q6, r73[:size])), added(q2, r73[size:]), narrow(added(q1, r5))
    q6, p73, p5, q1 = fence(q6, p73, p5, q1)
    r6, r73, r5 = swap(q6, SIDE), swap(p73, NEAR), swap(p5, SIDE)
    away = weight_grads(1, (a, b), factors)
    r6, r5, away = fence(r6, r5, away)
    q2 = swap(narrow(q2 + r6.astype(f32)), FAR)
    size = p6.shape[0]
    p1 = narrow(added(p1, r5))
    p6, r73, away, q1, p1 = fence(p6, r73, away, q1, p1)
    p6 = narrow(added(p6, r73[:size]))
    p6, away, q1, q4 = fence(p6, away, q1, q4)
    r6, q1, q4, away = swap(p6, SIDE), swap(q1, NEAR), swap(q4, SIDE), swap(away, CORE)
    r6, p1, p4 = fence(r6, p1, p4)
    p2 = narrow(added(p2, r73[size:]) + r6.astype(f32))
    p2, p1, p4, away = fence(p2, p1, p4, away)
    p2, p1, p4 = swap(p2, FAR), swap(p1, NEAR), swap(p4, SIDE)
    grad_w = weight_grads(0, (a, b), factors, away)
    p2, p1, p4, q4, q2, q1, grad_w = fence(p2, p1, p4, q4, q2, q1, grad_w)

    q = added(q0, q4) + added(q1, q2)
    p = added(p0, p4) + added(p1, p2)
    combined = narrow(jnp.concatenate([q[:mid], p[:mid]], axis=0))
    grad_latent = narrow(jnp.concatenate([q[mid : 2 * mid], p[mid : 2 * mid]], axis=0))
    inner = p[2 * mid :].reshape(-1, devices_ep, tok_count)[:3].sum(axis=0)
    grad_combine = jnp.sum(jnp.where(chosen, inner[:, :, None], 0.0), axis=0)
    return (combined, grad_latent, grad_combine, *[v[None] for v in grad_w])


def local(latent_in, routes, combine_weights, cotangent, w_gate, w_up, w_down):
    plan = paired if w_gate.shape[0] == 1 and lax.axis_size("ep") == 2 * len(REACH) else exchanged
    return plan(latent_in, routes, combine_weights, cotangent, w_gate, w_up, w_down)


def solution(mesh):
    return jax.shard_map(
        local,
        mesh=mesh,
        in_specs=(
            P(("grp", "ep"), None),
            P(("grp", "ep"), None),
            P(("grp", "ep"), None),
            P(("grp", "ep"), None),
            P("ep", None, None),
            P("ep", None, None),
            P("ep", None, None),
        ),
        out_specs=(
            P(("grp", "ep"), None),
            P(("grp", "ep"), None),
            P(("grp", "ep"), None),
            P(("grp", "ep"), None, None),
            P(("grp", "ep"), None, None),
            P(("grp", "ep"), None, None),
        ),
        check_vma=False,
    )
```

```python
import jax
import jax.numpy as jnp
from jax import lax
from jax.experimental import pallas as pl
from jax.experimental.pallas import tpu as pltpu
from jax.sharding import PartitionSpec as P


def assign_slots(route_rows, expert_count):
    flat_ids = route_rows.reshape(-1)
    onehot = (flat_ids[:, None] == jnp.arange(expert_count, dtype=jnp.int32)[None, :]).astype(
        jnp.int32
    )
    ranks = jnp.cumsum(onehot, axis=0) - 1
    return (flat_ids, jnp.sum(onehot * ranks, axis=1))


def expert_forward(rows, gate_w, up_w, down_w):
    gate_pre = jnp.einsum("erl,elf->erf", rows, gate_w, preferred_element_type=jnp.float32)
    up_pre = jnp.einsum("erl,elf->erf", rows, up_w, preferred_element_type=jnp.float32)
    sigma = jax.nn.sigmoid(gate_pre)
    silu_val = gate_pre * sigma
    hidden = (silu_val * up_pre).astype(jnp.bfloat16)
    expert_out = jnp.einsum(
        "erf,efl->erl", hidden, down_w, preferred_element_type=jnp.float32
    ).astype(jnp.bfloat16)
    return (expert_out, (gate_pre, up_pre, sigma, silu_val, hidden))


def expert_backward(rows, grad_out, saved, gate_w, up_w, down_w):
    gate_pre, up_pre, sigma, silu_val, hidden = saved
    grad_down = jnp.einsum(
        "erf,erl->efl", hidden, grad_out, preferred_element_type=jnp.float32
    ).astype(jnp.bfloat16)
    grad_hidden = jnp.einsum("erl,efl->erf", grad_out, down_w, preferred_element_type=jnp.float32)
    grad_gate = (grad_hidden * up_pre * sigma * (1.0 + gate_pre * (1.0 - sigma))).astype(
        jnp.bfloat16
    )
    grad_up = (grad_hidden * silu_val).astype(jnp.bfloat16)
    grad_gw = jnp.einsum(
        "erl,erf->elf", rows, grad_gate, preferred_element_type=jnp.float32
    ).astype(jnp.bfloat16)
    grad_uw = jnp.einsum("erl,erf->elf", rows, grad_up, preferred_element_type=jnp.float32).astype(
        jnp.bfloat16
    )
    grad_rows = (
        jnp.einsum("erf,elf->erl", grad_gate, gate_w, preferred_element_type=jnp.float32)
        + jnp.einsum("erf,elf->erl", grad_up, up_w, preferred_element_type=jnp.float32)
    ).astype(jnp.bfloat16)
    return (grad_rows, grad_gw, grad_uw, grad_down)


def exchanged(latent_in, routes, combine_weights, cotangent, w_gate, w_up, w_down):
    devices_ep = lax.axis_size("ep")
    local_experts = w_gate.shape[0]
    expert_count = local_experts * devices_ep
    tok_count = latent_in.shape[0]
    top_count = routes.shape[1]
    width = latent_in.shape[1]
    capacity = tok_count * top_count * 3 // (2 * expert_count)
    expert_ids, slot_ids = assign_slots(routes, expert_count)
    position = expert_ids * capacity + slot_ids
    repeated = jnp.repeat(latent_in, top_count, axis=0)
    weighted = (combine_weights[:, :, None] * cotangent.astype(jnp.float32)[:, None, :]).astype(
        jnp.bfloat16
    )
    send_rows = jnp.zeros((expert_count * capacity, width), jnp.bfloat16).at[position].set(repeated)
    send_rows = send_rows.reshape(expert_count, capacity, width)
    send_cot = (
        jnp.zeros((expert_count * capacity, width), jnp.bfloat16)
        .at[position]
        .set(weighted.reshape(-1, width))
    )
    send_cot = send_cot.reshape(expert_count, capacity, width)

    def to_local(received):
        shaped = received.reshape(devices_ep, local_experts, capacity, width)
        return shaped.transpose(1, 0, 2, 3).reshape(local_experts, devices_ep * capacity, width)

    def to_home(local_rows):
        shaped = local_rows.reshape(local_experts, devices_ep, capacity, width)
        return shaped.transpose(1, 0, 2, 3).reshape(expert_count, capacity, width)

    got_rows = lax.all_to_all(send_rows, "ep", split_axis=0, concat_axis=0, tiled=True)
    rows_local = to_local(got_rows)
    expert_out, saved = expert_forward(rows_local, w_gate, w_up, w_down)
    back_out = lax.all_to_all(to_home(expert_out), "ep", split_axis=0, concat_axis=0, tiled=True)
    got_cot = lax.all_to_all(send_cot, "ep", split_axis=0, concat_axis=0, tiled=True)
    grad_rows, grad_gw, grad_uw, grad_down = expert_backward(
        rows_local, to_local(got_cot), saved, w_gate, w_up, w_down
    )
    back_grad = lax.all_to_all(to_home(grad_rows), "ep", split_axis=0, concat_axis=0, tiled=True)
    out_rows = (
        back_out.reshape(-1, width)[position]
        .reshape(tok_count, top_count, width)
        .astype(jnp.float32)
    )
    grad_back = (
        back_grad.reshape(-1, width)[position]
        .reshape(tok_count, top_count, width)
        .astype(jnp.float32)
    )
    combined = jnp.sum(combine_weights[:, :, None] * out_rows, axis=1).astype(jnp.bfloat16)
    grad_combine = jnp.sum(cotangent.astype(jnp.float32)[:, None, :] * out_rows, axis=2)
    grad_latent = jnp.sum(grad_back, axis=1).astype(jnp.bfloat16)
    return (combined, grad_latent, grad_combine, grad_gw, grad_uw, grad_down)


def dot(a, b, dims):
    return lax.dot_general(a, b, (dims, ((), ())), preferred_element_type=jnp.float32)


def swap(value, bit):
    pairs = [(i, i ^ bit) for i in range(lax.axis_size("ep"))]
    return lax.ppermute(value, "ep", pairs)


CORE, SIDE, NEAR, FAR = 1, 2, 4, 8
REACH = (0, NEAR, FAR, NEAR | FAR, SIDE, SIDE | NEAR, SIDE | FAR, SIDE | NEAR | FAR)


def fence(*values):
    return lax.optimization_barrier(values)


def added(a, b):
    return a.astype(jnp.float32) + b.astype(jnp.float32)


def narrow(value):
    return value.astype(jnp.bfloat16)


MIB = 1 << 20


class Fetch:
    def __init__(self, sems):
        self.sems, self.waiting = sems, {}

    def start(self, name, source, target):
        copy = pltpu.make_async_copy(source, target, self.sems.at[len(self.waiting)])
        copy.start()
        self.waiting[name] = [copy, False]

    def wait(self, *names):
        for name in names:
            if not self.waiting[name][1]:
                self.waiting[name][0].wait()
                self.waiting[name][1] = True

    def wait_all(self):
        self.wait(*self.waiting)


def kernel(body, outs, scratch, copies, flops, *operands, scalar=None):
    moved = sum(v.size * v.dtype.itemsize for v in (*operands, *outs))
    in_specs = [pl.BlockSpec(memory_space=pl.ANY)] * len(operands)
    if scalar is not None:
        operands = (scalar, *operands)
        in_specs = [pl.BlockSpec(memory_space=pltpu.SMEM), *in_specs]
    return pl.pallas_call(
        body,
        out_shape=outs,
        in_specs=in_specs,
        out_specs=[pl.BlockSpec(memory_space=pl.ANY)] * len(outs),
        scratch_shapes=[*scratch, pltpu.SemaphoreType.DMA((copies,))],
        compiler_params=pltpu.CompilerParams(vmem_limit_bytes=56 * MIB),
        cost_estimate=pl.CostEstimate(flops=flops, bytes_accessed=moved, transcendentals=0),
    )(*operands)


def shape(rows, columns, dtype):
    return jax.ShapeDtypeStruct((rows, columns), dtype)


def pieces(value):
    first = narrow(value)
    value = value - first.astype(jnp.float32)
    second = narrow(value)
    return first, second, narrow(value - second.astype(jnp.float32))


EXTRA = 16


def both_ways(number, blocks, weights, me, before=None):
    bf16, f32 = jnp.bfloat16, jnp.float32
    count, width = len(blocks), blocks[0].shape[1]
    units, last = weights[0][0].shape[1], before is not None
    tok_count = (blocks[0].shape[0] - (0 if last else EXTRA)) // 2
    every, size = count * tok_count, 2 * tok_count
    lanes = 128
    back = size + (EXTRA if last else 0)
    layout = [[0], [1], [2], [4], [5], [6], [7, 3]]
    place_of = {b: (i, j * back) for i, held in enumerate(layout) for j, b in enumerate(held)}

    def body(me_ref, *refs):
        b_refs, w_refs, refs = refs[:count], refs[count : count + 6], refs[count + 6 :]
        before_refs, refs = (refs[:2], refs[2:]) if last else ((), refs)
        q_refs, refs = refs[: len(layout)], refs[len(layout) :]
        weighted_ref, factor_ref, refs = refs[0], refs[1], refs[2:]
        after_refs, refs = ((), refs) if last else (refs[:2], refs[2:])
        wide_w, down_w, refs = refs[0], refs[1], refs[2:]
        x_buf, c_buf, y_buf, g_buf, weighted_buf, factor_buf, refs = *refs[:6], refs[6:]
        share_buf, inner_buf, wide_buf, extra_buf, sems = refs
        fetch = Fetch(sems)
        w_bufs = []
        for e in range(2):
            for i in (2 * e, 2 * e + 1):
                w_bufs.append(wide_w.at[:, pl.ds(i * units, units)])
            w_bufs.append(down_w.at[pl.ds(e * units, units)])
        me = me_ref[0]
        low = lax.rem(me, 8)
        for b in range(count):
            at = pl.ds(b * tok_count, tok_count)
            fetch.start(("x", b), b_refs[b].at[pl.ds(0, tok_count)], x_buf.at[at])
            if b == 0:
                fetch.start(("w", 0), w_refs[0], w_bufs[0])
        if last:
            fetch.start("share", before_refs[0], share_buf)
            fetch.start("inner", before_refs[1], inner_buf)
        else:
            for b in range(count):
                fetch.start(("s", b), b_refs[b].at[pl.ds(size, EXTRA)], extra_buf.at[b])
        for i in (1, 2):
            fetch.start(("w", i), w_refs[i], w_bufs[i])
        for b in range(count):
            at = pl.ds(b * tok_count, tok_count)
            fetch.start(("c", b), b_refs[b].at[pl.ds(tok_count, tok_count)], c_buf.at[at])
        for i in (3, 4, 5):
            fetch.start(("w", i), w_refs[i], w_bufs[i])

        def returned(b, first, rows):
            ref, offset = place_of[b]
            return q_refs[ref].at[pl.ds(offset + first, rows)]

        def place(e):
            number = lax.rem(low + e, 2) + low - lax.rem(low, 2)
            return pl.ds(pl.multiple_of(number * lanes, lanes), lanes)

        upper = me >= 8
        if last:
            fetch.wait("share", "inner")
        else:
            inner_buf[...] = jnp.zeros((lanes, lanes), f32)
            share_buf[...] = jnp.zeros((lanes, lanes), f32)
            for b in range(count):
                fetch.wait(("s", b))
                wide_buf[b] = extra_buf[b].astype(f32)
            for e in range(2):
                for b in range(count):
                    tile = wide_buf[b, :, place(e)]
                    sums = [tile[r : r + 1] + tile[r + 2 : r + 3] + tile[r + 4 : r + 5] for r in (0, 1)]
                    row = e * count + b
                    share_buf[row : row + 1, :] = jnp.where(upper, sums[1], sums[0])
            share_buf[...] = share_buf[...].T

        half = slice(number * tok_count, (number + 1) * tok_count)
        fetch.wait(*[("x", b) for b in range(count)])
        x = x_buf[...]
        for e in range(2):
            columns = slice(e * units, (e + 1) * units)
            fetch.wait(("w", 3 * e))
            gate = dot(x, wide_w[:, 2 * e * units : (2 * e + 1) * units], ((1,), (0,)))
            fetch.wait(("w", 3 * e + 1))
            up = dot(x, wide_w[:, (2 * e + 1) * units : (2 * e + 2) * units], ((1,), (0,)))
            fetch.wait(("w", 3 * e + 2))
            if e == 0:
                fetch.wait(*[("c", b) for b in range(count)])
            plain = dot(c_buf[...], down_w[columns, :], ((1,), (1,)))
            sigma = jax.nn.sigmoid(gate)
            silu_val = gate * sigma
            hidden = silu_val * up
            part = [share_buf[half, e * count + b : e * count + b + 1] for b in range(count)]
            part = jnp.concatenate(part, axis=0)
            weighted_buf[:, columns] = (part * hidden).astype(bf16)
            inner = jnp.sum(hidden * plain, axis=1, keepdims=True)
            for b in range(count):
                value = inner[b * tok_count : (b + 1) * tok_count]
                inner_buf[half, e * count + b : e * count + b + 1] = value
            grad_hidden = part * plain
            grad_gate = (grad_hidden * up * (sigma * (1.0 + gate * (1.0 - sigma)))).astype(bf16)
            grad_up = (grad_hidden * silu_val).astype(bf16)
            factor_buf[:, 2 * e * units : (2 * e + 1) * units] = grad_gate
            factor_buf[:, (2 * e + 1) * units : (2 * e + 2) * units] = grad_up
        fetch.start("weighted", weighted_buf, weighted_ref)
        fetch.start("factor", factor_buf, factor_ref)
        y_buf[...] = dot(weighted_buf[...], down_w[...], ((1,), (0,))).astype(bf16)
        for b in range(count):
            at = pl.ds(b * tok_count, tok_count)
            fetch.start(("y", b), y_buf.at[at], returned(b, 0, tok_count))
        g_buf[...] = dot(factor_buf[...], wide_w[...], ((1,), (1,))).astype(bf16)
        for b in range(count):
            at = pl.ds(b * tok_count, tok_count)
            fetch.start(("g", b), g_buf.at[at], returned(b, tok_count, tok_count))
        if last:
            wide_buf[...] = jnp.zeros((count, EXTRA, width), f32)
            inner_buf[...] = inner_buf[...].T
            for e in range(2):
                for b in range(count):
                    row = e * count + b
                    value, lines = inner_buf[row : row + 1, :], []
                    for _ in range(3):
                        piece = value.astype(bf16).astype(f32)
                        lines += [jnp.where(upper, 0.0, piece), jnp.where(upper, piece, 0.0)]
                        value = value - piece
                    lines += [jnp.zeros((2, lanes), f32)]
                    wide_buf[b, 0:8, place(e)] = jnp.concatenate(lines, axis=0)
            for b in range(count):
                extra_buf[b] = wide_buf[b].astype(bf16)
                fetch.start(("i", b), extra_buf.at[b], returned(b, size, EXTRA))
        else:
            fetch.start("share", share_buf, after_refs[0])
            fetch.start("inner", inner_buf, after_refs[1])
        fetch.wait_all()

    outs = [shape(len(held) * back, width, bf16) for held in layout]
    outs += [shape(every, 2 * units, bf16), shape(every, 4 * units, bf16)]
    small = shape(lanes, lanes, f32)
    operands = (*blocks, *weights[0], *weights[1])
    if last:
        operands += before
    else:
        outs += [small, small]
    scratch = [pltpu.VMEM((width, 4 * units), bf16), pltpu.VMEM((2 * units, width), bf16)]
    scratch += [pltpu.VMEM((every, width), bf16)] * 4
    scratch += [pltpu.VMEM((every, 2 * units), bf16), pltpu.VMEM((every, 4 * units), bf16)]
    scratch += [pltpu.VMEM(small.shape, f32)] * 2
    scratch += [pltpu.VMEM((count, EXTRA, width), f32), pltpu.VMEM((count, EXTRA, width), bf16)]
    flops = 24 * every * width * units
    copies = 5 * count + 6 + 2 + 2
    outs = kernel(body, outs, scratch, copies, flops, *operands, scalar=me)
    return outs[: len(layout)], outs[len(layout) :]


def weight_grads(expert, blocks, factors, away=None, sums=()):
    bf16 = jnp.bfloat16
    parts, count, width = len(blocks), len(blocks[0]), blocks[0][0].shape[1]
    each = factors[0][0].shape[0]
    tok_count, every, units = each // count, each * parts, factors[0][0].shape[1] // 2
    extra = 0 if away is None else 1

    def body(*refs):
        b_refs, refs = refs[: parts * count], refs[parts * count :]
        f_refs, refs = refs[: 2 * parts], refs[2 * parts :]
        away_refs, sum_refs, refs = refs[:extra], refs[extra : extra + len(sums)], refs[extra + len(sums) :]
        out_refs, refs = refs[: len(outs)], refs[len(outs) :]
        x_buf, c_buf, weighted_buf, factor_buf, *bufs, sems = refs
        away_bufs, out_bufs = bufs[:extra], bufs[extra : 3 * extra + 1]
        sum_bufs = bufs[3 * extra + 1 :]
        fetch = Fetch(sems)
        names = range(parts * count)
        for i in names:
            at = pl.ds(i * tok_count, tok_count)
            fetch.start(("x", i), b_refs[i].at[pl.ds(0, tok_count)], x_buf.at[at])
        for p in range(parts):
            at = pl.ds(p * each, each)
            lanes = pl.ds(2 * expert * units, 2 * units)
            fetch.start(("f", p), f_refs[2 * p + 1].at[:, lanes], factor_buf.at[at])
        if extra:
            fetch.start("away", away_refs[0], away_bufs[0])
        for p in range(parts):
            at = pl.ds(p * each, each)
            lanes = pl.ds(expert * units, units)
            fetch.start(("w", p), f_refs[2 * p].at[:, lanes], weighted_buf.at[at])
        for i in names:
            at = pl.ds(i * tok_count, tok_count)
            fetch.start(("c", i), b_refs[i].at[pl.ds(tok_count, tok_count)], c_buf.at[at])
        for i, ref in enumerate(sum_refs):
            fetch.start(("sum", i), ref, sum_bufs[i])
        fetch.wait(*[("x", i) for i in names], *[("f", p) for p in range(parts)])
        for number in range(3):
            if number < 2:
                left, right = x_buf, factor_buf[:, number * units : (number + 1) * units]
                columns, into = slice(number * units, (number + 1) * units), slice(0, width)
            else:
                fetch.wait(*[("c", i) for i in names], *[("w", p) for p in range(parts)])
                left, right = weighted_buf, c_buf[...]
                columns, into = slice(0, width), slice(width, width + units)
            for start in range(0, into.stop - into.start, units):
                value = dot(left[:, start : start + units], right, ((0,), (0,)))
                at = slice(into.start + start, into.start + start + units)
                if not extra:
                    out_bufs[0][at, columns] = value.astype(bf16)
                else:
                    fetch.wait("away")
                    value = value + away_bufs[0][at, columns].astype(jnp.float32)
                    out_bufs[number][start : start + units, :] = value.astype(bf16)
                    block = out_bufs[number].at[start : start + units]
                    target = out_refs[number].at[start : start + units]
                    fetch.start(("out", number, start), block, target)
            if not extra and number:
                at = pl.ds(into.start, into.stop - into.start)
                fetch.start(("out", number), out_bufs[0].at[at], out_refs[0].at[at])
        if extra:
            fetch.wait(*[("sum", i) for i in range(len(sums))])
            total = sum(buf[...].astype(jnp.float32) for buf in sum_bufs[: len(sums)])
            sum_bufs[-1][...] = total.astype(bf16)
            for i, ref in enumerate(out_refs[3:]):
                half = sum_bufs[-1].at[pl.ds(i * tok_count, tok_count)]
                fetch.start(("half", i), half, ref.at[pl.ds(0, tok_count)])
        fetch.wait_all()

    flops = 6 * every * width * units
    operands = (*[b for part in blocks for b in part], *[f for part in factors for f in part])
    scratch = [pltpu.VMEM((every, width), bf16)] * 2
    scratch += [pltpu.VMEM((every, units), bf16), pltpu.VMEM((every, 2 * units), bf16)]
    packed = shape(width + units, width, bf16)
    if away is None:
        outs = [packed]
        scratch += [pltpu.VMEM(packed.shape, bf16)]
    else:
        operands += (away, *sums)
        outs = [shape(width, units, bf16)] * 2 + [shape(units, width, bf16)]
        scratch += [pltpu.VMEM(v.shape, bf16) for v in (packed, *outs, *sums, sums[0])]
        outs += [shape(*sums[0].shape, bf16)] * 2
    copies = 2 * parts * count + 2 * parts + 1 + 2 * -(-width // units) + 1 + len(sums) + 2
    outs = kernel(body, outs, scratch, copies, flops, *operands)
    return outs if extra else outs[0]


def paired(latent_in, routes, combine_weights, cotangent, w_gate, w_up, w_down):
    f32 = jnp.float32
    devices_ep, tok_count, width = lax.axis_size("ep"), *latent_in.shape
    me = lax.axis_index("ep")
    mid = tok_count // 2
    experts = jnp.arange(devices_ep, dtype=jnp.int32)
    own = (w_gate[0], w_up[0], w_down[0])

    chosen = routes[None, :, :] == experts[:, None, None]
    share = jnp.sum(jnp.where(chosen, combine_weights[None, :, :], 0.0), axis=2)
    lines = jnp.stack(pieces(share)).reshape(-1, width)
    lines = jnp.pad(lines, ((0, EXTRA - lines.shape[0]), (0, 0)))
    a0 = jnp.concatenate([latent_in[:mid], cotangent[:mid], lines], axis=0)
    b0 = jnp.concatenate([latent_in[mid:], cotangent[mid:]], axis=0)
    gate_w = swap(own[0], CORE)
    a0, b0, gate_w, own = fence(a0, b0, gate_w, own)

    a2, a4, b4, a1 = swap(a0, FAR), swap(a0, SIDE), swap(b0, SIDE), swap(a0, NEAR)
    up_w = swap(own[1], CORE)
    a1, a4, a2, b4, up_w, b0, own = fence(a1, a4, a2, b4, up_w, b0, own)
    a5, a6, a3, b2 = swap(a1, SIDE), swap(a2, SIDE), swap(a2, NEAR), swap(b0, FAR)
    down_w = swap(own[2], CORE)
    (a3,) = fence(a3)
    a7 = swap(a3, SIDE)
    b2, a5, a6 = fence(b2, a5, a6)
    b6, b1, b3 = swap(b2, SIDE), swap(b0, NEAR), swap(b2, NEAR)
    a7, b1, b6 = fence(a7, b1, b6)
    b5, b7 = swap(b1, SIDE), swap(b6, NEAR)
    weights, me = (own, (gate_w, up_w, down_w)), me.astype(jnp.int32).reshape(1)
    a = [a0, a1, a2, a3, a4, a5, a6, a7]
    q, (*a_factors, shares, inners) = both_ways(0, a, weights, me)
    q0, q1, q2, q4, q5, q6, q73 = q
    q73, q5, shares, inners, b5, b7 = fence(q73, q5, shares, inners, b5, b7)
    r73, r5 = swap(q73, NEAR), swap(q5, SIDE)
    b = [b0, b1, b2, b3, b4, b5, b6, b7]
    p, b_factors = both_ways(1, b, weights, me, (shares, inners))
    p0, p1, p2, p4, p5, p6, p73 = p
    r73, r5, q6, q4, p73, p6, p5, p4, b_factors = fence(r73, r5, q6, q4, p73, p6, p5, p4, b_factors)
    factors, size = (a_factors, b_factors), q6.shape[0]
    q6, q2, q1 = narrow(added(q6, r73[:size])), added(q2, r73[size:]), narrow(added(q1, r5))
    q6, p73, p5, q1 = fence(q6, p73, p5, q1)
    r6, r73, r5 = swap(q6, SIDE), swap(p73, NEAR), swap(p5, SIDE)
    away = weight_grads(1, (a, b), factors)
    r6, r5, away = fence(r6, r5, away)
    q2 = swap(narrow(q2 + r6.astype(f32)), FAR)
    size = p6.shape[0]
    p1 = narrow(added(p1, r5))
    p6, r73, away, q1, p1 = fence(p6, r73, away, q1, p1)
    p6 = narrow(added(p6, r73[:size]))
    p6, away, q1, q4 = fence(p6, away, q1, q4)
    r6, q1, q4, away = swap(p6, SIDE), swap(q1, NEAR), swap(q4, SIDE), swap(away, CORE)
    r6, p1, p4 = fence(r6, p1, p4)
    p2 = narrow(added(p2, r73[size:]) + r6.astype(f32))
    p2, p1, p4, away = fence(p2, p1, p4, away)
    p2, p1, p4 = swap(p2, FAR), swap(p1, NEAR), swap(p4, SIDE)
    *grad_w, combined, grad_latent = weight_grads(0, (a, b), factors, away, (q0, q4, q1, q2))
    p2, p1, p4, combined, grad_latent = fence(p2, p1, p4, combined, grad_latent)

    p = added(p0, p4) + added(p1, p2)
    combined = lax.dynamic_update_slice(combined, narrow(p[:mid]), (mid, 0))
    grad_latent = lax.dynamic_update_slice(grad_latent, narrow(p[mid : 2 * mid]), (mid, 0))
    inner = p[2 * mid :].reshape(-1, devices_ep, tok_count)[:3].sum(axis=0)
    grad_combine = jnp.sum(jnp.where(chosen, inner[:, :, None], 0.0), axis=0)
    return (combined, grad_latent, grad_combine, *[v[None] for v in grad_w])


def local(latent_in, routes, combine_weights, cotangent, w_gate, w_up, w_down):
    plan = paired if w_gate.shape[0] == 1 and lax.axis_size("ep") == 2 * len(REACH) else exchanged
    return plan(latent_in, routes, combine_weights, cotangent, w_gate, w_up, w_down)


def solution(mesh):
    return jax.shard_map(
        local,
        mesh=mesh,
        in_specs=(
            P(("grp", "ep"), None),
            P(("grp", "ep"), None),
            P(("grp", "ep"), None),
            P(("grp", "ep"), None),
            P("ep", None, None),
            P("ep", None, None),
            P("ep", None, None),
        ),
        out_specs=(
            P(("grp", "ep"), None),
            P(("grp", "ep"), None),
            P(("grp", "ep"), None),
            P(("grp", "ep"), None, None),
            P(("grp", "ep"), None, None),
            P(("grp", "ep"), None, None),
        ),
        check_vma=False,
    )
```

```python
import jax
import jax.numpy as jnp
from jax import lax
from jax.experimental import pallas as pl
from jax.experimental.pallas import tpu as pltpu
from jax.sharding import PartitionSpec as P


def assign_slots(route_rows, expert_count):
    flat_ids = route_rows.reshape(-1)
    onehot = (flat_ids[:, None] == jnp.arange(expert_count, dtype=jnp.int32)[None, :]).astype(
        jnp.int32
    )
    ranks = jnp.cumsum(onehot, axis=0) - 1
    return (flat_ids, jnp.sum(onehot * ranks, axis=1))


def expert_forward(rows, gate_w, up_w, down_w):
    gate_pre = jnp.einsum("erl,elf->erf", rows, gate_w, preferred_element_type=jnp.float32)
    up_pre = jnp.einsum("erl,elf->erf", rows, up_w, preferred_element_type=jnp.float32)
    sigma = jax.nn.sigmoid(gate_pre)
    silu_val = gate_pre * sigma
    hidden = (silu_val * up_pre).astype(jnp.bfloat16)
    expert_out = jnp.einsum(
        "erf,efl->erl", hidden, down_w, preferred_element_type=jnp.float32
    ).astype(jnp.bfloat16)
    return (expert_out, (gate_pre, up_pre, sigma, silu_val, hidden))


def expert_backward(rows, grad_out, saved, gate_w, up_w, down_w):
    gate_pre, up_pre, sigma, silu_val, hidden = saved
    grad_down = jnp.einsum(
        "erf,erl->efl", hidden, grad_out, preferred_element_type=jnp.float32
    ).astype(jnp.bfloat16)
    grad_hidden = jnp.einsum("erl,efl->erf", grad_out, down_w, preferred_element_type=jnp.float32)
    grad_gate = (grad_hidden * up_pre * sigma * (1.0 + gate_pre * (1.0 - sigma))).astype(
        jnp.bfloat16
    )
    grad_up = (grad_hidden * silu_val).astype(jnp.bfloat16)
    grad_gw = jnp.einsum(
        "erl,erf->elf", rows, grad_gate, preferred_element_type=jnp.float32
    ).astype(jnp.bfloat16)
    grad_uw = jnp.einsum("erl,erf->elf", rows, grad_up, preferred_element_type=jnp.float32).astype(
        jnp.bfloat16
    )
    grad_rows = (
        jnp.einsum("erf,elf->erl", grad_gate, gate_w, preferred_element_type=jnp.float32)
        + jnp.einsum("erf,elf->erl", grad_up, up_w, preferred_element_type=jnp.float32)
    ).astype(jnp.bfloat16)
    return (grad_rows, grad_gw, grad_uw, grad_down)


def exchanged(latent_in, routes, combine_weights, cotangent, w_gate, w_up, w_down):
    devices_ep = lax.axis_size("ep")
    local_experts = w_gate.shape[0]
    expert_count = local_experts * devices_ep
    tok_count = latent_in.shape[0]
    top_count = routes.shape[1]
    width = latent_in.shape[1]
    capacity = tok_count * top_count * 3 // (2 * expert_count)
    expert_ids, slot_ids = assign_slots(routes, expert_count)
    position = expert_ids * capacity + slot_ids
    repeated = jnp.repeat(latent_in, top_count, axis=0)
    weighted = (combine_weights[:, :, None] * cotangent.astype(jnp.float32)[:, None, :]).astype(
        jnp.bfloat16
    )
    send_rows = jnp.zeros((expert_count * capacity, width), jnp.bfloat16).at[position].set(repeated)
    send_rows = send_rows.reshape(expert_count, capacity, width)
    send_cot = (
        jnp.zeros((expert_count * capacity, width), jnp.bfloat16)
        .at[position]
        .set(weighted.reshape(-1, width))
    )
    send_cot = send_cot.reshape(expert_count, capacity, width)

    def to_local(received):
        shaped = received.reshape(devices_ep, local_experts, capacity, width)
        return shaped.transpose(1, 0, 2, 3).reshape(local_experts, devices_ep * capacity, width)

    def to_home(local_rows):
        shaped = local_rows.reshape(local_experts, devices_ep, capacity, width)
        return shaped.transpose(1, 0, 2, 3).reshape(expert_count, capacity, width)

    got_rows = lax.all_to_all(send_rows, "ep", split_axis=0, concat_axis=0, tiled=True)
    rows_local = to_local(got_rows)
    expert_out, saved = expert_forward(rows_local, w_gate, w_up, w_down)
    back_out = lax.all_to_all(to_home(expert_out), "ep", split_axis=0, concat_axis=0, tiled=True)
    got_cot = lax.all_to_all(send_cot, "ep", split_axis=0, concat_axis=0, tiled=True)
    grad_rows, grad_gw, grad_uw, grad_down = expert_backward(
        rows_local, to_local(got_cot), saved, w_gate, w_up, w_down
    )
    back_grad = lax.all_to_all(to_home(grad_rows), "ep", split_axis=0, concat_axis=0, tiled=True)
    out_rows = (
        back_out.reshape(-1, width)[position]
        .reshape(tok_count, top_count, width)
        .astype(jnp.float32)
    )
    grad_back = (
        back_grad.reshape(-1, width)[position]
        .reshape(tok_count, top_count, width)
        .astype(jnp.float32)
    )
    combined = jnp.sum(combine_weights[:, :, None] * out_rows, axis=1).astype(jnp.bfloat16)
    grad_combine = jnp.sum(cotangent.astype(jnp.float32)[:, None, :] * out_rows, axis=2)
    grad_latent = jnp.sum(grad_back, axis=1).astype(jnp.bfloat16)
    return (combined, grad_latent, grad_combine, grad_gw, grad_uw, grad_down)


def dot(a, b, dims):
    return lax.dot_general(a, b, (dims, ((), ())), preferred_element_type=jnp.float32)


def swap(value, bit):
    pairs = [(i, i ^ bit) for i in range(lax.axis_size("ep"))]
    return lax.ppermute(value, "ep", pairs)


CORE, SIDE, NEAR, FAR = 1, 2, 4, 8
REACH = (0, NEAR, FAR, NEAR | FAR, SIDE, SIDE | NEAR, SIDE | FAR, SIDE | NEAR | FAR)


def fence(*values):
    return lax.optimization_barrier(values)


def added(a, b):
    return a.astype(jnp.float32) + b.astype(jnp.float32)


def narrow(value):
    return value.astype(jnp.bfloat16)


MIB = 1 << 20


class Fetch:
    def __init__(self, sems):
        self.sems, self.waiting = sems, {}

    def start(self, name, source, target):
        copy = pltpu.make_async_copy(source, target, self.sems.at[len(self.waiting)])
        copy.start()
        self.waiting[name] = [copy, False]

    def wait(self, *names):
        for name in names:
            if not self.waiting[name][1]:
                self.waiting[name][0].wait()
                self.waiting[name][1] = True

    def wait_all(self):
        self.wait(*self.waiting)


def kernel(body, outs, scratch, copies, flops, *operands, scalar=None):
    moved = sum(v.size * v.dtype.itemsize for v in (*operands, *outs))
    in_specs = [pl.BlockSpec(memory_space=pl.ANY)] * len(operands)
    if scalar is not None:
        operands = (scalar, *operands)
        in_specs = [pl.BlockSpec(memory_space=pltpu.SMEM), *in_specs]
    return pl.pallas_call(
        body,
        out_shape=outs,
        in_specs=in_specs,
        out_specs=[pl.BlockSpec(memory_space=pl.ANY)] * len(outs),
        scratch_shapes=[*scratch, pltpu.SemaphoreType.DMA((copies,))],
        compiler_params=pltpu.CompilerParams(vmem_limit_bytes=56 * MIB),
        cost_estimate=pl.CostEstimate(flops=flops, bytes_accessed=moved, transcendentals=0),
    )(*operands)


def shape(rows, columns, dtype):
    return jax.ShapeDtypeStruct((rows, columns), dtype)


def pieces(value):
    first = narrow(value)
    value = value - first.astype(jnp.float32)
    second = narrow(value)
    return first, second, narrow(value - second.astype(jnp.float32))


EXTRA = 16


def both_ways(number, blocks, weights, me, before=None):
    bf16, f32 = jnp.bfloat16, jnp.float32
    count, width = len(blocks), blocks[0].shape[1]
    units, last = weights[0][0].shape[1], before is not None
    tok_count = (blocks[0].shape[0] - (0 if last else EXTRA)) // 2
    every, size = count * tok_count, 2 * tok_count
    lanes = 128
    back = size + (EXTRA if last else 0)
    layout = [[0], [1], [2], [4], [5], [6], [7, 3]]
    place_of = {b: (i, j * back) for i, held in enumerate(layout) for j, b in enumerate(held)}

    def body(me_ref, *refs):
        b_refs, w_refs, refs = refs[:count], refs[count : count + 6], refs[count + 6 :]
        before_refs, refs = (refs[:2], refs[2:]) if last else ((), refs)
        q_refs, refs = refs[: len(layout)], refs[len(layout) :]
        weighted_ref, factor_ref, refs = refs[0], refs[1], refs[2:]
        after_refs, refs = ((), refs) if last else (refs[:2], refs[2:])
        wide_w, down_w, refs = refs[0], refs[1], refs[2:]
        x_buf, c_buf, y_buf, g_buf, weighted_buf, factor_buf, refs = *refs[:6], refs[6:]
        share_buf, inner_buf, wide_buf, extra_buf, sems = refs
        fetch = Fetch(sems)
        w_bufs = []
        for e in range(2):
            for i in (2 * e, 2 * e + 1):
                w_bufs.append(wide_w.at[:, pl.ds(i * units, units)])
            w_bufs.append(down_w.at[pl.ds(e * units, units)])
        me = me_ref[0]
        low = lax.rem(me, 8)
        for b in range(count):
            at = pl.ds(b * tok_count, tok_count)
            fetch.start(("x", b), b_refs[b].at[pl.ds(0, tok_count)], x_buf.at[at])
            if b == 0:
                fetch.start(("w", 0), w_refs[0], w_bufs[0])
        if last:
            fetch.start("share", before_refs[0], share_buf)
            fetch.start("inner", before_refs[1], inner_buf)
        else:
            for b in range(count):
                fetch.start(("s", b), b_refs[b].at[pl.ds(size, EXTRA)], extra_buf.at[b])
        for i in (1, 2):
            fetch.start(("w", i), w_refs[i], w_bufs[i])
        for b in range(count):
            at = pl.ds(b * tok_count, tok_count)
            fetch.start(("c", b), b_refs[b].at[pl.ds(tok_count, tok_count)], c_buf.at[at])
        for i in (3, 4, 5):
            fetch.start(("w", i), w_refs[i], w_bufs[i])

        def returned(b, first, rows):
            ref, offset = place_of[b]
            return q_refs[ref].at[pl.ds(offset + first, rows)]

        def place(e):
            number = lax.rem(low + e, 2) + low - lax.rem(low, 2)
            return pl.ds(pl.multiple_of(number * lanes, lanes), lanes)

        upper = me >= 8
        if last:
            fetch.wait("share", "inner")
        else:
            inner_buf[...] = jnp.zeros((lanes, lanes), f32)
            share_buf[...] = jnp.zeros((lanes, lanes), f32)
            for b in range(count):
                fetch.wait(("s", b))
                wide_buf[b] = extra_buf[b].astype(f32)
            for e in range(2):
                for b in range(count):
                    tile = wide_buf[b, :, place(e)]
                    sums = [tile[r : r + 1] + tile[r + 2 : r + 3] + tile[r + 4 : r + 5] for r in (0, 1)]
                    row = e * count + b
                    share_buf[row : row + 1, :] = jnp.where(upper, sums[1], sums[0])
            share_buf[...] = share_buf[...].T

        half = slice(number * tok_count, (number + 1) * tok_count)
        fetch.wait(*[("x", b) for b in range(count)])
        x, products = x_buf[...], []
        for e in range(2):
            columns = slice(e * units, (e + 1) * units)
            fetch.wait(("w", 3 * e))
            gate = dot(x, wide_w[:, 2 * e * units : (2 * e + 1) * units], ((1,), (0,)))
            fetch.wait(("w", 3 * e + 1))
            up = dot(x, wide_w[:, (2 * e + 1) * units : (2 * e + 2) * units], ((1,), (0,)))
            fetch.wait(("w", 3 * e + 2))
            if e == 0:
                fetch.wait(*[("c", b) for b in range(count)])
            plain = dot(c_buf[...], down_w[columns, :], ((1,), (1,)))
            products.append((gate, up, plain))
        for e, (gate, up, plain) in enumerate(products):
            columns = slice(e * units, (e + 1) * units)
            sigma = jax.nn.sigmoid(gate)
            silu_val = gate * sigma
            hidden = silu_val * up
            part = [share_buf[half, e * count + b : e * count + b + 1] for b in range(count)]
            part = jnp.concatenate(part, axis=0)
            weighted_buf[:, columns] = (part * hidden).astype(bf16)
            inner = jnp.sum(hidden * plain, axis=1, keepdims=True)
            for b in range(count):
                value = inner[b * tok_count : (b + 1) * tok_count]
                inner_buf[half, e * count + b : e * count + b + 1] = value
            grad_hidden = part * plain
            grad_gate = (grad_hidden * up * (sigma * (1.0 + gate * (1.0 - sigma)))).astype(bf16)
            grad_up = (grad_hidden * silu_val).astype(bf16)
            factor_buf[:, 2 * e * units : (2 * e + 1) * units] = grad_gate
            factor_buf[:, (2 * e + 1) * units : (2 * e + 2) * units] = grad_up
        fetch.start("weighted", weighted_buf, weighted_ref)
        fetch.start("factor", factor_buf, factor_ref)
        y_buf[...] = dot(weighted_buf[...], down_w[...], ((1,), (0,))).astype(bf16)
        for b in range(count):
            at = pl.ds(b * tok_count, tok_count)
            fetch.start(("y", b), y_buf.at[at], returned(b, 0, tok_count))
        g_buf[...] = dot(factor_buf[...], wide_w[...], ((1,), (1,))).astype(bf16)
        for b in range(count):
            at = pl.ds(b * tok_count, tok_count)
            fetch.start(("g", b), g_buf.at[at], returned(b, tok_count, tok_count))
        if last:
            wide_buf[...] = jnp.zeros((count, EXTRA, width), f32)
            inner_buf[...] = inner_buf[...].T
            for e in range(2):
                for b in range(count):
                    row = e * count + b
                    value, lines = inner_buf[row : row + 1, :], []
                    for _ in range(3):
                        piece = value.astype(bf16).astype(f32)
                        lines += [jnp.where(upper, 0.0, piece), jnp.where(upper, piece, 0.0)]
                        value = value - piece
                    lines += [jnp.zeros((2, lanes), f32)]
                    wide_buf[b, 0:8, place(e)] = jnp.concatenate(lines, axis=0)
            for b in range(count):
                extra_buf[b] = wide_buf[b].astype(bf16)
                fetch.start(("i", b), extra_buf.at[b], returned(b, size, EXTRA))
        else:
            fetch.start("share", share_buf, after_refs[0])
            fetch.start("inner", inner_buf, after_refs[1])
        fetch.wait_all()

    outs = [shape(len(held) * back, width, bf16) for held in layout]
    outs += [shape(every, 2 * units, bf16), shape(every, 4 * units, bf16)]
    small = shape(lanes, lanes, f32)
    operands = (*blocks, *weights[0], *weights[1])
    if last:
        operands += before
    else:
        outs += [small, small]
    scratch = [pltpu.VMEM((width, 4 * units), bf16), pltpu.VMEM((2 * units, width), bf16)]
    scratch += [pltpu.VMEM((every, width), bf16)] * 4
    scratch += [pltpu.VMEM((every, 2 * units), bf16), pltpu.VMEM((every, 4 * units), bf16)]
    scratch += [pltpu.VMEM(small.shape, f32)] * 2
    scratch += [pltpu.VMEM((count, EXTRA, width), f32), pltpu.VMEM((count, EXTRA, width), bf16)]
    flops = 24 * every * width * units
    copies = 5 * count + 6 + 2 + 2
    outs = kernel(body, outs, scratch, copies, flops, *operands, scalar=me)
    return outs[: len(layout)], outs[len(layout) :]


def weight_grads(expert, blocks, factors, away=None, sums=()):
    bf16 = jnp.bfloat16
    parts, count, width = len(blocks), len(blocks[0]), blocks[0][0].shape[1]
    each = factors[0][0].shape[0]
    tok_count, every, units = each // count, each * parts, factors[0][0].shape[1] // 2
    extra = 0 if away is None else 1

    def body(*refs):
        b_refs, refs = refs[: parts * count], refs[parts * count :]
        f_refs, refs = refs[: 2 * parts], refs[2 * parts :]
        away_refs, sum_refs, refs = refs[:extra], refs[extra : extra + len(sums)], refs[extra + len(sums) :]
        out_refs, refs = refs[: len(outs)], refs[len(outs) :]
        x_buf, c_buf, weighted_buf, factor_buf, *bufs, sems = refs
        away_bufs, out_bufs = bufs[:extra], bufs[extra : 3 * extra + 1]
        sum_bufs = bufs[3 * extra + 1 :]
        fetch = Fetch(sems)
        names = range(parts * count)
        for i in names:
            at = pl.ds(i * tok_count, tok_count)
            fetch.start(("x", i), b_refs[i].at[pl.ds(0, tok_count)], x_buf.at[at])
        for p in range(parts):
            at = pl.ds(p * each, each)
            lanes = pl.ds(2 * expert * units, 2 * units)
            fetch.start(("f", p), f_refs[2 * p + 1].at[:, lanes], factor_buf.at[at])
        if extra:
            fetch.start("away", away_refs[0], away_bufs[0])
        for p in range(parts):
            at = pl.ds(p * each, each)
            lanes = pl.ds(expert * units, units)
            fetch.start(("w", p), f_refs[2 * p].at[:, lanes], weighted_buf.at[at])
        for i in names:
            at = pl.ds(i * tok_count, tok_count)
            fetch.start(("c", i), b_refs[i].at[pl.ds(tok_count, tok_count)], c_buf.at[at])
        for i, ref in enumerate(sum_refs):
            fetch.start(("sum", i), ref, sum_bufs[i])
        fetch.wait(*[("x", i) for i in names], *[("f", p) for p in range(parts)])
        for number in range(3):
            if number < 2:
                left, right = x_buf, factor_buf[:, number * units : (number + 1) * units]
                columns, into = slice(number * units, (number + 1) * units), slice(0, width)
            else:
                fetch.wait(*[("c", i) for i in names], *[("w", p) for p in range(parts)])
                left, right = weighted_buf, c_buf[...]
                columns, into = slice(0, width), slice(width, width + units)
            for start in range(0, into.stop - into.start, units):
                value = dot(left[:, start : start + units], right, ((0,), (0,)))
                at = slice(into.start + start, into.start + start + units)
                if not extra:
                    out_bufs[0][at, columns] = value.astype(bf16)
                else:
                    fetch.wait("away")
                    value = value + away_bufs[0][at, columns].astype(jnp.float32)
                    out_bufs[number][start : start + units, :] = value.astype(bf16)
                    block = out_bufs[number].at[start : start + units]
                    target = out_refs[number].at[start : start + units]
                    fetch.start(("out", number, start), block, target)
            if not extra and number:
                at = pl.ds(into.start, into.stop - into.start)
                fetch.start(("out", number), out_bufs[0].at[at], out_refs[0].at[at])
        if extra:
            fetch.wait(*[("sum", i) for i in range(len(sums))])
            total = sum(buf[...].astype(jnp.float32) for buf in sum_bufs[: len(sums)])
            sum_bufs[-1][...] = total.astype(bf16)
            for i, ref in enumerate(out_refs[3:]):
                half = sum_bufs[-1].at[pl.ds(i * tok_count, tok_count)]
                fetch.start(("half", i), half, ref.at[pl.ds(0, tok_count)])
        fetch.wait_all()

    flops = 6 * every * width * units
    operands = (*[b for part in blocks for b in part], *[f for part in factors for f in part])
    scratch = [pltpu.VMEM((every, width), bf16)] * 2
    scratch += [pltpu.VMEM((every, units), bf16), pltpu.VMEM((every, 2 * units), bf16)]
    packed = shape(width + units, width, bf16)
    if away is None:
        outs = [packed]
        scratch += [pltpu.VMEM(packed.shape, bf16)]
    else:
        operands += (away, *sums)
        outs = [shape(width, units, bf16)] * 2 + [shape(units, width, bf16)]
        scratch += [pltpu.VMEM(v.shape, bf16) for v in (packed, *outs, *sums, sums[0])]
        outs += [shape(*sums[0].shape, bf16)] * 2
    copies = 2 * parts * count + 2 * parts + 1 + 2 * -(-width // units) + 1 + len(sums) + 2
    outs = kernel(body, outs, scratch, copies, flops, *operands)
    return outs if extra else outs[0]


def paired(latent_in, routes, combine_weights, cotangent, w_gate, w_up, w_down):
    f32 = jnp.float32
    devices_ep, tok_count, width = lax.axis_size("ep"), *latent_in.shape
    me = lax.axis_index("ep")
    mid = tok_count // 2
    experts = jnp.arange(devices_ep, dtype=jnp.int32)
    own = (w_gate[0], w_up[0], w_down[0])

    chosen = routes[None, :, :] == experts[:, None, None]
    share = jnp.sum(jnp.where(chosen, combine_weights[None, :, :], 0.0), axis=2)
    lines = jnp.stack(pieces(share)).reshape(-1, width)
    lines = jnp.pad(lines, ((0, EXTRA - lines.shape[0]), (0, 0)))
    a0 = jnp.concatenate([latent_in[:mid], cotangent[:mid], lines], axis=0)
    b0 = jnp.concatenate([latent_in[mid:], cotangent[mid:]], axis=0)
    gate_w = swap(own[0], CORE)
    a0, b0, gate_w, own = fence(a0, b0, gate_w, own)

    a2, a4, b4, a1 = swap(a0, FAR), swap(a0, SIDE), swap(b0, SIDE), swap(a0, NEAR)
    up_w = swap(own[1], CORE)
    a1, a4, a2, b4, up_w, b0, own = fence(a1, a4, a2, b4, up_w, b0, own)
    a5, a6, a3, b2 = swap(a1, SIDE), swap(a2, SIDE), swap(a2, NEAR), swap(b0, FAR)
    down_w = swap(own[2], CORE)
    (a3,) = fence(a3)
    a7 = swap(a3, SIDE)
    b2, a5, a6 = fence(b2, a5, a6)
    b6, b1, b3 = swap(b2, SIDE), swap(b0, NEAR), swap(b2, NEAR)
    a7, b1, b6 = fence(a7, b1, b6)
    b5, b7 = swap(b1, SIDE), swap(b6, NEAR)
    weights, me = (own, (gate_w, up_w, down_w)), me.astype(jnp.int32).reshape(1)
    a = [a0, a1, a2, a3, a4, a5, a6, a7]
    q, (*a_factors, shares, inners) = both_ways(0, a, weights, me)
    q0, q1, q2, q4, q5, q6, q73 = q
    q73, q5, shares, inners, b5, b7 = fence(q73, q5, shares, inners, b5, b7)
    r73, r5 = swap(q73, NEAR), swap(q5, SIDE)
    b = [b0, b1, b2, b3, b4, b5, b6, b7]
    p, b_factors = both_ways(1, b, weights, me, (shares, inners))
    p0, p1, p2, p4, p5, p6, p73 = p
    r73, r5, q6, q4, p73, p6, p5, p4, b_factors = fence(r73, r5, q6, q4, p73, p6, p5, p4, b_factors)
    factors, size = (a_factors, b_factors), q6.shape[0]
    q6, q2, q1 = narrow(added(q6, r73[:size])), added(q2, r73[size:]), narrow(added(q1, r5))
    q6, p73, p5, q1 = fence(q6, p73, p5, q1)
    r6, r73, r5 = swap(q6, SIDE), swap(p73, NEAR), swap(p5, SIDE)
    away = weight_grads(1, (a, b), factors)
    r6, r5, away = fence(r6, r5, away)
    q2 = swap(narrow(q2 + r6.astype(f32)), FAR)
    size = p6.shape[0]
    p1 = narrow(added(p1, r5))
    p6, r73, away, q1, p1 = fence(p6, r73, away, q1, p1)
    p6 = narrow(added(p6, r73[:size]))
    p6, away, q1, q4 = fence(p6, away, q1, q4)
    r6, q1, q4, away = swap(p6, SIDE), swap(q1, NEAR), swap(q4, SIDE), swap(away, CORE)
    r6, p1, p4 = fence(r6, p1, p4)
    p2 = narrow(added(p2, r73[size:]) + r6.astype(f32))
    p2, p1, p4, away = fence(p2, p1, p4, away)
    p2, p1, p4 = swap(p2, FAR), swap(p1, NEAR), swap(p4, SIDE)
    *grad_w, combined, grad_latent = weight_grads(0, (a, b), factors, away, (q0, q4, q1, q2))
    p2, p1, p4, combined, grad_latent = fence(p2, p1, p4, combined, grad_latent)

    p = added(p0, p4) + added(p1, p2)
    combined = lax.dynamic_update_slice(combined, narrow(p[:mid]), (mid, 0))
    grad_latent = lax.dynamic_update_slice(grad_latent, narrow(p[mid : 2 * mid]), (mid, 0))
    inner = p[2 * mid :].reshape(-1, devices_ep, tok_count)[:3].sum(axis=0)
    grad_combine = jnp.sum(jnp.where(chosen, inner[:, :, None], 0.0), axis=0)
    return (combined, grad_latent, grad_combine, *[v[None] for v in grad_w])


def local(latent_in, routes, combine_weights, cotangent, w_gate, w_up, w_down):
    plan = paired if w_gate.shape[0] == 1 and lax.axis_size("ep") == 2 * len(REACH) else exchanged
    return plan(latent_in, routes, combine_weights, cotangent, w_gate, w_up, w_down)


def solution(mesh):
    return jax.shard_map(
        local,
        mesh=mesh,
        in_specs=(
            P(("grp", "ep"), None),
            P(("grp", "ep"), None),
            P(("grp", "ep"), None),
            P(("grp", "ep"), None),
            P("ep", None, None),
            P("ep", None, None),
            P("ep", None, None),
        ),
        out_specs=(
            P(("grp", "ep"), None),
            P(("grp", "ep"), None),
            P(("grp", "ep"), None),
            P(("grp", "ep"), None, None),
            P(("grp", "ep"), None, None),
            P(("grp", "ep"), None, None),
        ),
        check_vma=False,
    )
```

```python
import jax
import jax.numpy as jnp
from jax import lax
from jax.experimental import pallas as pl
from jax.experimental.pallas import tpu as pltpu
from jax.sharding import PartitionSpec as P


def assign_slots(route_rows, expert_count):
    flat_ids = route_rows.reshape(-1)
    onehot = (flat_ids[:, None] == jnp.arange(expert_count, dtype=jnp.int32)[None, :]).astype(
        jnp.int32
    )
    ranks = jnp.cumsum(onehot, axis=0) - 1
    return (flat_ids, jnp.sum(onehot * ranks, axis=1))


def expert_forward(rows, gate_w, up_w, down_w):
    gate_pre = jnp.einsum("erl,elf->erf", rows, gate_w, preferred_element_type=jnp.float32)
    up_pre = jnp.einsum("erl,elf->erf", rows, up_w, preferred_element_type=jnp.float32)
    sigma = jax.nn.sigmoid(gate_pre)
    silu_val = gate_pre * sigma
    hidden = (silu_val * up_pre).astype(jnp.bfloat16)
    expert_out = jnp.einsum(
        "erf,efl->erl", hidden, down_w, preferred_element_type=jnp.float32
    ).astype(jnp.bfloat16)
    return (expert_out, (gate_pre, up_pre, sigma, silu_val, hidden))


def expert_backward(rows, grad_out, saved, gate_w, up_w, down_w):
    gate_pre, up_pre, sigma, silu_val, hidden = saved
    grad_down = jnp.einsum(
        "erf,erl->efl", hidden, grad_out, preferred_element_type=jnp.float32
    ).astype(jnp.bfloat16)
    grad_hidden = jnp.einsum("erl,efl->erf", grad_out, down_w, preferred_element_type=jnp.float32)
    grad_gate = (grad_hidden * up_pre * sigma * (1.0 + gate_pre * (1.0 - sigma))).astype(
        jnp.bfloat16
    )
    grad_up = (grad_hidden * silu_val).astype(jnp.bfloat16)
    grad_gw = jnp.einsum(
        "erl,erf->elf", rows, grad_gate, preferred_element_type=jnp.float32
    ).astype(jnp.bfloat16)
    grad_uw = jnp.einsum("erl,erf->elf", rows, grad_up, preferred_element_type=jnp.float32).astype(
        jnp.bfloat16
    )
    grad_rows = (
        jnp.einsum("erf,elf->erl", grad_gate, gate_w, preferred_element_type=jnp.float32)
        + jnp.einsum("erf,elf->erl", grad_up, up_w, preferred_element_type=jnp.float32)
    ).astype(jnp.bfloat16)
    return (grad_rows, grad_gw, grad_uw, grad_down)


def exchanged(latent_in, routes, combine_weights, cotangent, w_gate, w_up, w_down):
    devices_ep = lax.axis_size("ep")
    local_experts = w_gate.shape[0]
    expert_count = local_experts * devices_ep
    tok_count = latent_in.shape[0]
    top_count = routes.shape[1]
    width = latent_in.shape[1]
    capacity = tok_count * top_count * 3 // (2 * expert_count)
    expert_ids, slot_ids = assign_slots(routes, expert_count)
    position = expert_ids * capacity + slot_ids
    repeated = jnp.repeat(latent_in, top_count, axis=0)
    weighted = (combine_weights[:, :, None] * cotangent.astype(jnp.float32)[:, None, :]).astype(
        jnp.bfloat16
    )
    send_rows = jnp.zeros((expert_count * capacity, width), jnp.bfloat16).at[position].set(repeated)
    send_rows = send_rows.reshape(expert_count, capacity, width)
    send_cot = (
        jnp.zeros((expert_count * capacity, width), jnp.bfloat16)
        .at[position]
        .set(weighted.reshape(-1, width))
    )
    send_cot = send_cot.reshape(expert_count, capacity, width)

    def to_local(received):
        shaped = received.reshape(devices_ep, local_experts, capacity, width)
        return shaped.transpose(1, 0, 2, 3).reshape(local_experts, devices_ep * capacity, width)

    def to_home(local_rows):
        shaped = local_rows.reshape(local_experts, devices_ep, capacity, width)
        return shaped.transpose(1, 0, 2, 3).reshape(expert_count, capacity, width)

    got_rows = lax.all_to_all(send_rows, "ep", split_axis=0, concat_axis=0, tiled=True)
    rows_local = to_local(got_rows)
    expert_out, saved = expert_forward(rows_local, w_gate, w_up, w_down)
    back_out = lax.all_to_all(to_home(expert_out), "ep", split_axis=0, concat_axis=0, tiled=True)
    got_cot = lax.all_to_all(send_cot, "ep", split_axis=0, concat_axis=0, tiled=True)
    grad_rows, grad_gw, grad_uw, grad_down = expert_backward(
        rows_local, to_local(got_cot), saved, w_gate, w_up, w_down
    )
    back_grad = lax.all_to_all(to_home(grad_rows), "ep", split_axis=0, concat_axis=0, tiled=True)
    out_rows = (
        back_out.reshape(-1, width)[position]
        .reshape(tok_count, top_count, width)
        .astype(jnp.float32)
    )
    grad_back = (
        back_grad.reshape(-1, width)[position]
        .reshape(tok_count, top_count, width)
        .astype(jnp.float32)
    )
    combined = jnp.sum(combine_weights[:, :, None] * out_rows, axis=1).astype(jnp.bfloat16)
    grad_combine = jnp.sum(cotangent.astype(jnp.float32)[:, None, :] * out_rows, axis=2)
    grad_latent = jnp.sum(grad_back, axis=1).astype(jnp.bfloat16)
    return (combined, grad_latent, grad_combine, grad_gw, grad_uw, grad_down)


def dot(a, b, dims):
    return lax.dot_general(a, b, (dims, ((), ())), preferred_element_type=jnp.float32)


def swap(value, bit):
    pairs = [(i, i ^ bit) for i in range(lax.axis_size("ep"))]
    return lax.ppermute(value, "ep", pairs)


CORE, SIDE, NEAR, FAR = 1, 2, 4, 8
REACH = (0, NEAR, FAR, NEAR | FAR, SIDE, SIDE | NEAR, SIDE | FAR, SIDE | NEAR | FAR)


def fence(*values):
    return lax.optimization_barrier(values)


def added(a, b):
    return a.astype(jnp.float32) + b.astype(jnp.float32)


def narrow(value):
    return value.astype(jnp.bfloat16)


MIB = 1 << 20


class Fetch:
    def __init__(self, sems):
        self.sems, self.waiting = sems, {}

    def start(self, name, source, target):
        copy = pltpu.make_async_copy(source, target, self.sems.at[len(self.waiting)])
        copy.start()
        self.waiting[name] = [copy, False]

    def wait(self, *names):
        for name in names:
            if not self.waiting[name][1]:
                self.waiting[name][0].wait()
                self.waiting[name][1] = True

    def wait_all(self):
        self.wait(*self.waiting)


def kernel(body, outs, scratch, copies, flops, *operands, scalar=None):
    moved = sum(v.size * v.dtype.itemsize for v in (*operands, *outs))
    in_specs = [pl.BlockSpec(memory_space=pl.ANY)] * len(operands)
    if scalar is not None:
        operands = (scalar, *operands)
        in_specs = [pl.BlockSpec(memory_space=pltpu.SMEM), *in_specs]
    return pl.pallas_call(
        body,
        out_shape=outs,
        in_specs=in_specs,
        out_specs=[pl.BlockSpec(memory_space=pl.ANY)] * len(outs),
        scratch_shapes=[*scratch, pltpu.SemaphoreType.DMA((copies,))],
        compiler_params=pltpu.CompilerParams(vmem_limit_bytes=56 * MIB),
        cost_estimate=pl.CostEstimate(flops=flops, bytes_accessed=moved, transcendentals=0),
    )(*operands)


def shape(rows, columns, dtype):
    return jax.ShapeDtypeStruct((rows, columns), dtype)


def pieces(value):
    first = narrow(value)
    value = value - first.astype(jnp.float32)
    second = narrow(value)
    return first, second, narrow(value - second.astype(jnp.float32))


EXTRA = 16


def both_ways(number, blocks, weights, me, before=None):
    bf16, f32 = jnp.bfloat16, jnp.float32
    count, width = len(blocks), blocks[0].shape[1]
    units, last = weights[0][0].shape[1], before is not None
    tok_count = (blocks[0].shape[0] - (0 if last else EXTRA)) // 2
    every, size = count * tok_count, 2 * tok_count
    lanes = 128
    back = size + (EXTRA if last else 0)
    layout = [[0], [1], [2], [4], [5], [6], [7, 3]]
    place_of = {b: (i, j * back) for i, held in enumerate(layout) for j, b in enumerate(held)}

    def body(me_ref, *refs):
        b_refs, w_refs, refs = refs[:count], refs[count : count + 6], refs[count + 6 :]
        before_refs, refs = (refs[:2], refs[2:]) if last else ((), refs)
        q_refs, refs = refs[: len(layout)], refs[len(layout) :]
        weighted_ref, factor_ref, refs = refs[0], refs[1], refs[2:]
        after_refs, refs = ((), refs) if last else (refs[:2], refs[2:])
        wide_w, down_w, refs = refs[0], refs[1], refs[2:]
        x_buf, c_buf, y_buf, g_buf, weighted_buf, factor_buf, refs = *refs[:6], refs[6:]
        share_buf, inner_buf, wide_buf, extra_buf, sems = refs
        fetch = Fetch(sems)
        w_bufs = []
        for e in range(2):
            for i in (2 * e, 2 * e + 1):
                w_bufs.append(wide_w.at[:, pl.ds(i * units, units)])
            w_bufs.append(down_w.at[pl.ds(e * units, units)])
        me = me_ref[0]
        low = lax.rem(me, 8)
        for b in range(count):
            at = pl.ds(b * tok_count, tok_count)
            fetch.start(("x", b), b_refs[b].at[pl.ds(0, tok_count)], x_buf.at[at])
            if b == 0:
                fetch.start(("w", 0), w_refs[0], w_bufs[0])
        if last:
            fetch.start("share", before_refs[0], share_buf)
            fetch.start("inner", before_refs[1], inner_buf)
        else:
            for b in range(count):
                fetch.start(("s", b), b_refs[b].at[pl.ds(size, EXTRA)], extra_buf.at[b])
        for i in (1, 2):
            fetch.start(("w", i), w_refs[i], w_bufs[i])
        for b in range(count):
            at = pl.ds(b * tok_count, tok_count)
            fetch.start(("c", b), b_refs[b].at[pl.ds(tok_count, tok_count)], c_buf.at[at])
        for i in (3, 4, 5):
            fetch.start(("w", i), w_refs[i], w_bufs[i])

        def returned(b, first, rows):
            ref, offset = place_of[b]
            return q_refs[ref].at[pl.ds(offset + first, rows)]

        def place(e):
            number = lax.rem(low + e, 2) + low - lax.rem(low, 2)
            return pl.ds(pl.multiple_of(number * lanes, lanes), lanes)

        upper = me >= 8
        if last:
            fetch.wait("share", "inner")
        else:
            inner_buf[...] = jnp.zeros((lanes, lanes), f32)
            share_buf[...] = jnp.zeros((lanes, lanes), f32)
            for b in range(count):
                fetch.wait(("s", b))
                wide_buf[b] = extra_buf[b].astype(f32)
            for e in range(2):
                for b in range(count):
                    tile = wide_buf[b, :, place(e)]
                    sums = [tile[r : r + 1] + tile[r + 2 : r + 3] + tile[r + 4 : r + 5] for r in (0, 1)]
                    row = e * count + b
                    share_buf[row : row + 1, :] = jnp.where(upper, sums[1], sums[0])
            share_buf[...] = share_buf[...].T

        half = slice(number * tok_count, (number + 1) * tok_count)
        fetch.wait(*[("x", b) for b in range(count)])
        x, products = x_buf[...], []
        for e in range(2):
            columns = slice(e * units, (e + 1) * units)
            fetch.wait(("w", 3 * e))
            gate = dot(x, wide_w[:, 2 * e * units : (2 * e + 1) * units], ((1,), (0,)))
            fetch.wait(("w", 3 * e + 1))
            up = dot(x, wide_w[:, (2 * e + 1) * units : (2 * e + 2) * units], ((1,), (0,)))
            fetch.wait(("w", 3 * e + 2))
            if e == 0:
                fetch.wait(*[("c", b) for b in range(count)])
            plain = dot(c_buf[...], down_w[columns, :], ((1,), (1,)))
            products.append((gate, up, plain))
        for e, (gate, up, plain) in enumerate(products):
            columns = slice(e * units, (e + 1) * units)
            sigma = jax.nn.sigmoid(gate)
            silu_val = gate * sigma
            hidden = silu_val * up
            part = [share_buf[half, e * count + b : e * count + b + 1] for b in range(count)]
            part = jnp.concatenate(part, axis=0)
            weighted_buf[:, columns] = (part * hidden).astype(bf16)
            inner = jnp.sum(hidden * plain, axis=1, keepdims=True)
            for b in range(count):
                value = inner[b * tok_count : (b + 1) * tok_count]
                inner_buf[half, e * count + b : e * count + b + 1] = value
            grad_hidden = part * plain
            grad_gate = (grad_hidden * up * (sigma * (1.0 + gate * (1.0 - sigma)))).astype(bf16)
            grad_up = (grad_hidden * silu_val).astype(bf16)
            factor_buf[:, 2 * e * units : (2 * e + 1) * units] = grad_gate
            factor_buf[:, (2 * e + 1) * units : (2 * e + 2) * units] = grad_up
        fetch.start("weighted", weighted_buf, weighted_ref)
        fetch.start("factor", factor_buf, factor_ref)
        y_buf[...] = dot(weighted_buf[...], down_w[...], ((1,), (0,))).astype(bf16)
        for b in range(count):
            at = pl.ds(b * tok_count, tok_count)
            fetch.start(("y", b), y_buf.at[at], returned(b, 0, tok_count))
        for first in (0, count // 2):
            rows = slice(first * tok_count, (first + count // 2) * tok_count)
            g_buf[rows, :] = dot(factor_buf[rows, :], wide_w[...], ((1,), (1,))).astype(bf16)
            for b in range(first, first + count // 2):
                at = pl.ds(b * tok_count, tok_count)
                fetch.start(("g", b), g_buf.at[at], returned(b, tok_count, tok_count))
        if last:
            wide_buf[...] = jnp.zeros((count, EXTRA, width), f32)
            inner_buf[...] = inner_buf[...].T
            for e in range(2):
                for b in range(count):
                    row = e * count + b
                    value, lines = inner_buf[row : row + 1, :], []
                    for _ in range(3):
                        piece = value.astype(bf16).astype(f32)
                        lines += [jnp.where(upper, 0.0, piece), jnp.where(upper, piece, 0.0)]
                        value = value - piece
                    lines += [jnp.zeros((2, lanes), f32)]
                    wide_buf[b, 0:8, place(e)] = jnp.concatenate(lines, axis=0)
            for b in range(count):
                extra_buf[b] = wide_buf[b].astype(bf16)
                fetch.start(("i", b), extra_buf.at[b], returned(b, size, EXTRA))
        else:
            fetch.start("share", share_buf, after_refs[0])
            fetch.start("inner", inner_buf, after_refs[1])
        fetch.wait_all()

    outs = [shape(len(held) * back, width, bf16) for held in layout]
    outs += [shape(every, 2 * units, bf16), shape(every, 4 * units, bf16)]
    small = shape(lanes, lanes, f32)
    operands = (*blocks, *weights[0], *weights[1])
    if last:
        operands += before
    else:
        outs += [small, small]
    scratch = [pltpu.VMEM((width, 4 * units), bf16), pltpu.VMEM((2 * units, width), bf16)]
    scratch += [pltpu.VMEM((every, width), bf16)] * 4
    scratch += [pltpu.VMEM((every, 2 * units), bf16), pltpu.VMEM((every, 4 * units), bf16)]
    scratch += [pltpu.VMEM(small.shape, f32)] * 2
    scratch += [pltpu.VMEM((count, EXTRA, width), f32), pltpu.VMEM((count, EXTRA, width), bf16)]
    flops = 24 * every * width * units
    copies = 5 * count + 6 + 2 + 2
    outs = kernel(body, outs, scratch, copies, flops, *operands, scalar=me)
    return outs[: len(layout)], outs[len(layout) :]


def weight_grads(expert, blocks, factors, away=None, sums=()):
    bf16 = jnp.bfloat16
    parts, count, width = len(blocks), len(blocks[0]), blocks[0][0].shape[1]
    each = factors[0][0].shape[0]
    tok_count, every, units = each // count, each * parts, factors[0][0].shape[1] // 2
    extra = 0 if away is None else 1

    def body(*refs):
        b_refs, refs = refs[: parts * count], refs[parts * count :]
        f_refs, refs = refs[: 2 * parts], refs[2 * parts :]
        away_refs, sum_refs, refs = refs[:extra], refs[extra : extra + len(sums)], refs[extra + len(sums) :]
        out_refs, refs = refs[: len(outs)], refs[len(outs) :]
        x_buf, c_buf, weighted_buf, factor_buf, *bufs, sems = refs
        away_bufs, out_bufs = bufs[:extra], bufs[extra : 3 * extra + 1]
        sum_bufs = bufs[3 * extra + 1 :]
        fetch = Fetch(sems)
        names = range(parts * count)
        for i in names:
            at = pl.ds(i * tok_count, tok_count)
            fetch.start(("x", i), b_refs[i].at[pl.ds(0, tok_count)], x_buf.at[at])
        for p in range(parts):
            at = pl.ds(p * each, each)
            lanes = pl.ds(2 * expert * units, 2 * units)
            fetch.start(("f", p), f_refs[2 * p + 1].at[:, lanes], factor_buf.at[at])
        if extra:
            fetch.start("away", away_refs[0], away_bufs[0])
        for p in range(parts):
            at = pl.ds(p * each, each)
            lanes = pl.ds(expert * units, units)
            fetch.start(("w", p), f_refs[2 * p].at[:, lanes], weighted_buf.at[at])
        for i in names:
            at = pl.ds(i * tok_count, tok_count)
            fetch.start(("c", i), b_refs[i].at[pl.ds(tok_count, tok_count)], c_buf.at[at])
        for i, ref in enumerate(sum_refs):
            fetch.start(("sum", i), ref, sum_bufs[i])
        fetch.wait(*[("x", i) for i in names], *[("f", p) for p in range(parts)])
        for number in range(3):
            if number < 2:
                left, right = x_buf, factor_buf[:, number * units : (number + 1) * units]
                columns, into = slice(number * units, (number + 1) * units), slice(0, width)
            else:
                fetch.wait(*[("c", i) for i in names], *[("w", p) for p in range(parts)])
                left, right = weighted_buf, c_buf[...]
                columns, into = slice(0, width), slice(width, width + units)
            for start in range(0, into.stop - into.start, units):
                value = dot(left[:, start : start + units], right, ((0,), (0,)))
                at = slice(into.start + start, into.start + start + units)
                if not extra:
                    out_bufs[0][at, columns] = value.astype(bf16)
                else:
                    fetch.wait("away")
                    value = value + away_bufs[0][at, columns].astype(jnp.float32)
                    out_bufs[number][start : start + units, :] = value.astype(bf16)
                    block = out_bufs[number].at[start : start + units]
                    target = out_refs[number].at[start : start + units]
                    fetch.start(("out", number, start), block, target)
            if not extra and number:
                at = pl.ds(into.start, into.stop - into.start)
                fetch.start(("out", number), out_bufs[0].at[at], out_refs[0].at[at])
        if extra:
            fetch.wait(*[("sum", i) for i in range(len(sums))])
            total = sum(buf[...].astype(jnp.float32) for buf in sum_bufs[: len(sums)])
            sum_bufs[-1][...] = total.astype(bf16)
            for i, ref in enumerate(out_refs[3:]):
                half = sum_bufs[-1].at[pl.ds(i * tok_count, tok_count)]
                fetch.start(("half", i), half, ref.at[pl.ds(0, tok_count)])
        fetch.wait_all()

    flops = 6 * every * width * units
    operands = (*[b for part in blocks for b in part], *[f for part in factors for f in part])
    scratch = [pltpu.VMEM((every, width), bf16)] * 2
    scratch += [pltpu.VMEM((every, units), bf16), pltpu.VMEM((every, 2 * units), bf16)]
    packed = shape(width + units, width, bf16)
    if away is None:
        outs = [packed]
        scratch += [pltpu.VMEM(packed.shape, bf16)]
    else:
        operands += (away, *sums)
        outs = [shape(width, units, bf16)] * 2 + [shape(units, width, bf16)]
        scratch += [pltpu.VMEM(v.shape, bf16) for v in (packed, *outs, *sums, sums[0])]
        outs += [shape(*sums[0].shape, bf16)] * 2
    copies = 2 * parts * count + 2 * parts + 1 + 2 * -(-width // units) + 1 + len(sums) + 2
    outs = kernel(body, outs, scratch, copies, flops, *operands)
    return outs if extra else outs[0]


def paired(latent_in, routes, combine_weights, cotangent, w_gate, w_up, w_down):
    f32 = jnp.float32
    devices_ep, tok_count, width = lax.axis_size("ep"), *latent_in.shape
    me = lax.axis_index("ep")
    mid = tok_count // 2
    experts = jnp.arange(devices_ep, dtype=jnp.int32)
    own = (w_gate[0], w_up[0], w_down[0])

    chosen = routes[None, :, :] == experts[:, None, None]
    share = jnp.sum(jnp.where(chosen, combine_weights[None, :, :], 0.0), axis=2)
    lines = jnp.stack(pieces(share)).reshape(-1, width)
    lines = jnp.pad(lines, ((0, EXTRA - lines.shape[0]), (0, 0)))
    a0 = jnp.concatenate([latent_in[:mid], cotangent[:mid], lines], axis=0)
    b0 = jnp.concatenate([latent_in[mid:], cotangent[mid:]], axis=0)
    gate_w = swap(own[0], CORE)
    a0, b0, gate_w, own = fence(a0, b0, gate_w, own)

    a2, a4, b4, a1 = swap(a0, FAR), swap(a0, SIDE), swap(b0, SIDE), swap(a0, NEAR)
    up_w = swap(own[1], CORE)
    a1, a4, a2, b4, up_w, b0, own = fence(a1, a4, a2, b4, up_w, b0, own)
    a5, a6, a3, b2 = swap(a1, SIDE), swap(a2, SIDE), swap(a2, NEAR), swap(b0, FAR)
    down_w = swap(own[2], CORE)
    (a3,) = fence(a3)
    a7 = swap(a3, SIDE)
    b2, a5, a6 = fence(b2, a5, a6)
    b6, b1, b3 = swap(b2, SIDE), swap(b0, NEAR), swap(b2, NEAR)
    a7, b1, b6 = fence(a7, b1, b6)
    b5, b7 = swap(b1, SIDE), swap(b6, NEAR)
    weights, me = (own, (gate_w, up_w, down_w)), me.astype(jnp.int32).reshape(1)
    a = [a0, a1, a2, a3, a4, a5, a6, a7]
    q, (*a_factors, shares, inners) = both_ways(0, a, weights, me)
    q0, q1, q2, q4, q5, q6, q73 = q
    q73, q5, shares, inners, b5, b7 = fence(q73, q5, shares, inners, b5, b7)
    r73, r5 = swap(q73, NEAR), swap(q5, SIDE)
    b = [b0, b1, b2, b3, b4, b5, b6, b7]
    p, b_factors = both_ways(1, b, weights, me, (shares, inners))
    p0, p1, p2, p4, p5, p6, p73 = p
    r73, r5, q6, q4, p73, p6, p5, p4, b_factors = fence(r73, r5, q6, q4, p73, p6, p5, p4, b_factors)
    factors, size = (a_factors, b_factors), q6.shape[0]
    q6, q2, q1 = narrow(added(q6, r73[:size])), added(q2, r73[size:]), narrow(added(q1, r5))
    q6, p73, p5, q1 = fence(q6, p73, p5, q1)
    r6, r73, r5 = swap(q6, SIDE), swap(p73, NEAR), swap(p5, SIDE)
    away = weight_grads(1, (a, b), factors)
    r6, r5, away = fence(r6, r5, away)
    q2 = swap(narrow(q2 + r6.astype(f32)), FAR)
    size = p6.shape[0]
    p1 = narrow(added(p1, r5))
    p6, r73, away, q1, p1 = fence(p6, r73, away, q1, p1)
    p6 = narrow(added(p6, r73[:size]))
    p6, away, q1, q4 = fence(p6, away, q1, q4)
    r6, q1, q4, away = swap(p6, SIDE), swap(q1, NEAR), swap(q4, SIDE), swap(away, CORE)
    r6, p1, p4 = fence(r6, p1, p4)
    p2 = narrow(added(p2, r73[size:]) + r6.astype(f32))
    p2, p1, p4, away = fence(p2, p1, p4, away)
    p2, p1, p4 = swap(p2, FAR), swap(p1, NEAR), swap(p4, SIDE)
    *grad_w, combined, grad_latent = weight_grads(0, (a, b), factors, away, (q0, q4, q1, q2))
    p2, p1, p4, combined, grad_latent = fence(p2, p1, p4, combined, grad_latent)

    p = added(p0, p4) + added(p1, p2)
    combined = lax.dynamic_update_slice(combined, narrow(p[:mid]), (mid, 0))
    grad_latent = lax.dynamic_update_slice(grad_latent, narrow(p[mid : 2 * mid]), (mid, 0))
    inner = p[2 * mid :].reshape(-1, devices_ep, tok_count)[:3].sum(axis=0)
    grad_combine = jnp.sum(jnp.where(chosen, inner[:, :, None], 0.0), axis=0)
    return (combined, grad_latent, grad_combine, *[v[None] for v in grad_w])


def local(latent_in, routes, combine_weights, cotangent, w_gate, w_up, w_down):
    plan = paired if w_gate.shape[0] == 1 and lax.axis_size("ep") == 2 * len(REACH) else exchanged
    return plan(latent_in, routes, combine_weights, cotangent, w_gate, w_up, w_down)


def solution(mesh):
    return jax.shard_map(
        local,
        mesh=mesh,
        in_specs=(
            P(("grp", "ep"), None),
            P(("grp", "ep"), None),
            P(("grp", "ep"), None),
            P(("grp", "ep"), None),
            P("ep", None, None),
            P("ep", None, None),
            P("ep", None, None),
        ),
        out_specs=(
            P(("grp", "ep"), None),
            P(("grp", "ep"), None),
            P(("grp", "ep"), None),
            P(("grp", "ep"), None, None),
            P(("grp", "ep"), None, None),
            P(("grp", "ep"), None, None),
        ),
        check_vma=False,
    )
```
